256 devices in a mesh: frag: 16 (over z, core), grp: 16 (over y, x).
Axes of the slice: x: 4, y: 4, z: 8, core: 2. Of those that a mesh axis runs over, the one named last changes fastest.
Arguments:
- background: float32 [512, 512, 512], P('frag', 'grp'), may hold values from 0.25 to 4
- orbitals: bfloat16 [16, 16, 16, 8192], P(None, None, None, ('frag', 'grp')), may hold values from -3 to 3
- frag_info: int32 [512, 8], P(('frag', 'grp')), may hold values from -1 to 31, as said below
Outputs:
- total_density: float32 [512, 512, 512], P('frag', 'grp')
- frag_potential: float32 [512, 32768], P(('frag', 'grp'))
The draws below stay inside these ranges and needn't reach their ends.
Inputs may be any that keep to these rules, and one draw needn't show every extreme that they name: `frag_info`: row r belongs to the device r // 2 in the order frag then grp. A fragment's root x cell lies in the block of x cells that its device's frag index holds of total_density. Sizes are 1 or 2; the sign is -1 to the power of the number of sizes equal to 1; count lies between the number of cells of the box and twice it, and every device holds a fragment with count 16. Counting, for each grp block of total_density's second dimension, the fragments of one device that have box rows in it: at most 2, and in every frag group some block gets 2 from every device of the group.
All inputs are finite; a program needn't handle non-finite values.
Results may differ from the reference program's by a relative error of at most 0.0003.
Values sent between devices are 32-bit elements; how exact they have to be, the bound alone decides.
No kernel may reach another device: no remote copies, remote signals or barrier semaphores. Data moves between devices by JAX's collectives and lax.ppermute only.
A program may use at most 128 MiB of HBM per device.

```python
import math
import jax
import jax.numpy as jnp
from jax import lax

NG = 512
CELL = 16
MO = 16
FD = 2
BOX = 32
FRAGS = 512
ORBS = 8192
N_FRAG = 16
N_GRP = 16


def device_rows(device_key, group_pos, special):
    cell_total = NG // CELL
    cells_y = cell_total // N_GRP
    cells_x = cell_total // N_FRAG
    share_cap = (FD + N_GRP - 1) // N_GRP
    subkeys = jax.random.split(device_key, 9)
    labels = jnp.arange(N_GRP * share_cap, dtype=jnp.int32) // share_cap
    rank_order = jax.random.permutation(subkeys[0], N_GRP * share_cap).astype(jnp.int32)
    before = jnp.mod(special - 1, N_GRP)
    forced = (labels == before) | (labels == special)
    priority = jnp.where(forced, rank_order - N_GRP * share_cap, rank_order)
    arranged = jnp.argsort(priority, stable=True)
    owners = labels[arranged][:FD]
    crossing = owners == before
    largest = crossing & (jnp.cumsum(crossing.astype(jnp.int32)) == 1)
    size_x = jnp.where(largest, 2, jax.random.randint(subkeys[1], (FD,), 1, 3))
    size_y = jnp.where(crossing, 2, jax.random.randint(subkeys[2], (FD,), 1, 3))
    size_z = jnp.where(largest, 2, jax.random.randint(subkeys[3], (FD,), 1, 3))
    start_x = group_pos * cells_x + jax.random.randint(subkeys[4], (FD,), 0, cells_x)
    start_y = owners * cells_y + jnp.where(crossing, cells_y - 1, jax.random.randint(subkeys[5], (FD,), 0, cells_y))
    start_z = jax.random.randint(subkeys[6], (FD,), 0, cell_total)
    cell_count = size_x * size_y * size_z
    orbital_count = jnp.where(largest, MO, cell_count + jax.random.randint(subkeys[7], (FD,), 0, cell_count + 1))
    unit_sizes = (size_x == 1).astype(jnp.int32) + (size_y == 1).astype(jnp.int32) + (size_z == 1).astype(jnp.int32)
    parity_sign = 1 - 2 * jnp.mod(unit_sizes, 2)
    table_rows = jnp.stack([start_x, start_y, start_z, size_x, size_y, size_z, parity_sign, orbital_count], axis=1)
    shuffle = jax.random.permutation(subkeys[8], FD)
    return table_rows[shuffle].astype(jnp.int32)


def draw_frag_info(key, part):
    key = jax.random.fold_in(key, 11)
    group_key, device_key = jax.random.split(key)
    specials = jax.random.randint(group_key, (N_FRAG,), 0, N_GRP)
    device_ids = jnp.arange(N_FRAG * N_GRP, dtype=jnp.int32)
    group_ids = device_ids // N_GRP
    device_keys = jax.vmap(jax.random.fold_in, in_axes=(None, 0))(device_key, device_ids)
    table_rows = jax.vmap(device_rows)(device_keys, group_ids, specials[group_ids])
    return table_rows.reshape(N_FRAG * N_GRP * FD, 8)


def level_of(rng, dims, pieces, least, high):
    level = 1.0
    for axis_at, parts in pieces:
        steps = jax.random.uniform(jax.random.fold_in(jax.random.fold_in(rng, 6), axis_at), (parts,), jnp.float32, least / len(pieces), high / len(pieces))
        level = level * jnp.repeat(jnp.exp(steps), dims[axis_at] // parts).reshape((-1,) + (1,) * (len(dims) - 1 - axis_at))
    return level


def bell_draw(key, extent, deviation, bound, shards=(), kind=jnp.bfloat16):
    values = jax.random.normal(key, extent, jnp.float32) * deviation
    if len(shards) > 0:
        values = level_of(key, extent, shards, -0.22, 0.18) * values
    return jnp.clip(values, min=-bound, max=bound).astype(kind)


def setup_inputs(seed: int = 0) -> dict:
    seeds = jax.random.split(jax.random.key(seed), 4)
    return {
        "background": jnp.clip(jnp.exp(math.log(4.0) - 2.7725887 * jax.random.uniform(seeds[0], (NG, NG, NG), jnp.float32) ** level_of(seeds[0], (NG, NG, NG), ((0, 16), (1, 16)), -0.2, 0.2)), 0.25, 4.0),
        "orbitals": bell_draw(seeds[1], (CELL, CELL, CELL, ORBS), 0.5, 3.0, ((3, 256),)),
        "frag_info": draw_frag_info(jax.random.fold_in(seeds[3], 71), 0),
    }


SPACING = 0.2
HIGHEST = lax.Precision.HIGHEST

def synthesis_tables(span_cells, cell_edge):
    frequency = jnp.arange(cell_edge, dtype=jnp.int32) - cell_edge // 2
    grid_point = jnp.arange(2 * cell_edge, dtype=jnp.int32)
    box_span = span_cells.astype(jnp.int32) * cell_edge
    residue = jnp.mod(frequency[:, None, None] * grid_point[None, :, None], box_span[None, None, :])
    angle_value = 2.0 * math.pi * residue.astype(jnp.float32) / box_span.astype(jnp.float32)[None, None, :]
    quarter = box_span // 4
    live_mask = (frequency[:, None, None] >= -quarter[None, None, :]) & (frequency[:, None, None] < quarter[None, None, :]) & (grid_point[None, :, None] < box_span[None, None, :])
    weight = math.sqrt(2.0 / cell_edge) / span_cells.astype(jnp.float32)
    return jnp.where(live_mask, (jnp.cos(angle_value) + jnp.sin(angle_value)) * weight[None, None, :], 0.0)

def fragment_density(frag_row, coeffs):
    table_x = synthesis_tables(frag_row[3:4], CELL)[:, :, 0]
    table_y = synthesis_tables(frag_row[4:5], CELL)[:, :, 0]
    table_z = synthesis_tables(frag_row[5:6], CELL)[:, :, 0]
    partial_value = jnp.einsum('abcm,cz->abzm', coeffs, table_z, precision=HIGHEST)
    partial_value = jnp.einsum('abzm,by->ayzm', partial_value, table_y, precision=HIGHEST)
    partial_value = jnp.einsum('ayzm,ax->xyzm', partial_value, table_x, precision=HIGHEST)
    occupied = (jnp.arange(MO, dtype=jnp.int32) < frag_row[7]).astype(jnp.float32)
    return 2.0 * lax.optimization_barrier(jnp.sum(partial_value * partial_value * occupied, axis=3))

def box_indices(frag_row):
    steps_box = jnp.arange(BOX, dtype=jnp.int32)
    along_x = jnp.mod(frag_row[0] * CELL + steps_box, NG)
    along_y = jnp.mod(frag_row[1] * CELL + steps_box, NG)
    along_z = jnp.mod(frag_row[2] * CELL + steps_box, NG)
    return (along_x, along_y, along_z)

def reference(background, orbitals, frag_info):

    def add_fragment(number, grid):
        frag_row = frag_info[number]
        start = (number * MO).astype(jnp.int32)
        coeffs = lax.dynamic_slice_in_dim(orbitals, start, MO, 3).astype(jnp.float32)
        signed = frag_row[6].astype(jnp.float32) * fragment_density(frag_row, coeffs)
        along_x, along_y, along_z = box_indices(frag_row)
        return grid.at[along_x[:, None, None], along_y[None, :, None], along_z[None, None, :]].add(signed)
    deposit = lax.fori_loop(0, FRAGS, add_fragment, jnp.zeros((NG, NG, NG), jnp.float32))
    total_density = background + deposit
    spectrum = jnp.fft.rfftn(total_density)
    full_wave = jnp.arange(NG, dtype=jnp.int32)
    folded = jnp.minimum(full_wave, NG - full_wave)
    half_wave = jnp.arange(NG // 2 + 1, dtype=jnp.int32)
    square_sum = folded[:, None, None] ** 2 + folded[None, :, None] ** 2 + half_wave[None, None, :] ** 2
    factor = (NG * SPACING) ** 2 / math.pi
    kernel = jnp.where(square_sum > 0, factor / jnp.maximum(square_sum, 1).astype(jnp.float32), 0.0)
    potential = jnp.fft.irfftn(spectrum * kernel, s=(NG, NG, NG)).astype(jnp.float32)

    def take_box(frag_row):
        along_x, along_y, along_z = box_indices(frag_row)
        block = potential[along_x[:, None, None], along_y[None, :, None], along_z[None, None, :]]
        steps_box = jnp.arange(BOX, dtype=jnp.int32)
        inside = (steps_box[:, None, None] < frag_row[3] * CELL) & (steps_box[None, :, None] < frag_row[4] * CELL) & (steps_box[None, None, :] < frag_row[5] * CELL)
        return jnp.where(inside, block, 0.0).reshape(BOX * BOX * BOX)
    frag_potential = lax.map(take_box, frag_info)
    return (total_density, frag_potential)
```

```python
import math

import jax
import jax.numpy as jnp
import ml_dtypes
import numpy as np
from jax import lax
from jax.experimental import pallas as pl
from jax.experimental.pallas import tpu as pltpu
from jax.sharding import PartitionSpec as P

NG = 512
SPACING = 0.2
F32 = jnp.float32
BF16 = jnp.bfloat16
BOTH = ("frag", "grp")
VMEM_LIMIT = 56 * 1024 * 1024


def halves(table):
    high = table.astype(ml_dtypes.bfloat16)
    low = (table - high.astype(np.float64)).astype(ml_dtypes.bfloat16)
    return np.stack([high, low])


def synthesis_table(span):
    frequency = np.arange(16)[:, None] - 8
    point = np.arange(32)[None, :]
    angle = 2.0 * math.pi * np.mod(frequency * point, span * 16) / (span * 16)
    live = (frequency >= -4 * span) & (frequency < 4 * span) & (point < 16 * span)
    return np.where(live, (np.cos(angle) + np.sin(angle)) * math.sqrt(2.0 / 16) / span, 0.0)


def plane_tables():
    tables = []
    for span_y in (1, 2):
        for span_z in (1, 2):
            table_y = synthesis_table(span_y).reshape(16, 2, 16)
            table_z = synthesis_table(span_z)
            full = np.einsum("brg,cz->bcgrz", table_y, table_z)
            tables.append(halves(full.reshape(256, 1024)))
    return np.stack(tables)


def depth_tables():
    tables = []
    for span in (1, 2):
        full = np.einsum("ax,mn->mxan", synthesis_table(span), np.eye(16))
        tables.append(halves(full.reshape(512, 256)))
    return np.stack(tables)


def hartley():
    index = np.arange(NG)
    angle = 2.0 * math.pi / NG * np.mod(index[:, None] * index[None, :], NG)
    return np.cos(angle) + np.sin(angle)


def row_order():
    block, low, high = np.meshgrid(np.arange(16), np.arange(4), np.arange(8), indexing="ij")
    return (block * 32 + high * 4 + low).reshape(-1)


def cyclic_order():
    residue, cell = np.meshgrid(np.arange(16), np.arange(32), indexing="ij")
    return (cell * 16 + residue).reshape(-1)


def split(value):
    high = value.astype(BF16)
    return high, (value - high.astype(F32)).astype(BF16)


def product(left, right, dims):
    dims = (dims, ((), ()))
    total = lax.dot_general(left[0], right[1], dims, preferred_element_type=F32)
    total += lax.dot_general(left[1], right[0], dims, preferred_element_type=F32)
    return total + lax.dot_general(left[0], right[0], dims, preferred_element_type=F32)


NN = ((1,), (0,))
NT = ((1,), (1,))
TN = ((0,), (0,))


def lanes_of(shape):
    return lax.broadcasted_iota(jnp.int32, shape, len(shape) - 1)


def exchange(parts):
    lane = lanes_of(parts[0].shape)
    low = lane < 64
    even = (lane & 32) == 0
    v0, v1, v2, v3 = parts
    a0 = jnp.where(low, v0, pltpu.roll(v2, 64, 1))
    a1 = jnp.where(low, v1, pltpu.roll(v3, 64, 1))
    a2 = jnp.where(low, pltpu.roll(v0, 64, 1), v2)
    a3 = jnp.where(low, pltpu.roll(v1, 64, 1), v3)
    return (
        jnp.where(even, a0, pltpu.roll(a1, 32, 1)),
        jnp.where(even, pltpu.roll(a0, 96, 1), a1),
        jnp.where(even, a2, pltpu.roll(a3, 32, 1)),
        jnp.where(even, pltpu.roll(a2, 96, 1), a3),
    )


def density_kernel(info_ref, coeff_ref, plane_ref, depth_ref, note_ref, out_ref):
    f = pl.program_id(0)
    count = info_ref[f, 7]
    scale = 2.0 * info_ref[f, 6].astype(F32)
    coeffs = coeff_ref[:, pl.ds(pl.multiple_of(f * 16, 16), 16), :].reshape(256, 256)
    for part in range(4):
        columns = slice(part * 256, (part + 1) * 256)
        flat = jnp.dot(coeffs, plane_ref[0, 1, :, columns], preferred_element_type=F32)
        flat += jnp.dot(coeffs, plane_ref[0, 0, :, columns], preferred_element_type=F32)
        psi = product((depth_ref[0, 0], depth_ref[0, 1]), split(flat), NN)
        total = jnp.zeros((32, 256), F32)
        for m in range(16):
            orbital = psi[m * 32 : (m + 1) * 32]
            total += orbital * orbital * (m < count).astype(F32)
        total = total * scale
        for tile in range(2):
            here = total[:, tile * 128 : (tile + 1) * 128]
            turned = pltpu.roll(here, 64, 1)
            owner = 2 * (2 * part + tile)
            low = lanes_of(here.shape) < 64

            @pl.when(f == 0)
            def _():
                out_ref[owner, 0:32, :] = here
                out_ref[owner + 1, 0:32, :] = turned

            @pl.when(f == 1)
            def _():
                out_ref[owner, 0:32, :] = jnp.where(low, out_ref[owner, 0:32, :], turned)
                out_ref[owner + 1, 0:32, :] = jnp.where(low, out_ref[owner + 1, 0:32, :], here)

    for owner in range(16):
        out_ref[owner, 32:40, :] = note_ref[...]


def densities(info, coeffs, note):
    planes = jnp.asarray(plane_tables())
    depths = jnp.asarray(depth_tables())
    return pl.pallas_call(
        density_kernel,
        grid_spec=pltpu.PrefetchScalarGridSpec(
            num_scalar_prefetch=1,
            grid=(2,),
            in_specs=[
                pl.BlockSpec((16, 32, 256), lambda f, info: (0, 0, 0)),
                pl.BlockSpec(
                    (1, 2, 256, 1024), lambda f, info: (2 * info[f, 4] + info[f, 5] - 3, 0, 0, 0)
                ),
                pl.BlockSpec((1, 2, 512, 256), lambda f, info: (info[f, 3] - 1, 0, 0, 0)),
                pl.BlockSpec((8, 128), lambda f, info: (0, 0)),
            ],
            out_specs=pl.BlockSpec((16, 40, 128), lambda f, info: (0, 0, 0)),
        ),
        out_shape=jax.ShapeDtypeStruct((16, 40, 128), F32),
        compiler_params=pltpu.CompilerParams(vmem_limit_bytes=VMEM_LIMIT),
        name="densities",
    )(info, coeffs, planes, depths, note)


def deposit_kernel(info_ref, own_ref, past_ref, out_ref):
    out_ref[...] = jnp.zeros(out_ref.shape, F32)

    def source(s, carry):
        own = own_ref[s, 0:32, :]
        past = past_ref[s, 0:16, :]
        lane = lanes_of((16, 128))
        for f in range(2):
            for first, piece in ((0, own), (32, past)):
                number = first + 2 * s + f
                odd = info_ref[number, 0] & 1
                cell_z = info_ref[number, 2]
                tile = cell_z >> 3
                offset = (cell_z & 7) * 16
                inside = (lane >= offset) & (lane < offset + 32)
                beyond = lane < offset - 96
                for r in range(2):
                    row = (info_ref[number, 1] + r) & 31
                    turned = pltpu.roll(piece, (offset + 128 - (64 * f + 32 * r)) & 127, 1)
                    if first:
                        kept = (odd == 1).astype(F32)
                        moves = ((0, turned * kept),)
                    else:
                        kept = (odd == 0).astype(F32)
                        start = pl.multiple_of(odd * 16, 16)
                        moves = ((start, turned[0:16]), (16, turned[16:32] * kept))
                    for at, value in moves:
                        out_ref[row, tile, pl.ds(at, 16), :] += jnp.where(inside, value, 0.0)

                    @pl.when(offset == 112)
                    def _():
                        after = (tile + 1) & 3
                        for at, value in moves:
                            out_ref[row, after, pl.ds(at, 16), :] += jnp.where(beyond, value, 0.0)

        return carry

    lax.fori_loop(0, 16, source, 0)


def deposits(info, own, past):
    return pl.pallas_call(
        deposit_kernel,
        in_specs=[
            pl.BlockSpec(memory_space=pltpu.SMEM),
            pl.BlockSpec(memory_space=pltpu.VMEM),
            pl.BlockSpec(memory_space=pltpu.VMEM),
        ],
        out_specs=pl.BlockSpec(memory_space=pltpu.VMEM),
        out_shape=jax.ShapeDtypeStruct((32, 4, 32, 128), F32),
        compiler_params=pltpu.CompilerParams(vmem_limit_bytes=VMEM_LIMIT),
        name="deposits",
    )(info, own, past)


def forward_kernel(back_ref, held_ref, table_ref, total_ref, out_ref):
    table = (table_ref[0], table_ref[1])

    def block(b, carry):
        for x in range(8):
            plane = b * 8 + x
            for jj in range(2):
                for half in range(2):
                    rows = slice(jj * 16 + half * 8, jj * 16 + half * 8 + 8)
                    for tile in range(4):
                        start = half * 2048 + jj * 128 + tile * 32 + plane
                        columns = slice(tile * 128, (tile + 1) * 128)
                        total_ref[plane, rows, columns] = (
                            back_ref[plane, rows, columns]
                            + held_ref[pl.ds(start, 8, stride=256), :]
                        )
        total = total_ref[pl.ds(pl.multiple_of(b * 8, 8), 8), :, :].reshape(256, 512)
        waves = product(table, split(total), NT)
        for tile in range(2):
            out_ref[pl.ds(2 * b + tile, 512, stride=8), :] = waves[
                :, tile * 128 : (tile + 1) * 128
            ]
        return carry

    lax.fori_loop(0, 4, block, 0)


def forward_z(background, held, table):
    return pl.pallas_call(
        forward_kernel,
        in_specs=[pl.BlockSpec(memory_space=pltpu.VMEM)] * 3,
        out_specs=[pl.BlockSpec(memory_space=pltpu.VMEM)] * 2,
        out_shape=[
            jax.ShapeDtypeStruct((32, 32, 512), F32),
            jax.ShapeDtypeStruct((4096, 128), F32),
        ],
        compiler_params=pltpu.CompilerParams(vmem_limit_bytes=VMEM_LIMIT),
        name="forward_z",
    )(background, held, table)


def planes_kernel(place_ref, in_ref, side_ref, rows_ref, back_ref, cyclic_ref, out_ref, grid_ref):
    side = (side_ref[0], side_ref[1])
    rows = (rows_ref[0], rows_ref[1])
    back = (back_ref[0], back_ref[1])
    cyclic = (cyclic_ref[0], cyclic_ref[1])

    def plane(kk, carry):
        for quad in range(4):
            parts = [in_ref[:, 4 * quad + i, kk].reshape(128, 128) for i in range(4)]
            for i, part in enumerate(exchange(parts)):
                grid_ref[:, i, :, quad * 128 : (quad + 1) * 128] = part.reshape(16, 8, 128)
        value = product(split(grid_ref[...].reshape(512, 512)), side, NN)
        value = product(rows, split(value), NN)

        def folded(index):
            lowest = jnp.minimum(index, NG - index)
            return lowest * lowest

        wave = 2 * place_ref[0] + kk
        square = (
            folded(lax.broadcasted_iota(jnp.int32, (NG, 1), 0))
            + folded(lax.broadcasted_iota(jnp.int32, (1, NG), 1))
            + folded(wave)
        )
        factor = (NG * SPACING) ** 2 / math.pi / float(NG) ** 3
        value = value * jnp.where(
            square > 0, factor / jnp.maximum(square, 1).astype(F32), 0.0
        )
        value = product(back, split(value), NN)
        grid_ref[...] = product(split(value), cyclic, NN).reshape(16, 4, 8, 512)
        for quad in range(4):
            columns = slice(quad * 128, (quad + 1) * 128)
            parts = [grid_ref[:, i, :, columns].reshape(128, 128) for i in range(4)]
            for i, part in enumerate(exchange(parts)):
                out_ref[:, 4 * quad + i, kk] = part.reshape(16, 8, 128)
        return carry

    lax.fori_loop(0, 2, plane, 0)


def solve_planes(place, waves, tables):
    return pl.pallas_call(
        planes_kernel,
        in_specs=[pl.BlockSpec(memory_space=pltpu.SMEM)]
        + [pl.BlockSpec(memory_space=pltpu.VMEM)] * 5,
        out_specs=pl.BlockSpec(memory_space=pltpu.VMEM),
        out_shape=jax.ShapeDtypeStruct((16, 16, 2, 8, 128), F32),
        scratch_shapes=[pltpu.VMEM((16, 4, 8, 512), F32)],
        compiler_params=pltpu.CompilerParams(vmem_limit_bytes=VMEM_LIMIT),
        name="solve_planes",
    )(place, waves, *tables)


def boxes_kernel(info_ref, in_ref, table_ref, own_ref, past_ref, grid_ref):
    table = (table_ref[0], table_ref[1])

    def block(b, carry):
        waves = in_ref[pl.ds(b, 512, stride=8), :]
        value = product(split(waves), table, TN)
        for tile in range(4):
            grid_ref[tile, pl.ds(pl.multiple_of(b * 128, 128), 128), :] = value[
                :, tile * 128 : (tile + 1) * 128
            ]
        return carry

    lax.fori_loop(0, 8, block, 0)

    def source(s, carry):
        lane = lanes_of((16, 128))
        group = lane >> 5
        first_half = jnp.zeros((16, 128), F32)
        second_half = jnp.zeros((16, 128), F32)
        past_half = jnp.zeros((16, 128), F32)
        for f in range(2):
            for first in (0, 32):
                number = first + 2 * s + f
                odd = info_ref[number, 0] & 1
                cell_z = info_ref[number, 2]
                tile = cell_z >> 3
                after = (tile + 1) & 3
                offset = (cell_z & 7) * 16
                for r in range(2):
                    row = (info_ref[number, 1] + r) & 31
                    shift = (64 * f + 32 * r + 128 - offset) & 127
                    wanted = group == 2 * f + r

                    def rows_at(start):
                        value = jnp.where(
                            lane >= offset,
                            grid_ref[tile, pl.ds(start, 16, stride=32), :],
                            grid_ref[after, pl.ds(start, 16, stride=32), :],
                        )
                        return jnp.where(wanted, pltpu.roll(value, shift, 1), 0.0)

                    if first:
                        past_half += rows_at(row) * (odd == 1).astype(F32)
                    else:
                        first_half += rows_at(odd * 512 + row)
                        second_half += rows_at(512 + row) * (odd == 0).astype(F32)
        own_ref[s, 0:16, :] = first_half
        own_ref[s, 16:32, :] = second_half
        past_ref[s] = past_half
        return carry

    lax.fori_loop(0, 16, source, 0)


def boxes(info, waves, table):
    return pl.pallas_call(
        boxes_kernel,
        in_specs=[
            pl.BlockSpec(memory_space=pltpu.SMEM),
            pl.BlockSpec(memory_space=pltpu.VMEM),
            pl.BlockSpec(memory_space=pltpu.VMEM),
        ],
        out_specs=[pl.BlockSpec(memory_space=pltpu.VMEM)] * 2,
        out_shape=[
            jax.ShapeDtypeStruct((16, 32, 128), F32),
            jax.ShapeDtypeStruct((16, 16, 128), F32),
        ],
        scratch_shapes=[pltpu.VMEM((4, 1024, 128), F32)],
        compiler_params=pltpu.CompilerParams(vmem_limit_bytes=VMEM_LIMIT),
        name="boxes",
    )(info, waves, table)


def layout_kernel(info_ref, in_ref, out_ref):
    row = lax.broadcasted_iota(jnp.int32, (32, 128), 0)
    lane = lanes_of((32, 128))
    for quad in range(4):
        parts = exchange([in_ref[4 * quad + i] for i in range(4)])
        for f in range(2):
            for r in range(2):
                inside = (
                    (row < info_ref[f, 3] * 16)
                    & (16 * r + 4 * quad + (lane >> 5) < info_ref[f, 4] * 16)
                    & ((lane & 31) < info_ref[f, 5] * 16)
                )
                out_ref[pl.ds((4 * r + quad) * 2 + f, 32, stride=16), :] = jnp.where(
                    inside, parts[2 * f + r], 0.0
                )


def lay_out(info, pieces):
    return pl.pallas_call(
        layout_kernel,
        in_specs=[
            pl.BlockSpec(memory_space=pltpu.SMEM),
            pl.BlockSpec(memory_space=pltpu.VMEM),
        ],
        out_specs=pl.BlockSpec(memory_space=pltpu.VMEM),
        out_shape=jax.ShapeDtypeStruct((512, 128), F32),
        compiler_params=pltpu.CompilerParams(vmem_limit_bytes=VMEM_LIMIT),
        name="lay_out",
    )(info, pieces)


def along_frag(block, distance):
    devices = range(lax.axis_size("frag"))
    route = [(i, (i + distance) % len(devices)) for i in devices]
    return lax.ppermute(block, "frag", route)


def traded(block, axis):
    return lax.all_to_all(block, axis, split_axis=0, concat_axis=0, tiled=True)


def body(background, orbitals, frag_info):
    waves = hartley()
    straight = jnp.asarray(halves(waves))
    order = row_order()
    rows = jnp.asarray(halves(waves[:, order]))
    back = jnp.asarray(halves(waves[order, :]))
    cyclic = jnp.asarray(halves(waves[:, cyclic_order()]))
    place = (lax.axis_index("frag") * 16 + lax.axis_index("grp")).astype(jnp.int32).reshape(1)

    coeffs = jnp.transpose(orbitals.reshape(16, 256, 32), (0, 2, 1))
    note = jnp.pad(frag_info.astype(F32).reshape(1, 16), ((0, 7), (0, 112)))
    own = traded(densities(frag_info, coeffs, note), "grp")
    past = along_frag(own[:, 16:40, :], 1)
    info = jnp.concatenate([own[:, 32, :16], past[:, 16, :16]]).astype(jnp.int32).reshape(64, 8)
    region = deposits(info, own, past)
    held = traded(region.reshape(16, 256, 128), "grp").reshape(4096, 128)
    total_density, spectrum = forward_z(background, held, straight)
    spectrum = traded(spectrum.reshape(256, 16, 128), BOTH).reshape(16, 16, 2, 8, 128)
    spectrum = solve_planes(place, spectrum, (straight, rows, back, cyclic))
    spectrum = traded(spectrum.reshape(256, 16, 128), BOTH).reshape(4096, 128)
    pieces, beyond = boxes(info, spectrum, straight)
    beyond = along_frag(beyond, -1)
    pieces = pieces + jnp.pad(beyond, ((0, 0), (16, 0), (0, 0)))
    pieces = lay_out(frag_info, traded(pieces, "grp"))
    frag_potential = pieces.reshape(256, 2, 128).transpose(1, 0, 2).reshape(2, 32768)
    return total_density, frag_potential


def solution(mesh):
    return jax.shard_map(
        body,
        mesh=mesh,
        in_specs=(
            P("frag", "grp", None),
            P(None, None, None, ("frag", "grp")),
            P(("frag", "grp"), None),
        ),
        out_specs=(P("frag", "grp", None), P(("frag", "grp"), None)),
        check_vma=False,
    )
```

```python
import math

import jax
import jax.numpy as jnp
import ml_dtypes
import numpy as np
from jax import lax
from jax.experimental import pallas as pl
from jax.experimental.pallas import tpu as pltpu
from jax.sharding import PartitionSpec as P

NG = 512
SPACING = 0.2
F32 = jnp.float32
BF16 = jnp.bfloat16
BOTH = ("frag", "grp")
VMEM_LIMIT = 24 * 1024 * 1024


def halves(table):
    high = table.astype(ml_dtypes.bfloat16)
    low = (table - high.astype(np.float64)).astype(ml_dtypes.bfloat16)
    return np.stack([high, low])


def synthesis_table(span):
    frequency = np.arange(16)[:, None] - 8
    point = np.arange(32)[None, :]
    angle = 2.0 * math.pi * np.mod(frequency * point, span * 16) / (span * 16)
    live = (frequency >= -4 * span) & (frequency < 4 * span) & (point < 16 * span)
    return np.where(live, (np.cos(angle) + np.sin(angle)) * math.sqrt(2.0 / 16) / span, 0.0)


def plane_tables():
    tables = []
    for span_y in (1, 2):
        for span_z in (1, 2):
            table_y = synthesis_table(span_y).reshape(16, 2, 16)
            table_z = synthesis_table(span_z)
            full = np.einsum("brg,cz->bcgrz", table_y, table_z)
            tables.append(halves(full.reshape(256, 1024)))
    return np.stack(tables)


def depth_tables():
    tables = []
    for span in (1, 2):
        full = np.einsum("ax,mn->mxan", synthesis_table(span), np.eye(16))
        tables.append(halves(full.reshape(512, 256)))
    return np.stack(tables)


def cas(rows, columns):
    angle = 2.0 * math.pi / NG * np.mod(rows[:, None] * columns[None, :], NG)
    return np.cos(angle) + np.sin(angle)


def row_order():
    block, low, high = np.meshgrid(np.arange(16), np.arange(4), np.arange(8), indexing="ij")
    return (block * 32 + high * 4 + low).reshape(-1)


def cyclic_order(parity):
    residue, cell = np.meshgrid(np.arange(parity, 16, 2), np.arange(32), indexing="ij")
    return (cell * 16 + residue).reshape(-1)


def wave_tables():
    start = np.arange(256)
    even, odd = 2 * start, 2 * start + 1
    rows = row_order()[:256]
    low = np.concatenate([even[:128], odd[:128]])
    tables = [
        cas(even, start),
        cas(odd, start),
        cas(start, odd),
        cas(even, rows),
        cas(odd, rows),
        cas(rows, even),
        cas(rows, odd),
        cas(low, cyclic_order(0)),
        cas(low, cyclic_order(1)),
    ]
    return np.concatenate([halves(table) for table in tables])


def split(value):
    high = value.astype(BF16)
    return high, (value - high.astype(F32)).astype(BF16)


def product(left, right, dims):
    dims = (dims, ((), ()))
    total = lax.dot_general(left[0], right[1], dims, preferred_element_type=F32)
    total += lax.dot_general(left[1], right[0], dims, preferred_element_type=F32)
    return total + lax.dot_general(left[0], right[0], dims, preferred_element_type=F32)


NN = ((1,), (0,))
NT = ((1,), (1,))
TN = ((0,), (0,))


def lanes_of(shape):
    return lax.broadcasted_iota(jnp.int32, shape, len(shape) - 1)


def exchange(parts):
    lane = lanes_of(parts[0].shape)
    low = lane < 64
    even = (lane & 32) == 0
    v0, v1, v2, v3 = parts
    a0 = jnp.where(low, v0, pltpu.roll(v2, 64, 1))
    a1 = jnp.where(low, v1, pltpu.roll(v3, 64, 1))
    a2 = jnp.where(low, pltpu.roll(v0, 64, 1), v2)
    a3 = jnp.where(low, pltpu.roll(v1, 64, 1), v3)
    return (
        jnp.where(even, a0, pltpu.roll(a1, 32, 1)),
        jnp.where(even, pltpu.roll(a0, 96, 1), a1),
        jnp.where(even, a2, pltpu.roll(a3, 32, 1)),
        jnp.where(even, pltpu.roll(a2, 96, 1), a3),
    )


def density_kernel(
    info_ref, orbitals_ref, planes_ref, depths_ref, out_ref, coeff_ref, plane_ref, depth_ref, sems
):
    copies = []
    for f in range(2):
        pair = 2 * info_ref[f, 4] + info_ref[f, 5] - 3
        copies.append(pltpu.make_async_copy(planes_ref.at[pair], plane_ref.at[f], sems.at[2 * f]))
        copies.append(
            pltpu.make_async_copy(
                depths_ref.at[info_ref[f, 3] - 1], depth_ref.at[f], sems.at[2 * f + 1]
            )
        )
    for copy in copies:
        copy.start()
    for a in range(16):
        coeff_ref[a] = jnp.transpose(orbitals_ref[a].astype(F32)).astype(BF16)
    for f in range(2):
        count = info_ref[f, 7]
        scale = 2.0 * info_ref[f, 6].astype(F32)
        coeffs = coeff_ref[:, 16 * f : 16 * f + 16, :].reshape(256, 256)
        copies[2 * f].wait()
        copies[2 * f + 1].wait()
        for part in range(4):
            columns = slice(part * 256, (part + 1) * 256)
            flat = jnp.dot(coeffs, plane_ref[f, 1, :, columns], preferred_element_type=F32)
            flat += jnp.dot(coeffs, plane_ref[f, 0, :, columns], preferred_element_type=F32)
            psi = product((depth_ref[f, 0], depth_ref[f, 1]), split(flat), NN)
            total = jnp.zeros((32, 256), F32)
            for m in range(16):
                orbital = psi[m * 32 : (m + 1) * 32]
                total += orbital * orbital * (m < count).astype(F32)
            total = total * scale
            for tile in range(2):
                here = total[:, tile * 128 : (tile + 1) * 128]
                turned = pltpu.roll(here, 64, 1)
                owner = 2 * (2 * part + tile)
                low = lanes_of(here.shape) < 64
                if f == 0:
                    out_ref[owner, 0:32, :] = here
                    out_ref[owner + 1, 0:32, :] = turned
                else:
                    out_ref[owner, 0:32, :] = jnp.where(low, out_ref[owner, 0:32, :], turned)
                    out_ref[owner + 1, 0:32, :] = jnp.where(low, out_ref[owner + 1, 0:32, :], here)
    lane = lanes_of((8, 128))
    note = jnp.zeros((8, 128), F32)
    for place in range(16):
        note = jnp.where(lane == place, info_ref[place // 8, place % 8].astype(F32), note)
    for owner in range(16):
        out_ref[owner, 32:40, :] = note


def densities(info, orbitals):
    planes = jnp.asarray(plane_tables())
    depths = jnp.asarray(depth_tables())
    return pl.pallas_call(
        density_kernel,
        in_specs=[
            pl.BlockSpec(memory_space=pltpu.SMEM),
            pl.BlockSpec(memory_space=pltpu.VMEM),
            pl.BlockSpec(memory_space=pl.ANY),
            pl.BlockSpec(memory_space=pl.ANY),
        ],
        out_specs=pl.BlockSpec(memory_space=pltpu.VMEM),
        out_shape=jax.ShapeDtypeStruct((16, 40, 128), F32),
        scratch_shapes=[
            pltpu.VMEM((16, 32, 256), BF16),
            pltpu.VMEM((2, 2, 256, 1024), BF16),
            pltpu.VMEM((2, 2, 512, 256), BF16),
            pltpu.SemaphoreType.DMA((4,)),
        ],
        compiler_params=pltpu.CompilerParams(vmem_limit_bytes=56 * 1024 * 1024),
        name="densities",
    )(info, orbitals, planes, depths)


def deposit_kernel(info_ref, own_ref, past_ref, out_ref):
    out_ref[...] = jnp.zeros(out_ref.shape, F32)

    def source(s, carry):
        own = own_ref[s, 0:32, :]
        past = past_ref[s, 0:16, :]
        lane = lanes_of((16, 128))
        adds = []
        for f in range(2):
            for first, piece in ((0, own), (32, past)):
                number = first + 2 * s + f
                odd = info_ref[number, 0] & 1
                cell_y = info_ref[number, 1]
                cell_z = info_ref[number, 2]
                tile = cell_z >> 3
                after = (tile + 1) & 3
                offset = (cell_z & 7) * 16
                kept = odd == 1 if first else odd == 0
                low = jnp.where(kept, offset, 256)
                part_inside = (lane >= low) & (lane < low + 32)
                part_beyond = lane < jnp.where(kept, offset - 96, 0)
                inside = (lane >= offset) & (lane < offset + 32)
                beyond = lane < offset - 96
                for r in range(2):
                    row = (cell_y + r) & 31
                    turned = pltpu.roll(piece, (offset + 128 - (64 * f + 32 * r)) & 127, 1)
                    if first:
                        adds.append((row, tile, 0, jnp.where(part_inside, turned, 0.0)))
                        adds.append((row, after, 0, jnp.where(part_beyond, turned, 0.0)))
                    else:
                        start = pl.multiple_of(odd * 16, 16)
                        top, rest = turned[0:16], turned[16:32]
                        adds.append((row, tile, start, jnp.where(inside, top, 0.0)))
                        adds.append((row, after, start, jnp.where(beyond, top, 0.0)))
                        adds.append((row, tile, 16, jnp.where(part_inside, rest, 0.0)))
                        adds.append((row, after, 16, jnp.where(part_beyond, rest, 0.0)))
        for row, tile, start, value in adds:
            out_ref[row, tile, pl.ds(start, 16), :] += value
        return carry

    lax.fori_loop(0, 16, source, 0, unroll=2)


def deposits(info, own, past):
    return pl.pallas_call(
        deposit_kernel,
        in_specs=[
            pl.BlockSpec(memory_space=pltpu.SMEM),
            pl.BlockSpec(memory_space=pltpu.VMEM),
            pl.BlockSpec(memory_space=pltpu.VMEM),
        ],
        out_specs=pl.BlockSpec(memory_space=pltpu.VMEM),
        out_shape=jax.ShapeDtypeStruct((32, 4, 32, 128), F32),
        compiler_params=pltpu.CompilerParams(vmem_limit_bytes=VMEM_LIMIT),
        name="deposits",
    )(info, own, past)


def forward_kernel(back_ref, held_ref, table_ref, total_ref, out_ref, turned_ref):
    b = pl.program_id(0)
    for g in range(16):
        for jj in range(2):
            for tile in range(4):
                turned_ref[tile, pl.ds(jj * 16 + g, 8, stride=32), :] = held_ref[
                    (g * 2 + jj) * 4 + tile
                ]
    for tile in range(4):
        columns = slice(tile * 128, (tile + 1) * 128)
        total_ref[:, :, columns] = back_ref[:, :, columns] + turned_ref[tile].reshape(8, 32, 128)
    total = total_ref[...].reshape(256, 512)
    near, far = total[:, :256], total[:, 256:]
    for parity, value in ((0, near + far), (1, near - far)):
        table = (table_ref[2 * parity], table_ref[2 * parity + 1])
        waves = product(table, split(value), NT)
        for tile in range(2):
            place = pl.ds(2048 * parity + 2 * b + tile, 256, stride=8)
            out_ref[place, :] = waves[:, tile * 128 : (tile + 1) * 128]


def forward_z(background, held, table):
    return pl.pallas_call(
        forward_kernel,
        grid=(4,),
        in_specs=[
            pl.BlockSpec((8, 32, 512), lambda b: (b, 0, 0)),
            pl.BlockSpec((128, 8, 128), lambda b: (0, b, 0)),
            pl.BlockSpec((4, 256, 256), lambda b: (0, 0, 0)),
        ],
        out_specs=[
            pl.BlockSpec((8, 32, 512), lambda b: (b, 0, 0)),
            pl.BlockSpec((4096, 128), lambda b: (0, 0)),
        ],
        out_shape=[
            jax.ShapeDtypeStruct((32, 32, 512), F32),
            jax.ShapeDtypeStruct((4096, 128), F32),
        ],
        scratch_shapes=[pltpu.VMEM((4, 256, 128), F32)],
        compiler_params=pltpu.CompilerParams(vmem_limit_bytes=VMEM_LIMIT),
        name="forward_z",
    )(background, held, table)


def planes_kernel(place_ref, in_ref, tables_ref, out_ref, grid_ref):
    kk = pl.program_id(0)

    def table(i):
        return tables_ref[2 * i], tables_ref[2 * i + 1]

    for quad in range(4):
        parts = [in_ref[:, 4 * quad + i, 0].reshape(128, 128) for i in range(4)]
        for i, part in enumerate(exchange(parts)):
            grid_ref[:, i, :, quad * 128 : (quad + 1) * 128] = part.reshape(16, 8, 128)
    grid = grid_ref[...].reshape(512, 512)
    near, far = grid[:, :256], grid[:, 256:]
    value = jnp.concatenate(
        [product(split(near + far), table(0), NN), product(split(near - far), table(2), NN)], 1
    )
    near, far = value[:256], value[256:]
    value = jnp.concatenate(
        [product(table(3), split(near + far), NN), product(table(4), split(near - far), NN)], 0
    )

    def folded(place):
        wave = jnp.where(place < 256, 2 * place, 2 * place - 511)
        lowest = jnp.minimum(wave, NG - wave)
        return lowest * lowest

    square = (
        folded(lax.broadcasted_iota(jnp.int32, (NG, 1), 0))
        + folded(lax.broadcasted_iota(jnp.int32, (1, NG), 1))
        + folded(2 * place_ref[0] + kk)
    )
    factor = (NG * SPACING) ** 2 / math.pi / float(NG) ** 3
    value = value * jnp.where(square > 0, factor / jnp.maximum(square, 1).astype(F32), 0.0)
    even = product(table(5), split(value[:256]), NN)
    odd = product(table(6), split(value[256:]), NN)
    value = jnp.concatenate([even + odd, even - odd], 0)
    near = jnp.concatenate([value[:, 0:128], value[:, 256:384]], 1)
    far = jnp.concatenate([value[:, 128:256], value[:, 384:512]], 1)
    even = product(split(near + far), table(7), NN)
    odd = product(split(near - far), table(8), NN)
    grid_ref[...] = jnp.concatenate([even, odd], 1).reshape(16, 4, 8, 512)
    for quad in range(4):
        columns = slice(quad * 128, (quad + 1) * 128)
        parts = [grid_ref[:, i, :, columns].reshape(128, 128) for i in range(4)]
        for i, part in enumerate(exchange(parts)):
            owner = 2 * (4 * (quad % 2) + i) + quad // 2
            out_ref[:, owner, 0] = part.reshape(16, 8, 128)


def solve_planes(place, waves, tables):
    block = pl.BlockSpec((16, 16, 1, 8, 128), lambda kk: (0, 0, kk, 0, 0))
    return pl.pallas_call(
        planes_kernel,
        grid=(2,),
        in_specs=[
            pl.BlockSpec(memory_space=pltpu.SMEM),
            block,
            pl.BlockSpec(memory_space=pltpu.VMEM),
        ],
        out_specs=block,
        out_shape=jax.ShapeDtypeStruct((16, 16, 2, 8, 128), F32),
        scratch_shapes=[pltpu.VMEM((16, 4, 8, 512), F32)],
        compiler_params=pltpu.CompilerParams(vmem_limit_bytes=VMEM_LIMIT),
        name="solve_planes",
    )(place, waves, tables)


def boxes_kernel(info_ref, in_ref, table_ref, own_ref, past_ref, grid_ref):
    def block(b, carry):
        even = split(in_ref[pl.ds(b, 256, stride=8), :])
        odd = split(in_ref[pl.ds(2048 + b, 256, stride=8), :])
        even = product(even, (table_ref[0], table_ref[1]), TN)
        odd = product(odd, (table_ref[2], table_ref[3]), TN)
        value = jnp.concatenate([even + odd, even - odd], 1)
        for low in range(4):
            for cells in range(4):
                first = low * 32 + cells * 8
                for tile in range(4):
                    place = pl.ds(cells * 256 + 4 * b + low, 8, stride=32)
                    grid_ref[tile, place, :] = value[
                        first : first + 8, tile * 128 : (tile + 1) * 128
                    ]
        return carry

    lax.fori_loop(0, 8, block, 0)

    def source(s, carry):
        lane = lanes_of((16, 128))
        group = lane >> 5
        first_half = jnp.zeros((16, 128), F32)
        second_half = jnp.zeros((16, 128), F32)
        past_half = jnp.zeros((16, 128), F32)
        for f in range(2):
            for first in (0, 32):
                number = first + 2 * s + f
                odd = info_ref[number, 0] & 1
                cell_z = info_ref[number, 2]
                tile = cell_z >> 3
                after = (tile + 1) & 3
                offset = (cell_z & 7) * 16
                for r in range(2):
                    row = (info_ref[number, 1] + r) & 31
                    shift = (64 * f + 32 * r + 128 - offset) & 127
                    wanted = group == 2 * f + r

                    def rows_at(start):
                        place = pl.ds(pl.multiple_of(row * 32 + start, 16), 16)
                        value = jnp.where(
                            lane >= offset, grid_ref[tile, place, :], grid_ref[after, place, :]
                        )
                        return jnp.where(wanted, pltpu.roll(value, shift, 1), 0.0)

                    if first:
                        past_half += rows_at(0) * (odd == 1).astype(F32)
                    else:
                        first_half += rows_at(odd * 16)
                        second_half += rows_at(16) * (odd == 0).astype(F32)
        own_ref[s, 0:16, :] = first_half
        own_ref[s, 16:32, :] = second_half
        past_ref[s] = past_half
        return carry

    lax.fori_loop(0, 16, source, 0, unroll=2)


def boxes(info, waves, table):
    return pl.pallas_call(
        boxes_kernel,
        grid=(1,),
        in_specs=[
            pl.BlockSpec(memory_space=pltpu.SMEM),
            pl.BlockSpec(memory_space=pltpu.VMEM),
            pl.BlockSpec((4, 256, 256), lambda i: (0, 0, 0)),
        ],
        out_specs=[pl.BlockSpec(memory_space=pltpu.VMEM)] * 2,
        out_shape=[
            jax.ShapeDtypeStruct((16, 32, 128), F32),
            jax.ShapeDtypeStruct((16, 16, 128), F32),
        ],
        scratch_shapes=[pltpu.VMEM((4, 1024, 128), F32)],
        compiler_params=pltpu.CompilerParams(vmem_limit_bytes=VMEM_LIMIT),
        name="boxes",
    )(info, waves, table)


def layout_kernel(info_ref, in_ref, out_ref):
    row = lax.broadcasted_iota(jnp.int32, (32, 128), 0)
    lane = lanes_of((32, 128))
    for quad in range(4):
        parts = exchange([in_ref[4 * quad + i] for i in range(4)])
        for f in range(2):
            for r in range(2):
                inside = (
                    (row < info_ref[f, 3] * 16)
                    & (16 * r + 4 * quad + (lane >> 5) < info_ref[f, 4] * 16)
                    & ((lane & 31) < info_ref[f, 5] * 16)
                )
                out_ref[pl.ds((4 * r + quad) * 2 + f, 32, stride=16), :] = jnp.where(
                    inside, parts[2 * f + r], 0.0
                )


def lay_out(info, pieces):
    return pl.pallas_call(
        layout_kernel,
        in_specs=[
            pl.BlockSpec(memory_space=pltpu.SMEM),
            pl.BlockSpec(memory_space=pltpu.VMEM),
        ],
        out_specs=pl.BlockSpec(memory_space=pltpu.VMEM),
        out_shape=jax.ShapeDtypeStruct((512, 128), F32),
        compiler_params=pltpu.CompilerParams(vmem_limit_bytes=VMEM_LIMIT),
        name="lay_out",
    )(info, pieces)


def along_frag(block, distance):
    devices = range(lax.axis_size("frag"))
    route = [(i, (i + distance) % len(devices)) for i in devices]
    return lax.ppermute(block, "frag", route)


def traded(block, axis):
    return lax.all_to_all(block, axis, split_axis=0, concat_axis=0, tiled=True)


def body(background, orbitals, frag_info):
    tables = jnp.asarray(wave_tables())
    place = (lax.axis_index("frag") * 16 + lax.axis_index("grp")).astype(jnp.int32).reshape(1)
    frag_info, place = lax.optimization_barrier((frag_info, place))
    coeffs = orbitals.reshape(16, 256, 32)
    own = traded(densities(frag_info, coeffs), "grp")
    past = along_frag(own[:, 16:40, :], 1)
    info = jnp.concatenate([own[:, 32, :16], past[:, 16, :16]]).astype(jnp.int32).reshape(64, 8)
    region = deposits(info, own, past)
    held = traded(region.reshape(16, 256, 128), "grp").reshape(128, 32, 128)
    total_density, spectrum = forward_z(background, held, tables)
    spectrum = traded(spectrum.reshape(256, 16, 128), BOTH).reshape(16, 16, 2, 8, 128)
    spectrum = solve_planes(place, spectrum, tables)
    spectrum = traded(spectrum.reshape(256, 16, 128), BOTH).reshape(4096, 128)
    pieces, beyond = boxes(info, spectrum, tables)
    beyond = along_frag(beyond, -1)
    pieces = pieces + jnp.pad(beyond, ((0, 0), (16, 0), (0, 0)))
    pieces = lay_out(frag_info, traded(pieces, "grp"))
    frag_potential = pieces.reshape(256, 2, 128).transpose(1, 0, 2).reshape(2, 32768)
    return total_density, frag_potential


def solution(mesh):
    return jax.shard_map(
        body,
        mesh=mesh,
        in_specs=(
            P("frag", "grp", None),
            P(None, None, None, ("frag", "grp")),
            P(("frag", "grp"), None),
        ),
        out_specs=(P("frag", "grp", None), P(("frag", "grp"), None)),
        check_vma=False,
    )
```

```python
import math

import jax
import jax.numpy as jnp
import ml_dtypes
import numpy as np
from jax import lax
from jax.experimental import pallas as pl
from jax.experimental.pallas import tpu as pltpu
from jax.sharding import PartitionSpec as P

NG = 512
SPACING = 0.2
F32 = jnp.float32
BF16 = jnp.bfloat16
BOTH = ("frag", "grp")
PITCH = 40
VMEM_LIMIT = 24 * 1024 * 1024


def halves(table):
    high = table.astype(ml_dtypes.bfloat16)
    low = (table - high.astype(np.float64)).astype(ml_dtypes.bfloat16)
    return np.stack([high, low])


def synthesis_table(span):
    frequency = np.arange(16)[:, None] - 8
    point = np.arange(32)[None, :]
    angle = 2.0 * math.pi * np.mod(frequency * point, span * 16) / (span * 16)
    live = (frequency >= -4 * span) & (frequency < 4 * span) & (point < 16 * span)
    return np.where(live, (np.cos(angle) + np.sin(angle)) * math.sqrt(2.0 / 16) / span, 0.0)


def plane_tables():
    tables = []
    for span_y in (1, 2):
        for span_z in (1, 2):
            table_y = synthesis_table(span_y).reshape(16, 2, 16)
            table_z = synthesis_table(span_z)
            full = np.einsum("brg,cz->bcgrz", table_y, table_z)
            tables.append(halves(full.reshape(256, 1024)))
    return np.stack(tables)


def depth_tables():
    tables = []
    for span in (1, 2):
        full = np.einsum("ax,mn->mxan", synthesis_table(span), np.eye(16))
        tables.append(halves(full.reshape(512, 256)))
    return np.stack(tables)


def cas(rows, columns):
    angle = 2.0 * math.pi / NG * np.mod(rows[:, None] * columns[None, :], NG)
    return np.cos(angle) + np.sin(angle)


def row_order():
    block, low, high = np.meshgrid(np.arange(16), np.arange(4), np.arange(8), indexing="ij")
    return (block * 32 + high * 4 + low).reshape(-1)


def cyclic_order(parity):
    residue, cell = np.meshgrid(np.arange(parity, 16, 2), np.arange(32), indexing="ij")
    return (cell * 16 + residue).reshape(-1)


def wave_tables():
    start = np.arange(256)
    even, odd = 2 * start, 2 * start + 1
    rows = row_order()[:256]
    low = np.concatenate([even[:128], odd[:128]])
    tables = [
        cas(even, start),
        cas(odd, start),
        cas(start, odd),
        cas(even, rows),
        cas(odd, rows),
        cas(rows, even),
        cas(rows, odd),
        cas(low, cyclic_order(0)),
        cas(low, cyclic_order(1)),
    ]
    return np.concatenate([halves(table) for table in tables])


def split(value):
    high = value.astype(BF16)
    return high, (value - high.astype(F32)).astype(BF16)


def product(left, right, dims):
    dims = (dims, ((), ()))
    total = lax.dot_general(left[0], right[1], dims, preferred_element_type=F32)
    total += lax.dot_general(left[1], right[0], dims, preferred_element_type=F32)
    return total + lax.dot_general(left[0], right[0], dims, preferred_element_type=F32)


NN = ((1,), (0,))
NT = ((1,), (1,))
TN = ((0,), (0,))


def lanes_of(shape):
    return lax.broadcasted_iota(jnp.int32, shape, len(shape) - 1)


def exchange(parts):
    lane = lanes_of(parts[0].shape)
    low = lane < 64
    even = (lane & 32) == 0

    def swapped(first, second):
        crossed = pltpu.roll(jnp.where(low, second, first), 64, 1)
        return jnp.where(low, first, crossed), jnp.where(low, crossed, second)

    a0, a2 = swapped(parts[0], parts[2])
    a1, a3 = swapped(parts[1], parts[3])
    return (
        jnp.where(even, a0, pltpu.roll(a1, 32, 1)),
        jnp.where(even, pltpu.roll(a0, 96, 1), a1),
        jnp.where(even, a2, pltpu.roll(a3, 32, 1)),
        jnp.where(even, pltpu.roll(a2, 96, 1), a3),
    )


def density_kernel(
    info_ref, orbitals_ref, planes_ref, depths_ref, out_ref, coeff_ref, plane_ref, depth_ref, sems
):
    copies = []
    for f in range(2):
        pair = 2 * info_ref[f, 4] + info_ref[f, 5] - 3
        copies.append(pltpu.make_async_copy(planes_ref.at[pair], plane_ref.at[f], sems.at[2 * f]))
        copies.append(
            pltpu.make_async_copy(
                depths_ref.at[info_ref[f, 3] - 1], depth_ref.at[f], sems.at[2 * f + 1]
            )
        )
    for copy in copies:
        copy.start()
    for a in range(16):
        coeff_ref[a] = jnp.transpose(orbitals_ref[a].astype(F32)).astype(BF16)
    for f in range(2):
        count = info_ref[f, 7]
        scale = 2.0 * info_ref[f, 6].astype(F32)
        coeffs = coeff_ref[:, 16 * f : 16 * f + 16, :].reshape(256, 256)
        copies[2 * f].wait()
        copies[2 * f + 1].wait()
        for part in range(4):
            columns = slice(part * 256, (part + 1) * 256)
            flat = jnp.dot(coeffs, plane_ref[f, 1, :, columns], preferred_element_type=F32)
            flat += jnp.dot(coeffs, plane_ref[f, 0, :, columns], preferred_element_type=F32)
            psi = product((depth_ref[f, 0], depth_ref[f, 1]), split(flat), NN)
            total = jnp.zeros((32, 256), F32)
            for m in range(16):
                orbital = psi[m * 32 : (m + 1) * 32]
                total += orbital * orbital * (m < count).astype(F32)
            total = total * scale
            for tile in range(2):
                here = total[:, tile * 128 : (tile + 1) * 128]
                turned = pltpu.roll(here, 64, 1)
                owner = 2 * (2 * part + tile)
                low = lanes_of(here.shape) < 64
                if f == 0:
                    out_ref[owner, 0:32, :] = here
                    out_ref[owner + 1, 0:32, :] = turned
                else:
                    out_ref[owner, 0:32, :] = jnp.where(low, out_ref[owner, 0:32, :], turned)
                    out_ref[owner + 1, 0:32, :] = jnp.where(low, out_ref[owner + 1, 0:32, :], here)
    lane = lanes_of((8, 128))
    note = jnp.zeros((8, 128), F32)
    for place in range(16):
        note = jnp.where(lane == place, info_ref[place // 8, place % 8].astype(F32), note)
    for owner in range(16):
        out_ref[owner, 32:40, :] = note


def densities(info, orbitals):
    planes = jnp.asarray(plane_tables())
    depths = jnp.asarray(depth_tables())
    return pl.pallas_call(
        density_kernel,
        in_specs=[
            pl.BlockSpec(memory_space=pltpu.SMEM),
            pl.BlockSpec(memory_space=pltpu.VMEM),
            pl.BlockSpec(memory_space=pl.ANY),
            pl.BlockSpec(memory_space=pl.ANY),
        ],
        out_specs=pl.BlockSpec(memory_space=pltpu.VMEM),
        out_shape=jax.ShapeDtypeStruct((16, 40, 128), F32),
        scratch_shapes=[
            pltpu.VMEM((16, 32, 256), BF16),
            pltpu.VMEM((2, 2, 256, 1024), BF16),
            pltpu.VMEM((2, 2, 512, 256), BF16),
            pltpu.SemaphoreType.DMA((4,)),
        ],
        compiler_params=pltpu.CompilerParams(vmem_limit_bytes=56 * 1024 * 1024),
        name="densities",
    )(info, orbitals, planes, depths)


def deposit_kernel(info_ref, own_ref, past_ref, out_ref):
    out_ref[...] = jnp.zeros(out_ref.shape, F32)

    def source(s, carry):
        own = own_ref[s, 0:32, :]
        past = past_ref[s, 0:16, :]
        lane = lanes_of((16, 128))
        adds = []
        for f in range(2):
            for first, piece in ((0, own), (32, past)):
                number = first + 2 * s + f
                odd = info_ref[number, 0] & 1
                cell_y = info_ref[number, 1]
                cell_z = info_ref[number, 2]
                tile = cell_z >> 3
                after = (tile + 1) & 3
                offset = (cell_z & 7) * 16
                kept = odd == 1 if first else odd == 0
                low = jnp.where(kept, offset, 256)
                part_inside = (lane >= low) & (lane < low + 32)
                part_beyond = lane < jnp.where(kept, offset - 96, 0)
                inside = (lane >= offset) & (lane < offset + 32)
                beyond = lane < offset - 96
                for r in range(2):
                    row = (cell_y + r) & 31
                    turned = pltpu.roll(piece, (offset + 128 - (64 * f + 32 * r)) & 127, 1)
                    if first:
                        adds.append((row, tile, 0, jnp.where(part_inside, turned, 0.0)))
                        adds.append((row, after, 0, jnp.where(part_beyond, turned, 0.0)))
                    else:
                        start = pl.multiple_of(odd * 16, 16)
                        top, rest = turned[0:16], turned[16:32]
                        adds.append((row, tile, start, jnp.where(inside, top, 0.0)))
                        adds.append((row, after, start, jnp.where(beyond, top, 0.0)))
                        adds.append((row, tile, 16, jnp.where(part_inside, rest, 0.0)))
                        adds.append((row, after, 16, jnp.where(part_beyond, rest, 0.0)))
        for row, tile, start, value in adds:
            out_ref[row, tile, pl.ds(start, 16), :] += value
        return carry

    lax.fori_loop(0, 16, source, 0, unroll=2)


def deposits(info, own, past):
    return pl.pallas_call(
        deposit_kernel,
        in_specs=[
            pl.BlockSpec(memory_space=pltpu.SMEM),
            pl.BlockSpec(memory_space=pltpu.VMEM),
            pl.BlockSpec(memory_space=pltpu.VMEM),
        ],
        out_specs=pl.BlockSpec(memory_space=pltpu.VMEM),
        out_shape=jax.ShapeDtypeStruct((32, 4, 32, 128), F32),
        compiler_params=pltpu.CompilerParams(vmem_limit_bytes=VMEM_LIMIT),
        name="deposits",
    )(info, own, past)


def forward_kernel(back_ref, held_ref, table_ref, total_ref, out_ref, turned_ref):
    b = pl.program_id(0)
    for g in range(16):
        for jj in range(2):
            for tile in range(4):
                turned_ref[tile, pl.ds(jj * 16 + g, 8, stride=PITCH), :] = held_ref[
                    (g * 2 + jj) * 4 + tile
                ]
    for tile in range(4):
        columns = slice(tile * 128, (tile + 1) * 128)
        for x in range(8):
            total_ref[x, :, columns] = (
                back_ref[x, :, columns] + turned_ref[tile, x * PITCH : x * PITCH + 32, :]
            )
    total = total_ref[...].reshape(256, 512)
    near, far = total[:, :256], total[:, 256:]
    for parity, value in ((0, near + far), (1, near - far)):
        table = (table_ref[2 * parity], table_ref[2 * parity + 1])
        waves = product(table, split(value), NT)
        for tile in range(2):
            place = pl.ds(2048 * parity + 2 * b + tile, 256, stride=8)
            out_ref[place, :] = waves[:, tile * 128 : (tile + 1) * 128]


def forward_z(background, held, table):
    return pl.pallas_call(
        forward_kernel,
        grid=(4,),
        in_specs=[
            pl.BlockSpec((8, 32, 512), lambda b: (b, 0, 0)),
            pl.BlockSpec((128, 8, 128), lambda b: (0, b, 0)),
            pl.BlockSpec((4, 256, 256), lambda b: (0, 0, 0)),
        ],
        out_specs=[
            pl.BlockSpec((8, 32, 512), lambda b: (b, 0, 0)),
            pl.BlockSpec((4096, 128), lambda b: (0, 0)),
        ],
        out_shape=[
            jax.ShapeDtypeStruct((32, 32, 512), F32),
            jax.ShapeDtypeStruct((4096, 128), F32),
        ],
        scratch_shapes=[pltpu.VMEM((4, 8 * PITCH, 128), F32)],
        compiler_params=pltpu.CompilerParams(vmem_limit_bytes=VMEM_LIMIT),
        name="forward_z",
    )(background, held, table)


def planes_kernel(place_ref, in_ref, tables_ref, out_ref, grid_ref):
    kk = pl.program_id(0)

    def table(i):
        return tables_ref[2 * i], tables_ref[2 * i + 1]

    for quad in range(4):
        parts = [in_ref[:, 4 * quad + i, 0].reshape(128, 128) for i in range(4)]
        for i, part in enumerate(exchange(parts)):
            grid_ref[:, i, :, quad * 128 : (quad + 1) * 128] = part.reshape(16, 8, 128)
    grid = grid_ref[...].reshape(512, 512)
    near, far = grid[:, :256], grid[:, 256:]
    value = jnp.concatenate(
        [product(split(near + far), table(0), NN), product(split(near - far), table(2), NN)], 1
    )
    near, far = value[:256], value[256:]
    value = jnp.concatenate(
        [product(table(3), split(near + far), NN), product(table(4), split(near - far), NN)], 0
    )

    def folded(place):
        wave = jnp.where(place < 256, 2 * place, 2 * place - 511)
        lowest = jnp.minimum(wave, NG - wave)
        return lowest * lowest

    square = (
        folded(lax.broadcasted_iota(jnp.int32, (NG, 1), 0))
        + folded(lax.broadcasted_iota(jnp.int32, (1, NG), 1))
        + folded(2 * place_ref[0] + kk)
    )
    factor = (NG * SPACING) ** 2 / math.pi / float(NG) ** 3
    value = value * jnp.where(square > 0, factor / jnp.maximum(square, 1).astype(F32), 0.0)
    even = product(table(5), split(value[:256]), NN)
    odd = product(table(6), split(value[256:]), NN)
    value = jnp.concatenate([even + odd, even - odd], 0)
    near = jnp.concatenate([value[:, 0:128], value[:, 256:384]], 1)
    far = jnp.concatenate([value[:, 128:256], value[:, 384:512]], 1)
    even = product(split(near + far), table(7), NN)
    odd = product(split(near - far), table(8), NN)
    grid_ref[...] = jnp.concatenate([even, odd], 1).reshape(16, 4, 8, 512)
    for quad in range(4):
        columns = slice(quad * 128, (quad + 1) * 128)
        parts = [grid_ref[:, i, :, columns].reshape(128, 128) for i in range(4)]
        for i, part in enumerate(exchange(parts)):
            owner = 2 * (4 * (quad % 2) + i) + quad // 2
            out_ref[:, owner, 0] = part.reshape(16, 8, 128)


def solve_planes(place, waves, tables):
    block = pl.BlockSpec((16, 16, 1, 8, 128), lambda kk: (0, 0, kk, 0, 0))
    return pl.pallas_call(
        planes_kernel,
        grid=(2,),
        in_specs=[
            pl.BlockSpec(memory_space=pltpu.SMEM),
            block,
            pl.BlockSpec(memory_space=pltpu.VMEM),
        ],
        out_specs=block,
        out_shape=jax.ShapeDtypeStruct((16, 16, 2, 8, 128), F32),
        scratch_shapes=[pltpu.VMEM((16, 4, 8, 512), F32)],
        compiler_params=pltpu.CompilerParams(vmem_limit_bytes=VMEM_LIMIT),
        name="solve_planes",
    )(place, waves, tables)


def boxes_kernel(info_ref, in_ref, table_ref, own_ref, past_ref, grid_ref):
    def block(b, carry):
        even = split(in_ref[pl.ds(b, 256, stride=8), :])
        odd = split(in_ref[pl.ds(2048 + b, 256, stride=8), :])
        even = product(even, (table_ref[0], table_ref[1]), TN)
        odd = product(odd, (table_ref[2], table_ref[3]), TN)
        value = jnp.concatenate([even + odd, even - odd], 1)
        for low in range(4):
            for cells in range(4):
                first = low * 32 + cells * 8
                for tile in range(4):
                    place = pl.ds(cells * 8 * PITCH + 4 * b + low, 8, stride=PITCH)
                    grid_ref[tile, place, :] = value[
                        first : first + 8, tile * 128 : (tile + 1) * 128
                    ]
        return carry

    lax.fori_loop(0, 8, block, 0, unroll=4)

    def source(s, carry):
        lane = lanes_of((16, 128))
        group = lane >> 5
        first_half = jnp.zeros((16, 128), F32)
        second_half = jnp.zeros((16, 128), F32)
        past_half = jnp.zeros((16, 128), F32)
        for f in range(2):
            for first in (0, 32):
                number = first + 2 * s + f
                odd = info_ref[number, 0] & 1
                cell_z = info_ref[number, 2]
                tile = cell_z >> 3
                after = (tile + 1) & 3
                offset = (cell_z & 7) * 16
                for r in range(2):
                    row = (info_ref[number, 1] + r) & 31
                    shift = (64 * f + 32 * r + 128 - offset) & 127
                    wanted = group == 2 * f + r

                    def rows_at(start):
                        place = pl.ds(pl.multiple_of(row * PITCH + start, 8), 16)
                        value = jnp.where(
                            lane >= offset, grid_ref[tile, place, :], grid_ref[after, place, :]
                        )
                        return jnp.where(wanted, pltpu.roll(value, shift, 1), 0.0)

                    if first:
                        past_half += rows_at(0) * (odd == 1).astype(F32)
                    else:
                        first_half += rows_at(odd * 16)
                        second_half += rows_at(16) * (odd == 0).astype(F32)
        own_ref[s, 0:16, :] = first_half
        own_ref[s, 16:32, :] = second_half
        past_ref[s] = past_half
        return carry

    lax.fori_loop(0, 16, source, 0, unroll=2)


def boxes(info, waves, table):
    return pl.pallas_call(
        boxes_kernel,
        grid=(1,),
        in_specs=[
            pl.BlockSpec(memory_space=pltpu.SMEM),
            pl.BlockSpec(memory_space=pltpu.VMEM),
            pl.BlockSpec((4, 256, 256), lambda i: (0, 0, 0)),
        ],
        out_specs=[pl.BlockSpec(memory_space=pltpu.VMEM)] * 2,
        out_shape=[
            jax.ShapeDtypeStruct((16, 32, 128), F32),
            jax.ShapeDtypeStruct((16, 16, 128), F32),
        ],
        scratch_shapes=[pltpu.VMEM((4, 32 * PITCH, 128), F32)],
        compiler_params=pltpu.CompilerParams(vmem_limit_bytes=VMEM_LIMIT),
        name="boxes",
    )(info, waves, table)


def layout_kernel(info_ref, in_ref, out_ref):
    row = lax.broadcasted_iota(jnp.int32, (32, 128), 0)
    lane = lanes_of((32, 128))
    for quad in range(4):
        parts = exchange([in_ref[4 * quad + i] for i in range(4)])
        for f in range(2):
            for r in range(2):
                inside = (
                    (row < info_ref[f, 3] * 16)
                    & (16 * r + 4 * quad + (lane >> 5) < info_ref[f, 4] * 16)
                    & ((lane & 31) < info_ref[f, 5] * 16)
                )
                out_ref[pl.ds((4 * r + quad) * 2 + f, 32, stride=16), :] = jnp.where(
                    inside, parts[2 * f + r], 0.0
                )


def lay_out(info, pieces):
    return pl.pallas_call(
        layout_kernel,
        in_specs=[
            pl.BlockSpec(memory_space=pltpu.SMEM),
            pl.BlockSpec(memory_space=pltpu.VMEM),
        ],
        out_specs=pl.BlockSpec(memory_space=pltpu.VMEM),
        out_shape=jax.ShapeDtypeStruct((512, 128), F32),
        compiler_params=pltpu.CompilerParams(vmem_limit_bytes=VMEM_LIMIT),
        name="lay_out",
    )(info, pieces)


def along_frag(block, distance):
    devices = range(lax.axis_size("frag"))
    route = [(i, (i + distance) % len(devices)) for i in devices]
    return lax.ppermute(block, "frag", route)


def traded(block, axis):
    return lax.all_to_all(block, axis, split_axis=0, concat_axis=0, tiled=True)


def body(background, orbitals, frag_info):
    tables = jnp.asarray(wave_tables())
    place = (lax.axis_index("frag") * 16 + lax.axis_index("grp")).astype(jnp.int32).reshape(1)
    frag_info, place = lax.optimization_barrier((frag_info, place))
    coeffs = orbitals.reshape(16, 256, 32)
    own = traded(densities(frag_info, coeffs), "grp")
    past = along_frag(own[:, 16:40, :], 1)
    info = jnp.concatenate([own[:, 32, :16], past[:, 16, :16]]).astype(jnp.int32).reshape(64, 8)
    region = deposits(info, own, past)
    held = traded(region.reshape(16, 256, 128), "grp").reshape(128, 32, 128)
    total_density, spectrum = forward_z(background, held, tables)
    spectrum = traded(spectrum.reshape(256, 16, 128), BOTH).reshape(16, 16, 2, 8, 128)
    spectrum = solve_planes(place, spectrum, tables)
    spectrum = traded(spectrum.reshape(256, 16, 128), BOTH).reshape(4096, 128)
    pieces, beyond = boxes(info, spectrum, tables)
    beyond = along_frag(beyond, -1)
    pieces = pieces + jnp.pad(beyond, ((0, 0), (16, 0), (0, 0)))
    pieces = lay_out(frag_info, traded(pieces, "grp"))
    frag_potential = pieces.reshape(256, 2, 128).transpose(1, 0, 2).reshape(2, 32768)
    return total_density, frag_potential


def solution(mesh):
    return jax.shard_map(
        body,
        mesh=mesh,
        in_specs=(
            P("frag", "grp", None),
            P(None, None, None, ("frag", "grp")),
            P(("frag", "grp"), None),
        ),
        out_specs=(P("frag", "grp", None), P(("frag", "grp"), None)),
        check_vma=False,
    )
```

```python
import math

import jax
import jax.numpy as jnp
import ml_dtypes
import numpy as np
from jax import lax
from jax.experimental import pallas as pl
from jax.experimental.pallas import tpu as pltpu
from jax.sharding import PartitionSpec as P

NG = 512
SPACING = 0.2
F32 = jnp.float32
BF16 = jnp.bfloat16
BOTH = ("frag", "grp")
PITCH = 40
VMEM_LIMIT = 24 * 1024 * 1024


def halves(table):
    high = table.astype(ml_dtypes.bfloat16)
    low = (table - high.astype(np.float64)).astype(ml_dtypes.bfloat16)
    return np.stack([high, low])


def synthesis_table(span):
    frequency = np.arange(16)[:, None] - 8
    point = np.arange(32)[None, :]
    angle = 2.0 * math.pi * np.mod(frequency * point, span * 16) / (span * 16)
    live = (frequency >= -4 * span) & (frequency < 4 * span) & (point < 16 * span)
    return np.where(live, (np.cos(angle) + np.sin(angle)) * math.sqrt(2.0 / 16) / span, 0.0)


def plane_tables():
    tables = []
    for span_y in (1, 2):
        for span_z in (1, 2):
            table_y = synthesis_table(span_y).reshape(16, 2, 16)
            table_z = synthesis_table(span_z)
            full = np.einsum("brg,cz->bcgrz", table_y, table_z)
            tables.append(halves(full.reshape(256, 1024)))
    return np.stack(tables)


def depth_tables():
    tables = []
    for span in (1, 2):
        full = np.einsum("ax,mn->mxan", synthesis_table(span), np.eye(16))
        tables.append(halves(full.reshape(512, 256)))
    return np.stack(tables)


def cas(rows, columns):
    angle = 2.0 * math.pi / NG * np.mod(rows[:, None] * columns[None, :], NG)
    return np.cos(angle) + np.sin(angle)


def row_order():
    block, low, high = np.meshgrid(np.arange(16), np.arange(4), np.arange(8), indexing="ij")
    return (block * 32 + high * 4 + low).reshape(-1)


def wave_tables():
    start = np.arange(256)
    even, odd = 2 * start, 2 * start + 1
    rows = row_order()[:256]
    tables = [
        cas(even, start),
        cas(odd, start),
        cas(start, odd),
        cas(even, rows),
        cas(odd, rows),
    ]
    return np.concatenate([halves(table) for table in tables])


def window_table():
    waves = np.concatenate([np.arange(0, NG, 2), np.arange(1, NG, 2)])
    return halves(cas(np.arange(NG + 64) % NG, waves))


def split(value):
    high = value.astype(BF16)
    return high, (value - high.astype(F32)).astype(BF16)


def product(left, right, dims):
    dims = (dims, ((), ()))
    total = lax.dot_general(left[0], right[1], dims, preferred_element_type=F32)
    total += lax.dot_general(left[1], right[0], dims, preferred_element_type=F32)
    return total + lax.dot_general(left[0], right[0], dims, preferred_element_type=F32)


NN = ((1,), (0,))
NT = ((1,), (1,))
TN = ((0,), (0,))


def lanes_of(shape):
    return lax.broadcasted_iota(jnp.int32, shape, len(shape) - 1)


def exchange(parts):
    lane = lanes_of(parts[0].shape)
    low = lane < 64
    even = (lane & 32) == 0

    def swapped(first, second):
        crossed = pltpu.roll(jnp.where(low, second, first), 64, 1)
        return jnp.where(low, first, crossed), jnp.where(low, crossed, second)

    a0, a2 = swapped(parts[0], parts[2])
    a1, a3 = swapped(parts[1], parts[3])
    return (
        jnp.where(even, a0, pltpu.roll(a1, 32, 1)),
        jnp.where(even, pltpu.roll(a0, 96, 1), a1),
        jnp.where(even, a2, pltpu.roll(a3, 32, 1)),
        jnp.where(even, pltpu.roll(a2, 96, 1), a3),
    )


def density_kernel(
    info_ref, orbitals_ref, planes_ref, depths_ref, out_ref, coeff_ref, plane_ref, depth_ref, sems
):
    copies = []
    for f in range(2):
        pair = 2 * info_ref[f, 4] + info_ref[f, 5] - 3
        copies.append(pltpu.make_async_copy(planes_ref.at[pair], plane_ref.at[f], sems.at[2 * f]))
        copies.append(
            pltpu.make_async_copy(
                depths_ref.at[info_ref[f, 3] - 1], depth_ref.at[f], sems.at[2 * f + 1]
            )
        )
    for copy in copies:
        copy.start()
    for a in range(16):
        coeff_ref[a] = jnp.transpose(orbitals_ref[a].astype(F32)).astype(BF16)
    for f in range(2):
        count = info_ref[f, 7]
        scale = 2.0 * info_ref[f, 6].astype(F32)
        coeffs = coeff_ref[:, 16 * f : 16 * f + 16, :].reshape(256, 256)
        copies[2 * f].wait()
        copies[2 * f + 1].wait()
        for part in range(4):
            columns = slice(part * 256, (part + 1) * 256)
            flat = jnp.dot(coeffs, plane_ref[f, 1, :, columns], preferred_element_type=F32)
            flat += jnp.dot(coeffs, plane_ref[f, 0, :, columns], preferred_element_type=F32)
            psi = product((depth_ref[f, 0], depth_ref[f, 1]), split(flat), NN)
            total = jnp.zeros((32, 256), F32)
            for m in range(16):
                orbital = psi[m * 32 : (m + 1) * 32]
                total += orbital * orbital * (m < count).astype(F32)
            total = total * scale
            for tile in range(2):
                here = total[:, tile * 128 : (tile + 1) * 128]
                turned = pltpu.roll(here, 64, 1)
                owner = 2 * (2 * part + tile)
                low = lanes_of(here.shape) < 64
                if f == 0:
                    out_ref[owner, 0:32, :] = here
                    out_ref[owner + 1, 0:32, :] = turned
                else:
                    out_ref[owner, 0:32, :] = jnp.where(low, out_ref[owner, 0:32, :], turned)
                    out_ref[owner + 1, 0:32, :] = jnp.where(low, out_ref[owner + 1, 0:32, :], here)
    lane = lanes_of((8, 128))
    note = jnp.zeros((8, 128), F32)
    for place in range(16):
        note = jnp.where(lane == place, info_ref[place // 8, place % 8].astype(F32), note)
    for owner in range(16):
        out_ref[owner, 32:40, :] = note


def densities(info, orbitals):
    planes = jnp.asarray(plane_tables())
    depths = jnp.asarray(depth_tables())
    return pl.pallas_call(
        density_kernel,
        in_specs=[
            pl.BlockSpec(memory_space=pltpu.SMEM),
            pl.BlockSpec(memory_space=pltpu.VMEM),
            pl.BlockSpec(memory_space=pl.ANY),
            pl.BlockSpec(memory_space=pl.ANY),
        ],
        out_specs=pl.BlockSpec(memory_space=pltpu.VMEM),
        out_shape=jax.ShapeDtypeStruct((16, 40, 128), F32),
        scratch_shapes=[
            pltpu.VMEM((16, 32, 256), BF16),
            pltpu.VMEM((2, 2, 256, 1024), BF16),
            pltpu.VMEM((2, 2, 512, 256), BF16),
            pltpu.SemaphoreType.DMA((4,)),
        ],
        compiler_params=pltpu.CompilerParams(vmem_limit_bytes=56 * 1024 * 1024),
        name="densities",
    )(info, orbitals, planes, depths)


def first_cell(info_ref):
    def touched(number):
        cell = info_ref[number, 1]
        return cell >> 1, ((cell + info_ref[number, 4] - 1) & 31) >> 1

    first, last = touched(0)
    shared = jnp.int32(1)
    for number in range(1, 32):
        one, other = touched(number)
        shared = shared * ((one == first) | (other == first)).astype(jnp.int32)
    return (2 * jnp.where(shared == 1, first, last) + 31) & 31


def deposit_kernel(info_ref, own_ref, past_ref, out_ref, cell_ref):
    cell_ref[...] = jnp.full((8, 128), first_cell(info_ref).astype(F32))
    out_ref[...] = jnp.zeros(out_ref.shape, F32)

    def source(s, carry):
        own = own_ref[s, 0:32, :]
        past = past_ref[s, 0:16, :]
        lane = lanes_of((16, 128))
        adds = []
        for f in range(2):
            for first, piece in ((0, own), (32, past)):
                number = first + 2 * s + f
                odd = info_ref[number, 0] & 1
                cell_y = info_ref[number, 1]
                cell_z = info_ref[number, 2]
                tile = cell_z >> 3
                after = (tile + 1) & 3
                offset = (cell_z & 7) * 16
                kept = odd == 1 if first else odd == 0
                low = jnp.where(kept, offset, 256)
                part_inside = (lane >= low) & (lane < low + 32)
                part_beyond = lane < jnp.where(kept, offset - 96, 0)
                inside = (lane >= offset) & (lane < offset + 32)
                beyond = lane < offset - 96
                for r in range(2):
                    row = (cell_y + r) & 31
                    turned = pltpu.roll(piece, (offset + 128 - (64 * f + 32 * r)) & 127, 1)
                    if first:
                        adds.append((row, tile, 0, jnp.where(part_inside, turned, 0.0)))
                        adds.append((row, after, 0, jnp.where(part_beyond, turned, 0.0)))
                    else:
                        start = pl.multiple_of(odd * 16, 16)
                        top, rest = turned[0:16], turned[16:32]
                        adds.append((row, tile, start, jnp.where(inside, top, 0.0)))
                        adds.append((row, after, start, jnp.where(beyond, top, 0.0)))
                        adds.append((row, tile, 16, jnp.where(part_inside, rest, 0.0)))
                        adds.append((row, after, 16, jnp.where(part_beyond, rest, 0.0)))
        for row, tile, start, value in adds:
            out_ref[row, tile, pl.ds(start, 16), :] += value
        return carry

    lax.fori_loop(0, 16, source, 0, unroll=2)


def deposits(info, own, past):
    return pl.pallas_call(
        deposit_kernel,
        in_specs=[
            pl.BlockSpec(memory_space=pltpu.SMEM),
            pl.BlockSpec(memory_space=pltpu.VMEM),
            pl.BlockSpec(memory_space=pltpu.VMEM),
        ],
        out_specs=[pl.BlockSpec(memory_space=pltpu.VMEM)] * 2,
        out_shape=[
            jax.ShapeDtypeStruct((32, 4, 32, 128), F32),
            jax.ShapeDtypeStruct((8, 128), F32),
        ],
        compiler_params=pltpu.CompilerParams(vmem_limit_bytes=VMEM_LIMIT),
        name="deposits",
    )(info, own, past)


def forward_kernel(back_ref, held_ref, table_ref, total_ref, out_ref, turned_ref):
    b = pl.program_id(0)
    for g in range(16):
        for jj in range(2):
            for tile in range(4):
                turned_ref[tile, pl.ds(jj * 16 + g, 8, stride=PITCH), :] = held_ref[
                    (g * 2 + jj) * 4 + tile
                ]
    for tile in range(4):
        columns = slice(tile * 128, (tile + 1) * 128)
        for x in range(8):
            total_ref[x, :, columns] = (
                back_ref[x, :, columns] + turned_ref[tile, x * PITCH : x * PITCH + 32, :]
            )
    total = total_ref[...].reshape(256, 512)
    near, far = total[:, :256], total[:, 256:]
    for parity, value in ((0, near + far), (1, near - far)):
        table = (table_ref[2 * parity], table_ref[2 * parity + 1])
        waves = product(table, split(value), NT)
        for tile in range(2):
            place = pl.ds(2048 * parity + 2 * b + tile, 256, stride=8)
            out_ref[place, :] = waves[:, tile * 128 : (tile + 1) * 128]


def forward_z(background, held, table):
    return pl.pallas_call(
        forward_kernel,
        grid=(4,),
        in_specs=[
            pl.BlockSpec((8, 32, 512), lambda b: (b, 0, 0)),
            pl.BlockSpec((128, 8, 128), lambda b: (0, b, 0)),
            pl.BlockSpec((4, 256, 256), lambda b: (0, 0, 0)),
        ],
        out_specs=[
            pl.BlockSpec((8, 32, 512), lambda b: (b, 0, 0)),
            pl.BlockSpec((4096, 128), lambda b: (0, 0)),
        ],
        out_shape=[
            jax.ShapeDtypeStruct((32, 32, 512), F32),
            jax.ShapeDtypeStruct((4096, 128), F32),
        ],
        scratch_shapes=[pltpu.VMEM((4, 8 * PITCH, 128), F32)],
        compiler_params=pltpu.CompilerParams(vmem_limit_bytes=VMEM_LIMIT),
        name="forward_z",
    )(background, held, table)


def planes_kernel(place_ref, cells_ref, in_ref, tables_ref, window_ref, out_ref, grid_ref, wave_ref):
    kk = pl.program_id(0)

    def table(i):
        return tables_ref[2 * i], tables_ref[2 * i + 1]

    for quad in range(4):
        parts = [in_ref[:, 4 * quad + i, 0].reshape(128, 128) for i in range(4)]
        for i, part in enumerate(exchange(parts)):
            grid_ref[:, i, :, quad * 128 : (quad + 1) * 128] = part.reshape(16, 8, 128)
    grid = grid_ref[...].reshape(512, 512)
    near, far = grid[:, :256], grid[:, 256:]
    value = jnp.concatenate(
        [product(split(near + far), table(0), NN), product(split(near - far), table(2), NN)], 1
    )
    near, far = value[:256], value[256:]
    value = jnp.concatenate(
        [product(table(3), split(near + far), NN), product(table(4), split(near - far), NN)], 0
    )

    def folded(place):
        wave = jnp.where(place < 256, 2 * place, 2 * place - 511)
        lowest = jnp.minimum(wave, NG - wave)
        return lowest * lowest

    square = (
        folded(lax.broadcasted_iota(jnp.int32, (NG, 1), 0))
        + folded(lax.broadcasted_iota(jnp.int32, (1, NG), 1))
        + folded(2 * place_ref[0] + kk)
    )
    factor = (NG * SPACING) ** 2 / math.pi / float(NG) ** 3
    value = value * jnp.where(square > 0, factor / jnp.maximum(square, 1).astype(F32), 0.0)
    even = product(table(0), split(value[:256]), NN)
    odd = product(table(2), split(value[256:]), NN)
    for i, value in enumerate(split(jnp.concatenate([even + odd, even - odd, even[:32] + odd[:32]]))):
        wave_ref[i] = value
    lane = lanes_of((16, 128))
    for group in range(16):
        place = pl.ds(pl.multiple_of(cells_ref[group] * 16, 16), 64)
        window = (window_ref[0, place, :], window_ref[1, place, :])
        rows = slice(group * 32, group * 32 + 64)
        value = product(window, (wave_ref[0, rows, :], wave_ref[1, rows, :]), NT)
        for half in range(2):
            joined = jnp.zeros((16, 128), F32)
            for cell in range(4):
                piece = jnp.concatenate([value[16 * cell : 16 * cell + 16]] * 2, 1)
                piece = pltpu.roll(piece, (32 * (cell - half)) % 128, 1)
                joined = jnp.where((lane >> 5) == cell, piece, joined)
            out_ref[pl.ds(group * 64 + 2 * kk + half, 16, stride=4), :] = joined


def solve_planes(place, cells, waves, tables, window):
    return pl.pallas_call(
        planes_kernel,
        grid=(2,),
        in_specs=[
            pl.BlockSpec(memory_space=pltpu.SMEM),
            pl.BlockSpec(memory_space=pltpu.SMEM),
            pl.BlockSpec((16, 16, 1, 8, 128), lambda kk: (0, 0, kk, 0, 0)),
            pl.BlockSpec(memory_space=pltpu.VMEM),
            pl.BlockSpec(memory_space=pltpu.VMEM),
        ],
        out_specs=pl.BlockSpec((1024, 128), lambda kk: (0, 0)),
        out_shape=jax.ShapeDtypeStruct((1024, 128), F32),
        scratch_shapes=[pltpu.VMEM((16, 4, 8, 512), F32), pltpu.VMEM((2, 544, 512), BF16)],
        compiler_params=pltpu.CompilerParams(vmem_limit_bytes=VMEM_LIMIT),
        name="solve_planes",
    )(place, cells, waves, tables, window)


def boxes_kernel(info_ref, in_ref, table_ref, out_ref, grid_ref):
    for half in range(2):
        even = split(in_ref[pl.ds(half, 256, stride=2), :])
        odd = split(in_ref[pl.ds(512 + half, 256, stride=2), :])
        even = product(even, (table_ref[0], table_ref[1]), TN)
        odd = product(odd, (table_ref[2], table_ref[3]), TN)
        for cell in range(4):
            first = 32 * cell
            for tile in range(4):
                columns = slice(tile % 2 * 128, tile % 2 * 128 + 128)
                near, far = even[first : first + 32, columns], odd[first : first + 32, columns]
                place = slice(64 * cell + 32 * half, 64 * cell + 32 * half + 32)
                grid_ref[tile, place, :] = near + far if tile < 2 else near - far
    base = first_cell(info_ref)

    def source(s, carry):
        lane = lanes_of((32, 128))
        group = lane >> 5
        total = jnp.zeros((32, 128), F32)
        for f in range(2):
            number = 2 * s + f
            start = (info_ref[number, 0] & 1) * 16
            cell_z = info_ref[number, 2]
            tile = cell_z >> 3
            after = (tile + 1) & 3
            offset = (cell_z & 7) * 16
            for r in range(2):
                cell = (info_ref[number, 1] + r - base) & 3
                place = pl.ds(pl.multiple_of(cell * 64 + start, 16), 32)
                value = jnp.where(
                    lane >= offset, grid_ref[tile, place, :], grid_ref[after, place, :]
                )
                value = pltpu.roll(value, (64 * f + 32 * r + 128 - offset) & 127, 1)
                total = jnp.where(group == 2 * f + r, value, total)
        out_ref[s] = total
        return carry

    lax.fori_loop(0, 16, source, 0, unroll=2)


def boxes(info, waves, table):
    return pl.pallas_call(
        boxes_kernel,
        grid=(1,),
        in_specs=[
            pl.BlockSpec(memory_space=pltpu.SMEM),
            pl.BlockSpec(memory_space=pltpu.VMEM),
            pl.BlockSpec((4, 256, 256), lambda i: (0, 0, 0)),
        ],
        out_specs=pl.BlockSpec(memory_space=pltpu.VMEM),
        out_shape=jax.ShapeDtypeStruct((16, 32, 128), F32),
        scratch_shapes=[pltpu.VMEM((4, 256, 128), F32)],
        compiler_params=pltpu.CompilerParams(vmem_limit_bytes=VMEM_LIMIT),
        name="boxes",
    )(info, waves, table)


def layout_kernel(info_ref, in_ref, out_ref):
    row = lax.broadcasted_iota(jnp.int32, (32, 128), 0)
    lane = lanes_of((32, 128))
    for quad in range(4):
        parts = exchange([in_ref[4 * quad + i] for i in range(4)])
        for f in range(2):
            for r in range(2):
                inside = (
                    (row < info_ref[f, 3] * 16)
                    & (16 * r + 4 * quad + (lane >> 5) < info_ref[f, 4] * 16)
                    & ((lane & 31) < info_ref[f, 5] * 16)
                )
                out_ref[pl.ds((4 * r + quad) * 2 + f, 32, stride=16), :] = jnp.where(
                    inside, parts[2 * f + r], 0.0
                )


def lay_out(info, pieces):
    return pl.pallas_call(
        layout_kernel,
        in_specs=[
            pl.BlockSpec(memory_space=pltpu.SMEM),
            pl.BlockSpec(memory_space=pltpu.VMEM),
        ],
        out_specs=pl.BlockSpec(memory_space=pltpu.VMEM),
        out_shape=jax.ShapeDtypeStruct((512, 128), F32),
        compiler_params=pltpu.CompilerParams(vmem_limit_bytes=VMEM_LIMIT),
        name="lay_out",
    )(info, pieces)


def along_frag(block, distance):
    devices = range(lax.axis_size("frag"))
    route = [(i, (i + distance) % len(devices)) for i in devices]
    return lax.ppermute(block, "frag", route)


def traded(block, axis):
    return lax.all_to_all(block, axis, split_axis=0, concat_axis=0, tiled=True)


def body(background, orbitals, frag_info):
    tables, window = jnp.asarray(wave_tables()), jnp.asarray(window_table())
    place = (lax.axis_index("frag") * 16 + lax.axis_index("grp")).astype(jnp.int32).reshape(1)
    frag_info, place = lax.optimization_barrier((frag_info, place))
    coeffs = orbitals.reshape(16, 256, 32)
    own = traded(densities(frag_info, coeffs), "grp")
    past = along_frag(own[:, 16:40, :], 1)
    info = jnp.concatenate([own[:, 32, :16], past[:, 16, :16]]).astype(jnp.int32).reshape(64, 8)
    region, cell = deposits(info, own, past)
    cells = lax.all_gather(cell, BOTH, axis=0, tiled=True)[::128, 0].astype(jnp.int32)
    held = traded(region.reshape(16, 256, 128), "grp").reshape(128, 32, 128)
    total_density, spectrum = forward_z(background, held, tables)
    spectrum = traded(spectrum.reshape(256, 16, 128), BOTH).reshape(16, 16, 2, 8, 128)
    spectrum = solve_planes(place, cells, spectrum, tables, window)
    spectrum = traded(spectrum.reshape(256, 4, 128), BOTH).reshape(1024, 128)
    pieces = boxes(info, spectrum, tables)
    pieces = lay_out(frag_info, traded(pieces, "grp"))
    frag_potential = pieces.reshape(256, 2, 128).transpose(1, 0, 2).reshape(2, 32768)
    return total_density, frag_potential


def solution(mesh):
    return jax.shard_map(
        body,
        mesh=mesh,
        in_specs=(
            P("frag", "grp", None),
            P(None, None, None, ("frag", "grp")),
            P(("frag", "grp"), None),
        ),
        out_specs=(P("frag", "grp", None), P(("frag", "grp"), None)),
        check_vma=False,
    )
```

```python
import math

import jax
import jax.numpy as jnp
import ml_dtypes
import numpy as np
from jax import lax
from jax.experimental import pallas as pl
from jax.experimental.pallas import tpu as pltpu
from jax.sharding import PartitionSpec as P

NG = 512
SPACING = 0.2
F32 = jnp.float32
BF16 = jnp.bfloat16
BOTH = ("frag", "grp")
PITCH = 40
VMEM_LIMIT = 24 * 1024 * 1024


def halves(table):
    high = table.astype(ml_dtypes.bfloat16)
    low = (table - high.astype(np.float64)).astype(ml_dtypes.bfloat16)
    return np.stack([high, low])


def synthesis_table(span):
    frequency = np.arange(16)[:, None] - 8
    point = np.arange(32)[None, :]
    angle = 2.0 * math.pi * np.mod(frequency * point, span * 16) / (span * 16)
    live = (frequency >= -4 * span) & (frequency < 4 * span) & (point < 16 * span)
    return np.where(live, (np.cos(angle) + np.sin(angle)) * math.sqrt(2.0 / 16) / span, 0.0)


def plane_tables():
    tables = []
    for span_y in (1, 2):
        for span_z in (1, 2):
            table_y = synthesis_table(span_y).reshape(16, 2, 16)
            table_z = synthesis_table(span_z)
            full = np.einsum("brg,cz->bcgrz", table_y, table_z)
            tables.append(halves(full.reshape(256, 1024)))
    return np.stack(tables)


def depth_tables():
    tables = []
    for span in (1, 2):
        full = np.einsum("ax,mn->mxan", synthesis_table(span), np.eye(16))
        tables.append(halves(full.reshape(512, 256)))
    return np.stack(tables)


def cas(rows, columns):
    angle = 2.0 * math.pi / NG * np.mod(rows[:, None] * columns[None, :], NG)
    return np.cos(angle) + np.sin(angle)


def row_order():
    block, low, high = np.meshgrid(np.arange(16), np.arange(4), np.arange(8), indexing="ij")
    return (block * 32 + high * 4 + low).reshape(-1)


def wave_tables():
    start = np.arange(256)
    even, odd = 2 * start, 2 * start + 1
    rows = row_order()[:256]
    tables = [
        cas(even, start),
        cas(odd, start),
        cas(start, odd),
        cas(even, rows),
        cas(odd, rows),
    ]
    return np.concatenate([halves(table) for table in tables])


def window_table():
    waves = np.concatenate([np.arange(0, NG, 2), np.arange(1, NG, 2)])
    return halves(cas(np.arange(NG + 64) % NG, waves))


def split(value):
    high = value.astype(BF16)
    return high, (value - high.astype(F32)).astype(BF16)


def product(left, right, dims):
    dims = (dims, ((), ()))
    total = lax.dot_general(left[0], right[1], dims, preferred_element_type=F32)
    total += lax.dot_general(left[1], right[0], dims, preferred_element_type=F32)
    return total + lax.dot_general(left[0], right[0], dims, preferred_element_type=F32)


NN = ((1,), (0,))
NT = ((1,), (1,))
TN = ((0,), (0,))


def lanes_of(shape):
    return lax.broadcasted_iota(jnp.int32, shape, len(shape) - 1)


def exchange(parts):
    lane = lanes_of(parts[0].shape)
    low = lane < 64
    even = (lane & 32) == 0

    def swapped(first, second):
        crossed = pltpu.roll(jnp.where(low, second, first), 64, 1)
        return jnp.where(low, first, crossed), jnp.where(low, crossed, second)

    a0, a2 = swapped(parts[0], parts[2])
    a1, a3 = swapped(parts[1], parts[3])
    return (
        jnp.where(even, a0, pltpu.roll(a1, 32, 1)),
        jnp.where(even, pltpu.roll(a0, 96, 1), a1),
        jnp.where(even, a2, pltpu.roll(a3, 32, 1)),
        jnp.where(even, pltpu.roll(a2, 96, 1), a3),
    )


def density_kernel(
    info_ref, orbitals_ref, planes_ref, depths_ref, out_ref, coeff_ref, plane_ref, depth_ref, sems
):
    copies = []
    for f in range(2):
        pair = 2 * info_ref[f, 4] + info_ref[f, 5] - 3
        copies.append(pltpu.make_async_copy(planes_ref.at[pair], plane_ref.at[f], sems.at[2 * f]))
        copies.append(
            pltpu.make_async_copy(
                depths_ref.at[info_ref[f, 3] - 1], depth_ref.at[f], sems.at[2 * f + 1]
            )
        )
    for copy in copies:
        copy.start()
    for a in range(16):
        coeff_ref[a] = jnp.transpose(orbitals_ref[a].astype(F32)).astype(BF16)
    for f in range(2):
        count = info_ref[f, 7]
        scale = 2.0 * info_ref[f, 6].astype(F32)
        coeffs = coeff_ref[:, 16 * f : 16 * f + 16, :].reshape(256, 256)
        copies[2 * f].wait()
        copies[2 * f + 1].wait()
        for part in range(4):
            columns = slice(part * 256, (part + 1) * 256)
            flat = jnp.dot(coeffs, plane_ref[f, 1, :, columns], preferred_element_type=F32)
            flat += jnp.dot(coeffs, plane_ref[f, 0, :, columns], preferred_element_type=F32)
            psi = product((depth_ref[f, 0], depth_ref[f, 1]), split(flat), NN)
            total = jnp.zeros((32, 256), F32)
            for m in range(16):
                orbital = psi[m * 32 : (m + 1) * 32]
                total += orbital * orbital * (m < count).astype(F32)
            total = total * scale
            for tile in range(2):
                here = total[:, tile * 128 : (tile + 1) * 128]
                turned = pltpu.roll(here, 64, 1)
                owner = 2 * (2 * part + tile)
                low = lanes_of(here.shape) < 64
                if f == 0:
                    out_ref[owner, 0:32, :] = here
                    out_ref[owner + 1, 0:32, :] = turned
                else:
                    out_ref[owner, 0:32, :] = jnp.where(low, out_ref[owner, 0:32, :], turned)
                    out_ref[owner + 1, 0:32, :] = jnp.where(low, out_ref[owner + 1, 0:32, :], here)
    lane = lanes_of((8, 128))
    note = jnp.zeros((8, 128), F32)
    for place in range(16):
        note = jnp.where(lane == place, info_ref[place // 8, place % 8].astype(F32), note)
    for owner in range(16):
        out_ref[owner, 32:40, :] = note


def densities(info, orbitals):
    planes = jnp.asarray(plane_tables())
    depths = jnp.asarray(depth_tables())
    return pl.pallas_call(
        density_kernel,
        in_specs=[
            pl.BlockSpec(memory_space=pltpu.SMEM),
            pl.BlockSpec(memory_space=pltpu.VMEM),
            pl.BlockSpec(memory_space=pl.ANY),
            pl.BlockSpec(memory_space=pl.ANY),
        ],
        out_specs=pl.BlockSpec(memory_space=pltpu.VMEM),
        out_shape=jax.ShapeDtypeStruct((16, 40, 128), F32),
        scratch_shapes=[
            pltpu.VMEM((16, 32, 256), BF16),
            pltpu.VMEM((2, 2, 256, 1024), BF16),
            pltpu.VMEM((2, 2, 512, 256), BF16),
            pltpu.SemaphoreType.DMA((4,)),
        ],
        compiler_params=pltpu.CompilerParams(vmem_limit_bytes=56 * 1024 * 1024),
        name="densities",
    )(info, orbitals, planes, depths)


def first_cell(info_ref):
    def touched(number):
        cell = info_ref[number, 1]
        return cell >> 1, ((cell + info_ref[number, 4] - 1) & 31) >> 1

    first, last = touched(0)
    shared = jnp.int32(1)
    for number in range(1, 32):
        one, other = touched(number)
        shared = shared * ((one == first) | (other == first)).astype(jnp.int32)
    return (2 * jnp.where(shared == 1, first, last) + 31) & 31


def deposit_kernel(info_ref, own_ref, past_ref, out_ref, cell_ref):
    cell_ref[...] = jnp.full((8, 128), first_cell(info_ref).astype(F32))
    out_ref[...] = jnp.zeros(out_ref.shape, F32)

    def source(s, carry):
        own = own_ref[s, 0:32, :]
        past = past_ref[s, 0:16, :]
        lane = lanes_of((16, 128))
        adds = []
        for f in range(2):
            for first, piece in ((0, own), (32, past)):
                number = first + 2 * s + f
                odd = info_ref[number, 0] & 1
                cell_y = info_ref[number, 1]
                cell_z = info_ref[number, 2]
                tile = cell_z >> 3
                after = (tile + 1) & 3
                offset = (cell_z & 7) * 16
                kept = odd == 1 if first else odd == 0
                low = jnp.where(kept, offset, 256)
                part_inside = (lane >= low) & (lane < low + 32)
                part_beyond = lane < jnp.where(kept, offset - 96, 0)
                inside = (lane >= offset) & (lane < offset + 32)
                beyond = lane < offset - 96
                for r in range(2):
                    row = (cell_y + r) & 31
                    turned = pltpu.roll(piece, (offset + 128 - (64 * f + 32 * r)) & 127, 1)
                    if first:
                        adds.append((row, tile, 0, jnp.where(part_inside, turned, 0.0)))
                        adds.append((row, after, 0, jnp.where(part_beyond, turned, 0.0)))
                    else:
                        start = pl.multiple_of(odd * 16, 16)
                        top, rest = turned[0:16], turned[16:32]
                        adds.append((row, tile, start, jnp.where(inside, top, 0.0)))
                        adds.append((row, after, start, jnp.where(beyond, top, 0.0)))
                        adds.append((row, tile, 16, jnp.where(part_inside, rest, 0.0)))
                        adds.append((row, after, 16, jnp.where(part_beyond, rest, 0.0)))
        for row, tile, start, value in adds:
            out_ref[row, tile, pl.ds(start, 16), :] += value
        return carry

    lax.fori_loop(0, 16, source, 0, unroll=2)


def deposits(info, own, past):
    return pl.pallas_call(
        deposit_kernel,
        in_specs=[
            pl.BlockSpec(memory_space=pltpu.SMEM),
            pl.BlockSpec(memory_space=pltpu.VMEM),
            pl.BlockSpec(memory_space=pltpu.VMEM),
        ],
        out_specs=[pl.BlockSpec(memory_space=pltpu.VMEM)] * 2,
        out_shape=[
            jax.ShapeDtypeStruct((32, 4, 32, 128), F32),
            jax.ShapeDtypeStruct((8, 128), F32),
        ],
        compiler_params=pltpu.CompilerParams(vmem_limit_bytes=VMEM_LIMIT),
        name="deposits",
    )(info, own, past)


def forward_kernel(back_ref, held_ref, table_ref, cell_ref, total_ref, out_ref, turned_ref):
    b = pl.program_id(0)

    @pl.when(b == 0)
    def _():
        out_ref[pl.ds(16, 256, stride=17), :] = jnp.broadcast_to(cell_ref[0:1, :], (256, 128))

    for g in range(16):
        for jj in range(2):
            for tile in range(4):
                turned_ref[tile, pl.ds(jj * 16 + g, 8, stride=PITCH), :] = held_ref[
                    (g * 2 + jj) * 4 + tile
                ]
    for tile in range(4):
        columns = slice(tile * 128, (tile + 1) * 128)
        for x in range(8):
            total_ref[x, :, columns] = (
                back_ref[x, :, columns] + turned_ref[tile, x * PITCH : x * PITCH + 32, :]
            )
    total = total_ref[...].reshape(256, 512)
    near, far = total[:, :256], total[:, 256:]
    for parity, value in ((0, near + far), (1, near - far)):
        table = (table_ref[2 * parity], table_ref[2 * parity + 1])
        waves = product(table, split(value), NT)
        for tile in range(2):
            place = pl.ds(8 * parity + 2 * b + tile, 256, stride=17)
            out_ref[place, :] = waves[:, tile * 128 : (tile + 1) * 128]


def forward_z(background, held, table, cell):
    return pl.pallas_call(
        forward_kernel,
        grid=(4,),
        in_specs=[
            pl.BlockSpec((8, 32, 512), lambda b: (b, 0, 0)),
            pl.BlockSpec((128, 8, 128), lambda b: (0, b, 0)),
            pl.BlockSpec((4, 256, 256), lambda b: (0, 0, 0)),
            pl.BlockSpec((8, 128), lambda b: (0, 0)),
        ],
        out_specs=[
            pl.BlockSpec((8, 32, 512), lambda b: (b, 0, 0)),
            pl.BlockSpec((4352, 128), lambda b: (0, 0)),
        ],
        out_shape=[
            jax.ShapeDtypeStruct((32, 32, 512), F32),
            jax.ShapeDtypeStruct((4352, 128), F32),
        ],
        scratch_shapes=[pltpu.VMEM((4, 8 * PITCH, 128), F32)],
        compiler_params=pltpu.CompilerParams(vmem_limit_bytes=VMEM_LIMIT),
        name="forward_z",
    )(background, held, table, cell)


def planes_kernel(
    place_ref, in_ref, tables_ref, window_ref, out_ref, grid_ref, wave_ref, cells_ref
):
    kk = pl.program_id(0)

    @pl.when(kk == 0)
    def _():
        for group in range(16):
            row = group * 272 + 16
            cells_ref[group] = jnp.max(in_ref[row : row + 1, :]).astype(jnp.int32)

    def table(i):
        return tables_ref[2 * i], tables_ref[2 * i + 1]

    for quad in range(4):
        parts = [
            jnp.concatenate(
                [
                    in_ref[pl.ds((group * 16 + 4 * quad + i) * 17 + 8 * kk, 8), :]
                    for group in range(16)
                ]
            )
            for i in range(4)
        ]
        for i, part in enumerate(exchange(parts)):
            grid_ref[:, i, :, quad * 128 : (quad + 1) * 128] = part.reshape(16, 8, 128)
    grid = grid_ref[...].reshape(512, 512)
    near, far = grid[:, :256], grid[:, 256:]
    value = jnp.concatenate(
        [product(split(near + far), table(0), NN), product(split(near - far), table(2), NN)], 1
    )
    near, far = value[:256], value[256:]
    value = jnp.concatenate(
        [product(table(3), split(near + far), NN), product(table(4), split(near - far), NN)], 0
    )

    def folded(wave):
        lowest = jnp.minimum(wave, NG - wave)
        return lowest * lowest

    def ordered(place):
        return jnp.where(place < 256, 2 * place, 2 * place - 511)

    square = (
        folded(ordered(lax.broadcasted_iota(jnp.int32, (NG, 1), 0)))
        + folded(ordered(lax.broadcasted_iota(jnp.int32, (1, NG), 1)))
        + folded(2 * place_ref[0] + kk)
    )
    factor = (NG * SPACING) ** 2 / math.pi / float(NG) ** 3
    value = value * jnp.where(square > 0, factor / jnp.maximum(square, 1).astype(F32), 0.0)
    even = product(table(0), split(value[:256]), NN)
    odd = product(table(2), split(value[256:]), NN)
    for i, value in enumerate(split(jnp.concatenate([even + odd, even - odd, even[:32] + odd[:32]]))):
        wave_ref[i] = value
    lane = lanes_of((16, 128))
    for group in range(16):
        place = pl.ds(pl.multiple_of(cells_ref[group] * 16, 16), 64)
        window = (window_ref[0, place, :], window_ref[1, place, :])
        rows = slice(group * 32, group * 32 + 64)
        value = product(window, (wave_ref[0, rows, :], wave_ref[1, rows, :]), NT)
        for half in range(2):
            joined = jnp.zeros((16, 128), F32)
            for cell in range(4):
                piece = jnp.concatenate([value[16 * cell : 16 * cell + 16]] * 2, 1)
                piece = pltpu.roll(piece, (32 * (cell - half)) % 128, 1)
                joined = jnp.where((lane >> 5) == cell, piece, joined)
            out_ref[pl.ds(group * 64 + 2 * kk + half, 16, stride=4), :] = joined


def solve_planes(place, waves, tables, window):
    return pl.pallas_call(
        planes_kernel,
        grid=(2,),
        in_specs=[
            pl.BlockSpec(memory_space=pltpu.SMEM),
            pl.BlockSpec(memory_space=pltpu.VMEM),
            pl.BlockSpec(memory_space=pltpu.VMEM),
            pl.BlockSpec(memory_space=pltpu.VMEM),
        ],
        out_specs=pl.BlockSpec((1024, 128), lambda kk: (0, 0)),
        out_shape=jax.ShapeDtypeStruct((1024, 128), F32),
        scratch_shapes=[
            pltpu.VMEM((16, 4, 8, 512), F32),
            pltpu.VMEM((2, 544, 512), BF16),
            pltpu.SMEM((16,), jnp.int32),
        ],
        compiler_params=pltpu.CompilerParams(vmem_limit_bytes=VMEM_LIMIT),
        name="solve_planes",
    )(place, waves, tables, window)


def boxes_kernel(info_ref, in_ref, table_ref, out_ref, grid_ref):
    for half in range(2):
        even = split(in_ref[pl.ds(half, 256, stride=4), :])
        odd = split(in_ref[pl.ds(2 + half, 256, stride=4), :])
        even = product(even, (table_ref[0], table_ref[1]), TN)
        odd = product(odd, (table_ref[2], table_ref[3]), TN)
        for cell in range(4):
            first = 32 * cell
            for tile in range(4):
                columns = slice(tile % 2 * 128, tile % 2 * 128 + 128)
                near, far = even[first : first + 32, columns], odd[first : first + 32, columns]
                place = slice(64 * cell + 32 * half, 64 * cell + 32 * half + 32)
                grid_ref[tile, place, :] = near + far if tile < 2 else near - far
    base = first_cell(info_ref)

    def source(s, carry):
        lane = lanes_of((32, 128))
        group = lane >> 5
        total = jnp.zeros((32, 128), F32)
        for f in range(2):
            number = 2 * s + f
            start = (info_ref[number, 0] & 1) * 16
            cell_z = info_ref[number, 2]
            tile = cell_z >> 3
            after = (tile + 1) & 3
            offset = (cell_z & 7) * 16
            for r in range(2):
                cell = (info_ref[number, 1] + r - base) & 3
                place = pl.ds(pl.multiple_of(cell * 64 + start, 16), 32)
                value = jnp.where(
                    lane >= offset, grid_ref[tile, place, :], grid_ref[after, place, :]
                )
                value = pltpu.roll(value, (64 * f + 32 * r + 128 - offset) & 127, 1)
                total = jnp.where(group == 2 * f + r, value, total)
        out_ref[s] = total
        return carry

    lax.fori_loop(0, 16, source, 0, unroll=2)


def boxes(info, waves, table):
    return pl.pallas_call(
        boxes_kernel,
        grid=(1,),
        in_specs=[
            pl.BlockSpec(memory_space=pltpu.SMEM),
            pl.BlockSpec(memory_space=pltpu.VMEM),
            pl.BlockSpec((4, 256, 256), lambda i: (0, 0, 0)),
        ],
        out_specs=pl.BlockSpec(memory_space=pltpu.VMEM),
        out_shape=jax.ShapeDtypeStruct((16, 32, 128), F32),
        scratch_shapes=[pltpu.VMEM((4, 256, 128), F32)],
        compiler_params=pltpu.CompilerParams(vmem_limit_bytes=VMEM_LIMIT),
        name="boxes",
    )(info, waves, table)


def layout_kernel(info_ref, in_ref, out_ref):
    row = lax.broadcasted_iota(jnp.int32, (32, 128), 0)
    lane = lanes_of((32, 128))
    for quad in range(4):
        parts = exchange([in_ref[4 * quad + i] for i in range(4)])
        for f in range(2):
            for r in range(2):
                inside = (
                    (row < info_ref[f, 3] * 16)
                    & (16 * r + 4 * quad + (lane >> 5) < info_ref[f, 4] * 16)
                    & ((lane & 31) < info_ref[f, 5] * 16)
                )
                out_ref[pl.ds((4 * r + quad) * 2 + f, 32, stride=16), :] = jnp.where(
                    inside, parts[2 * f + r], 0.0
                )


def lay_out(info, pieces):
    return pl.pallas_call(
        layout_kernel,
        in_specs=[
            pl.BlockSpec(memory_space=pltpu.SMEM),
            pl.BlockSpec(memory_space=pltpu.VMEM),
        ],
        out_specs=pl.BlockSpec(memory_space=pltpu.VMEM),
        out_shape=jax.ShapeDtypeStruct((512, 128), F32),
        compiler_params=pltpu.CompilerParams(vmem_limit_bytes=VMEM_LIMIT),
        name="lay_out",
    )(info, pieces)


def along_frag(block, distance):
    devices = range(lax.axis_size("frag"))
    route = [(i, (i + distance) % len(devices)) for i in devices]
    return lax.ppermute(block, "frag", route)


def traded(block, axis):
    return lax.all_to_all(block, axis, split_axis=0, concat_axis=0, tiled=True)


def body(background, orbitals, frag_info):
    tables, window = jnp.asarray(wave_tables()), jnp.asarray(window_table())
    place = (lax.axis_index("frag") * 16 + lax.axis_index("grp")).astype(jnp.int32).reshape(1)
    frag_info, place = lax.optimization_barrier((frag_info, place))
    coeffs = orbitals.reshape(16, 256, 32)
    own = traded(densities(frag_info, coeffs), "grp")
    past = along_frag(own[:, 16:40, :], 1)
    info = jnp.concatenate([own[:, 32, :16], past[:, 16, :16]]).astype(jnp.int32).reshape(64, 8)
    region, cell = deposits(info, own, past)
    held = traded(region.reshape(16, 256, 128), "grp").reshape(128, 32, 128)
    total_density, spectrum = forward_z(background, held, tables, cell)
    spectrum = traded(spectrum.reshape(256, 1, 2176), BOTH).reshape(4352, 128)
    spectrum = solve_planes(place, spectrum, tables, window)
    spectrum = traded(spectrum.reshape(256, 4, 128), BOTH).reshape(1024, 128)
    pieces = boxes(info, spectrum, tables)
    pieces = lay_out(frag_info, traded(pieces, "grp"))
    frag_potential = pieces.reshape(256, 2, 128).transpose(1, 0, 2).reshape(2, 32768)
    return total_density, frag_potential


def solution(mesh):
    return jax.shard_map(
        body,
        mesh=mesh,
        in_specs=(
            P("frag", "grp", None),
            P(None, None, None, ("frag", "grp")),
            P(("frag", "grp"), None),
        ),
        out_specs=(P("frag", "grp", None), P(("frag", "grp"), None)),
        check_vma=False,
    )
```

```python
import math

import jax
import jax.numpy as jnp
import ml_dtypes
import numpy as np
from jax import lax
from jax.experimental import pallas as pl
from jax.experimental.pallas import tpu as pltpu
from jax.sharding import PartitionSpec as P

NG = 512
SPACING = 0.2
F32 = jnp.float32
BF16 = jnp.bfloat16
BOTH = ("frag", "grp")
PITCH = 40
VMEM_LIMIT = 24 * 1024 * 1024


def halves(table):
    high = table.astype(ml_dtypes.bfloat16)
    low = (table - high.astype(np.float64)).astype(ml_dtypes.bfloat16)
    return np.stack([high, low])


def synthesis_table(span):
    frequency = np.arange(16)[:, None] - 8
    point = np.arange(32)[None, :]
    angle = 2.0 * math.pi * np.mod(frequency * point, span * 16) / (span * 16)
    live = (frequency >= -4 * span) & (frequency < 4 * span) & (point < 16 * span)
    return np.where(live, (np.cos(angle) + np.sin(angle)) * math.sqrt(2.0 / 16) / span, 0.0)


def plane_tables():
    tables = []
    for span_y in (1, 2):
        for span_z in (1, 2):
            table_y = synthesis_table(span_y).reshape(16, 2, 16)
            table_z = synthesis_table(span_z)
            full = np.einsum("brg,cz->bcgrz", table_y, table_z)
            tables.append(halves(full.reshape(256, 1024)))
    return np.stack(tables)


def depth_tables():
    tables = []
    for span in (1, 2):
        full = np.einsum("ax,mn->mxan", synthesis_table(span), np.eye(16))
        tables.append(halves(full.reshape(512, 256)))
    return np.stack(tables)


def cas(rows, columns):
    angle = 2.0 * math.pi / NG * np.mod(rows[:, None] * columns[None, :], NG)
    return np.cos(angle) + np.sin(angle)


def row_order():
    block, low, high = np.meshgrid(np.arange(16), np.arange(4), np.arange(8), indexing="ij")
    return (block * 32 + high * 4 + low).reshape(-1)


def wave_tables():
    start = np.arange(256)
    even, odd = 2 * start, 2 * start + 1
    rows = row_order()[:256]
    tables = [
        cas(even, start),
        cas(odd, start),
        cas(start, odd),
        cas(even, rows),
        cas(odd, rows),
    ]
    return np.concatenate([halves(table) for table in tables])


def window_table():
    waves = np.concatenate([np.arange(0, NG, 2), np.arange(1, NG, 2)])
    return halves(cas(np.arange(NG + 64) % NG, waves))


def split(value):
    high = value.astype(BF16)
    return high, (value - high.astype(F32)).astype(BF16)


def product(left, right, dims):
    dims = (dims, ((), ()))
    total = lax.dot_general(left[0], right[1], dims, preferred_element_type=F32)
    total += lax.dot_general(left[1], right[0], dims, preferred_element_type=F32)
    return total + lax.dot_general(left[0], right[0], dims, preferred_element_type=F32)


NN = ((1,), (0,))
NT = ((1,), (1,))
TN = ((0,), (0,))


def lanes_of(shape):
    return lax.broadcasted_iota(jnp.int32, shape, len(shape) - 1)


def exchange(parts):
    lane = lanes_of(parts[0].shape)
    low = lane < 64
    even = (lane & 32) == 0

    def swapped(first, second):
        crossed = pltpu.roll(jnp.where(low, second, first), 64, 1)
        return jnp.where(low, first, crossed), jnp.where(low, crossed, second)

    a0, a2 = swapped(parts[0], parts[2])
    a1, a3 = swapped(parts[1], parts[3])
    return (
        jnp.where(even, a0, pltpu.roll(a1, 32, 1)),
        jnp.where(even, pltpu.roll(a0, 96, 1), a1),
        jnp.where(even, a2, pltpu.roll(a3, 32, 1)),
        jnp.where(even, pltpu.roll(a2, 96, 1), a3),
    )


def density_kernel(
    info_ref, orbitals_ref, planes_ref, depths_ref, out_ref, coeff_ref, plane_ref, depth_ref, sems
):
    copies = []
    for f in range(2):
        pair = 2 * info_ref[f, 4] + info_ref[f, 5] - 3
        copies.append(pltpu.make_async_copy(planes_ref.at[pair], plane_ref.at[f], sems.at[2 * f]))
        copies.append(
            pltpu.make_async_copy(
                depths_ref.at[info_ref[f, 3] - 1], depth_ref.at[f], sems.at[2 * f + 1]
            )
        )
    for copy in copies:
        copy.start()
    for a in range(16):
        coeff_ref[a] = jnp.transpose(orbitals_ref[a].astype(F32)).astype(BF16)
    for f in range(2):
        count = info_ref[f, 7]
        scale = 2.0 * info_ref[f, 6].astype(F32)
        coeffs = coeff_ref[:, 16 * f : 16 * f + 16, :].reshape(256, 256)
        copies[2 * f].wait()
        copies[2 * f + 1].wait()
        for part in range(4):
            columns = slice(part * 256, (part + 1) * 256)
            flat = jnp.dot(coeffs, plane_ref[f, 1, :, columns], preferred_element_type=F32)
            flat += jnp.dot(coeffs, plane_ref[f, 0, :, columns], preferred_element_type=F32)
            psi = product((depth_ref[f, 0], depth_ref[f, 1]), split(flat), NN)
            total = jnp.zeros((32, 256), F32)
            for m in range(16):
                orbital = psi[m * 32 : (m + 1) * 32]
                total += orbital * orbital * (m < count).astype(F32)
            total = total * scale
            for tile in range(2):
                here = total[:, tile * 128 : (tile + 1) * 128]
                turned = pltpu.roll(here, 64, 1)
                owner = 2 * (2 * part + tile)
                low = lanes_of(here.shape) < 64
                if f == 0:
                    out_ref[33 * owner : 33 * owner + 32, :] = here
                    out_ref[33 * owner + 33 : 33 * owner + 65, :] = turned
                else:
                    for first, value in ((33 * owner, turned), (33 * owner + 33, here)):
                        place = slice(first, first + 32)
                        out_ref[place, :] = jnp.where(low, out_ref[place, :], value)
    lane = lanes_of((1, 128))
    note = jnp.zeros((1, 128), F32)
    for place in range(16):
        note = jnp.where(lane == place, info_ref[place // 8, place % 8].astype(F32), note)
    for owner in range(16):
        out_ref[33 * owner + 32 : 33 * owner + 33, :] = note


def densities(info, orbitals):
    planes = jnp.asarray(plane_tables())
    depths = jnp.asarray(depth_tables())
    return pl.pallas_call(
        density_kernel,
        in_specs=[
            pl.BlockSpec(memory_space=pltpu.SMEM),
            pl.BlockSpec(memory_space=pltpu.VMEM),
            pl.BlockSpec(memory_space=pl.ANY),
            pl.BlockSpec(memory_space=pl.ANY),
        ],
        out_specs=pl.BlockSpec(memory_space=pltpu.VMEM),
        out_shape=jax.ShapeDtypeStruct((528, 128), F32),
        scratch_shapes=[
            pltpu.VMEM((16, 32, 256), BF16),
            pltpu.VMEM((2, 2, 256, 1024), BF16),
            pltpu.VMEM((2, 2, 512, 256), BF16),
            pltpu.SemaphoreType.DMA((4,)),
        ],
        compiler_params=pltpu.CompilerParams(vmem_limit_bytes=56 * 1024 * 1024),
        name="densities",
    )(info, orbitals, planes, depths)


def first_cell(info_ref):
    def touched(number):
        cell = info_ref[number, 1]
        return cell >> 1, ((cell + info_ref[number, 4] - 1) & 31) >> 1

    first, last = touched(0)
    shared = jnp.int32(1)
    for number in range(1, 32):
        one, other = touched(number)
        shared = shared * ((one == first) | (other == first)).astype(jnp.int32)
    return (2 * jnp.where(shared == 1, first, last) + 31) & 31


def deposit_kernel(info_ref, own_ref, past_ref, out_ref, cell_ref):
    cell_ref[...] = jnp.full((8, 128), first_cell(info_ref).astype(F32))
    out_ref[...] = jnp.zeros(out_ref.shape, F32)

    def source(s, carry):
        own = own_ref[pl.ds(s * 33, 32), :]
        past = past_ref[pl.ds(s * 17, 16), :]
        lane = lanes_of((16, 128))
        adds = []
        for f in range(2):
            for first, piece in ((0, own), (32, past)):
                number = first + 2 * s + f
                odd = info_ref[number, 0] & 1
                cell_y = info_ref[number, 1]
                cell_z = info_ref[number, 2]
                tile = cell_z >> 3
                after = (tile + 1) & 3
                offset = (cell_z & 7) * 16
                kept = odd == 1 if first else odd == 0
                low = jnp.where(kept, offset, 256)
                part_inside = (lane >= low) & (lane < low + 32)
                part_beyond = lane < jnp.where(kept, offset - 96, 0)
                inside = (lane >= offset) & (lane < offset + 32)
                beyond = lane < offset - 96
                for r in range(2):
                    row = (cell_y + r) & 31
                    turned = pltpu.roll(piece, (offset + 128 - (64 * f + 32 * r)) & 127, 1)
                    if first:
                        adds.append((row, tile, 0, jnp.where(part_inside, turned, 0.0)))
                        adds.append((row, after, 0, jnp.where(part_beyond, turned, 0.0)))
                    else:
                        start = pl.multiple_of(odd * 16, 16)
                        top, rest = turned[0:16], turned[16:32]
                        adds.append((row, tile, start, jnp.where(inside, top, 0.0)))
                        adds.append((row, after, start, jnp.where(beyond, top, 0.0)))
                        adds.append((row, tile, 16, jnp.where(part_inside, rest, 0.0)))
                        adds.append((row, after, 16, jnp.where(part_beyond, rest, 0.0)))
        for row, tile, start, value in adds:
            out_ref[row, tile, pl.ds(start, 16), :] += value
        return carry

    lax.fori_loop(0, 16, source, 0, unroll=2)


def deposits(info, own, past):
    return pl.pallas_call(
        deposit_kernel,
        in_specs=[
            pl.BlockSpec(memory_space=pltpu.SMEM),
            pl.BlockSpec(memory_space=pltpu.VMEM),
            pl.BlockSpec(memory_space=pltpu.VMEM),
        ],
        out_specs=[pl.BlockSpec(memory_space=pltpu.VMEM)] * 2,
        out_shape=[
            jax.ShapeDtypeStruct((32, 4, 32, 128), F32),
            jax.ShapeDtypeStruct((8, 128), F32),
        ],
        compiler_params=pltpu.CompilerParams(vmem_limit_bytes=VMEM_LIMIT),
        name="deposits",
    )(info, own, past)


def forward_kernel(back_ref, held_ref, table_ref, cell_ref, total_ref, out_ref, turned_ref):
    b = pl.program_id(0)

    @pl.when(b == 0)
    def _():
        out_ref[pl.ds(16, 256, stride=17), :] = jnp.broadcast_to(cell_ref[0:1, :], (256, 128))

    for g in range(16):
        for jj in range(2):
            for tile in range(4):
                turned_ref[tile, pl.ds(jj * 16 + g, 8, stride=PITCH), :] = held_ref[
                    (g * 2 + jj) * 4 + tile
                ]
    for tile in range(4):
        columns = slice(tile * 128, (tile + 1) * 128)
        for x in range(8):
            total_ref[x, :, columns] = (
                back_ref[x, :, columns] + turned_ref[tile, x * PITCH : x * PITCH + 32, :]
            )
    total = total_ref[...].reshape(256, 512)
    near, far = total[:, :256], total[:, 256:]
    for parity, value in ((0, near + far), (1, near - far)):
        table = (table_ref[2 * parity], table_ref[2 * parity + 1])
        waves = product(table, split(value), NT)
        for tile in range(2):
            place = pl.ds(8 * parity + 2 * b + tile, 256, stride=17)
            out_ref[place, :] = waves[:, tile * 128 : (tile + 1) * 128]


def forward_z(background, held, table, cell):
    return pl.pallas_call(
        forward_kernel,
        grid=(4,),
        in_specs=[
            pl.BlockSpec((8, 32, 512), lambda b: (b, 0, 0)),
            pl.BlockSpec((128, 8, 128), lambda b: (0, b, 0)),
            pl.BlockSpec((4, 256, 256), lambda b: (0, 0, 0)),
            pl.BlockSpec((8, 128), lambda b: (0, 0)),
        ],
        out_specs=[
            pl.BlockSpec((8, 32, 512), lambda b: (b, 0, 0)),
            pl.BlockSpec((4352, 128), lambda b: (0, 0)),
        ],
        out_shape=[
            jax.ShapeDtypeStruct((32, 32, 512), F32),
            jax.ShapeDtypeStruct((4352, 128), F32),
        ],
        scratch_shapes=[pltpu.VMEM((4, 8 * PITCH, 128), F32)],
        compiler_params=pltpu.CompilerParams(vmem_limit_bytes=VMEM_LIMIT),
        name="forward_z",
    )(background, held, table, cell)


def planes_kernel(
    place_ref, in_ref, tables_ref, window_ref, out_ref, grid_ref, wave_ref, cells_ref
):
    kk = pl.program_id(0)

    @pl.when(kk == 0)
    def _():
        for group in range(16):
            row = group * 272 + 16
            cells_ref[group] = jnp.max(in_ref[row : row + 1, :]).astype(jnp.int32)

    def table(i):
        return tables_ref[2 * i], tables_ref[2 * i + 1]

    for quad in range(4):
        parts = [
            jnp.concatenate(
                [
                    in_ref[pl.ds((group * 16 + 4 * quad + i) * 17 + 8 * kk, 8), :]
                    for group in range(16)
                ]
            )
            for i in range(4)
        ]
        for i, part in enumerate(exchange(parts)):
            grid_ref[:, i, :, quad * 128 : (quad + 1) * 128] = part.reshape(16, 8, 128)
    grid = grid_ref[...].reshape(512, 512)
    near, far = grid[:, :256], grid[:, 256:]
    value = jnp.concatenate(
        [product(split(near + far), table(0), NN), product(split(near - far), table(2), NN)], 1
    )
    near, far = value[:256], value[256:]
    value = jnp.concatenate(
        [product(table(3), split(near + far), NN), product(table(4), split(near - far), NN)], 0
    )

    def folded(wave):
        lowest = jnp.minimum(wave, NG - wave)
        return lowest * lowest

    def ordered(place):
        return jnp.where(place < 256, 2 * place, 2 * place - 511)

    square = (
        folded(ordered(lax.broadcasted_iota(jnp.int32, (NG, 1), 0)))
        + folded(ordered(lax.broadcasted_iota(jnp.int32, (1, NG), 1)))
        + folded(2 * place_ref[0] + kk)
    )
    factor = (NG * SPACING) ** 2 / math.pi / float(NG) ** 3
    value = value * jnp.where(square > 0, factor / jnp.maximum(square, 1).astype(F32), 0.0)
    even = product(table(0), split(value[:256]), NN)
    odd = product(table(2), split(value[256:]), NN)
    for i, value in enumerate(split(jnp.concatenate([even + odd, even - odd, even[:32] + odd[:32]]))):
        wave_ref[i] = value
    lane = lanes_of((16, 128))
    for group in range(16):
        place = pl.ds(pl.multiple_of(cells_ref[group] * 16, 16), 64)
        window = (window_ref[0, place, :], window_ref[1, place, :])
        rows = slice(group * 32, group * 32 + 64)
        value = product(window, (wave_ref[0, rows, :], wave_ref[1, rows, :]), NT)
        joined = jnp.zeros((16, 128), F32)
        spare = jnp.zeros((16, 128), F32)
        for cell in range(4):
            piece = jnp.concatenate([value[16 * cell : 16 * cell + 16]] * 2, 1)
            here = pltpu.roll(piece, 32 * cell, 1) if cell else piece
            joined = jnp.where((lane >> 5) == cell, here, joined)
            here = pltpu.roll(piece, (16 * cell + 96) % 128, 1)
            spare = jnp.where(((lane >> 4) & 3) == cell, here, spare)
        out_ref[pl.ds(group * 48 + kk, 16, stride=3), :] = joined
        place = pl.ds(group * 48 + 2, 16, stride=3)

        @pl.when(kk == 0)
        def _():
            out_ref[place, :] = spare

        @pl.when(kk == 1)
        def _():
            out_ref[place, :] = jnp.where(lane < 64, out_ref[place, :], pltpu.roll(spare, 64, 1))


def solve_planes(place, waves, tables, window):
    return pl.pallas_call(
        planes_kernel,
        grid=(2,),
        in_specs=[
            pl.BlockSpec(memory_space=pltpu.SMEM),
            pl.BlockSpec(memory_space=pltpu.VMEM),
            pl.BlockSpec(memory_space=pltpu.VMEM),
            pl.BlockSpec(memory_space=pltpu.VMEM),
        ],
        out_specs=pl.BlockSpec((768, 128), lambda kk: (0, 0)),
        out_shape=jax.ShapeDtypeStruct((768, 128), F32),
        scratch_shapes=[
            pltpu.VMEM((16, 4, 8, 512), F32),
            pltpu.VMEM((2, 544, 512), BF16),
            pltpu.SMEM((16,), jnp.int32),
        ],
        compiler_params=pltpu.CompilerParams(vmem_limit_bytes=VMEM_LIMIT),
        name="solve_planes",
    )(place, waves, tables, window)


def boxes_kernel(info_ref, in_ref, table_ref, out_ref, grid_ref):
    even = product(split(in_ref[pl.ds(0, 256, stride=3), :]), (table_ref[0], table_ref[1]), TN)
    odd = product(split(in_ref[pl.ds(1, 256, stride=3), :]), (table_ref[2], table_ref[3]), TN)
    spare = split(in_ref[pl.ds(2, 256, stride=3), :])
    spare_even = product(spare, (table_ref[0], table_ref[1]), TN)
    spare_odd = product(spare, (table_ref[2], table_ref[3]), TN)
    for cell in range(4):
        for tile in range(4):
            columns = slice(tile % 2 * 128, tile % 2 * 128 + 128)
            rows = slice(32 * cell, 32 * cell + 32)
            near, far = even[rows, columns], odd[rows, columns]
            grid_ref[tile, 48 * cell : 48 * cell + 32, :] = near + far if tile < 2 else near - far
            near = spare_even[16 * cell : 16 * cell + 16, columns]
            far = spare_odd[64 + 16 * cell : 80 + 16 * cell, columns]
            place = slice(48 * cell + 32, 48 * cell + 48)
            grid_ref[tile, place, :] = near + far if tile < 2 else near - far
    base = first_cell(info_ref)

    def source(s, carry):
        lane = lanes_of((32, 128))
        group = lane >> 5
        total = jnp.zeros((32, 128), F32)
        for f in range(2):
            number = 2 * s + f
            start = (info_ref[number, 0] & 1) * 16
            cell_z = info_ref[number, 2]
            tile = cell_z >> 3
            after = (tile + 1) & 3
            offset = (cell_z & 7) * 16
            for r in range(2):
                cell = (info_ref[number, 1] + r - base) & 3
                place = pl.ds(pl.multiple_of(cell * 48 + start, 16), 32)
                value = jnp.where(
                    lane >= offset, grid_ref[tile, place, :], grid_ref[after, place, :]
                )
                value = pltpu.roll(value, (64 * f + 32 * r + 128 - offset) & 127, 1)
                total = jnp.where(group == 2 * f + r, value, total)
        out_ref[s] = total
        return carry

    lax.fori_loop(0, 16, source, 0, unroll=2)


def boxes(info, waves, table):
    return pl.pallas_call(
        boxes_kernel,
        grid=(1,),
        in_specs=[
            pl.BlockSpec(memory_space=pltpu.SMEM),
            pl.BlockSpec(memory_space=pltpu.VMEM),
            pl.BlockSpec((4, 256, 256), lambda i: (0, 0, 0)),
        ],
        out_specs=pl.BlockSpec(memory_space=pltpu.VMEM),
        out_shape=jax.ShapeDtypeStruct((16, 32, 128), F32),
        scratch_shapes=[pltpu.VMEM((4, 192, 128), F32)],
        compiler_params=pltpu.CompilerParams(vmem_limit_bytes=VMEM_LIMIT),
        name="boxes",
    )(info, waves, table)


def layout_kernel(info_ref, in_ref, out_ref):
    row = lax.broadcasted_iota(jnp.int32, (32, 128), 0)
    lane = lanes_of((32, 128))
    for quad in range(4):
        parts = exchange([in_ref[4 * quad + i] for i in range(4)])
        for f in range(2):
            for r in range(2):
                inside = (
                    (row < info_ref[f, 3] * 16)
                    & (16 * r + 4 * quad + (lane >> 5) < info_ref[f, 4] * 16)
                    & ((lane & 31) < info_ref[f, 5] * 16)
                )
                out_ref[pl.ds((4 * r + quad) * 2 + f, 32, stride=16), :] = jnp.where(
                    inside, parts[2 * f + r], 0.0
                )


def lay_out(info, pieces):
    return pl.pallas_call(
        layout_kernel,
        in_specs=[
            pl.BlockSpec(memory_space=pltpu.SMEM),
            pl.BlockSpec(memory_space=pltpu.VMEM),
        ],
        out_specs=pl.BlockSpec(memory_space=pltpu.VMEM),
        out_shape=jax.ShapeDtypeStruct((512, 128), F32),
        compiler_params=pltpu.CompilerParams(vmem_limit_bytes=VMEM_LIMIT),
        name="lay_out",
    )(info, pieces)


def along_frag(block, distance):
    devices = range(lax.axis_size("frag"))
    route = [(i, (i + distance) % len(devices)) for i in devices]
    return lax.ppermute(block, "frag", route)


def traded(block, axis):
    return lax.all_to_all(block, axis, split_axis=0, concat_axis=0, tiled=True)


def body(background, orbitals, frag_info):
    tables, window = jnp.asarray(wave_tables()), jnp.asarray(window_table())
    place = (lax.axis_index("frag") * 16 + lax.axis_index("grp")).astype(jnp.int32).reshape(1)
    frag_info, place = lax.optimization_barrier((frag_info, place))
    coeffs = orbitals.reshape(16, 256, 32)
    own = traded(densities(frag_info, coeffs).reshape(16, 1, 4224), "grp")
    past = along_frag(own[:, :, 2048:], 1)
    info = jnp.concatenate([own[:, 0, 4096:4112], past[:, 0, 2048:2064]])
    info = info.astype(jnp.int32).reshape(64, 8)
    own, past = own.reshape(528, 128), past.reshape(272, 128)
    region, cell = deposits(info, own, past)
    held = traded(region.reshape(16, 256, 128), "grp").reshape(128, 32, 128)
    total_density, spectrum = forward_z(background, held, tables, cell)
    spectrum = traded(spectrum.reshape(256, 1, 2176), BOTH).reshape(4352, 128)
    spectrum = solve_planes(place, spectrum, tables, window)
    spectrum = traded(spectrum.reshape(256, 1, 384), BOTH).reshape(768, 128)
    pieces = boxes(info, spectrum, tables)
    pieces = lay_out(frag_info, traded(pieces, "grp"))
    frag_potential = pieces.reshape(256, 2, 128).transpose(1, 0, 2).reshape(2, 32768)
    return total_density, frag_potential


def solution(mesh):
    return jax.shard_map(
        body,
        mesh=mesh,
        in_specs=(
            P("frag", "grp", None),
            P(None, None, None, ("frag", "grp")),
            P(("frag", "grp"), None),
        ),
        out_specs=(P("frag", "grp", None), P(("frag", "grp"), None)),
        check_vma=False,
    )
```

```python
import math

import jax
import jax.numpy as jnp
import ml_dtypes
import numpy as np
from jax import lax
from jax.experimental import pallas as pl
from jax.experimental.pallas import tpu as pltpu
from jax.sharding import PartitionSpec as P

NG = 512
SPACING = 0.2
F32 = jnp.float32
BF16 = jnp.bfloat16
BOTH = ("frag", "grp")
PITCH = 40
VMEM_LIMIT = 24 * 1024 * 1024


def halves(table):
    high = table.astype(ml_dtypes.bfloat16)
    low = (table - high.astype(np.float64)).astype(ml_dtypes.bfloat16)
    return np.stack([high, low])


def synthesis_table(span):
    frequency = np.arange(16)[:, None] - 8
    point = np.arange(32)[None, :]
    angle = 2.0 * math.pi * np.mod(frequency * point, span * 16) / (span * 16)
    live = (frequency >= -4 * span) & (frequency < 4 * span) & (point < 16 * span)
    return np.where(live, (np.cos(angle) + np.sin(angle)) * math.sqrt(2.0 / 16) / span, 0.0)


def plane_tables():
    tables = []
    for span_y in (1, 2):
        for span_z in (1, 2):
            table_y = synthesis_table(span_y).reshape(16, 2, 16)
            table_z = synthesis_table(span_z)
            full = np.einsum("brg,cz->bcgrz", table_y, table_z)
            tables.append(halves(full.reshape(256, 1024)))
    return np.stack(tables)


def depth_tables():
    tables = []
    for span in (1, 2):
        full = np.einsum("ax,mn->mxan", synthesis_table(span), np.eye(16))
        tables.append(halves(full.reshape(512, 256)))
    return np.stack(tables)


def cas(rows, columns):
    angle = 2.0 * math.pi / NG * np.mod(rows[:, None] * columns[None, :], NG)
    return np.cos(angle) + np.sin(angle)


def row_order():
    block, low, high = np.meshgrid(np.arange(16), np.arange(4), np.arange(8), indexing="ij")
    return (block * 32 + high * 4 + low).reshape(-1)


def wave_tables():
    start = np.arange(256)
    even, odd = 2 * start, 2 * start + 1
    rows = row_order()[:256]
    tables = [
        cas(even, start),
        cas(odd, start),
        cas(start, odd),
        cas(even, rows),
        cas(odd, rows),
    ]
    return np.concatenate([halves(table) for table in tables])


def window_table():
    waves = np.concatenate([np.arange(0, NG, 2), np.arange(1, NG, 2)])
    return halves(cas(np.arange(NG + 64) % NG, waves))


def split(value):
    high = value.astype(BF16)
    return high, (value - high.astype(F32)).astype(BF16)


def product(left, right, dims):
    dims = (dims, ((), ()))
    total = lax.dot_general(left[0], right[1], dims, preferred_element_type=F32)
    total += lax.dot_general(left[1], right[0], dims, preferred_element_type=F32)
    return total + lax.dot_general(left[0], right[0], dims, preferred_element_type=F32)


NN = ((1,), (0,))
NT = ((1,), (1,))
TN = ((0,), (0,))


def lanes_of(shape):
    return lax.broadcasted_iota(jnp.int32, shape, len(shape) - 1)


def exchange(parts):
    lane = lanes_of(parts[0].shape)
    low = lane < 64
    even = (lane & 32) == 0

    def swapped(first, second):
        crossed = pltpu.roll(jnp.where(low, second, first), 64, 1)
        return jnp.where(low, first, crossed), jnp.where(low, crossed, second)

    a0, a2 = swapped(parts[0], parts[2])
    a1, a3 = swapped(parts[1], parts[3])
    return (
        jnp.where(even, a0, pltpu.roll(a1, 32, 1)),
        jnp.where(even, pltpu.roll(a0, 96, 1), a1),
        jnp.where(even, a2, pltpu.roll(a3, 32, 1)),
        jnp.where(even, pltpu.roll(a2, 96, 1), a3),
    )


def density_kernel(
    info_ref,
    source_ref,
    planes_ref,
    depths_ref,
    out_ref,
    orbitals_ref,
    coeff_ref,
    plane_ref,
    depth_ref,
    sems,
):
    orbitals_copy = pltpu.make_async_copy(source_ref, orbitals_ref, sems.at[4])
    orbitals_copy.start()
    copies = []
    for f in range(2):
        pair = 2 * info_ref[f, 4] + info_ref[f, 5] - 3
        copies.append(pltpu.make_async_copy(planes_ref.at[pair], plane_ref.at[f], sems.at[2 * f]))
        copies.append(
            pltpu.make_async_copy(
                depths_ref.at[info_ref[f, 3] - 1], depth_ref.at[f], sems.at[2 * f + 1]
            )
        )
    copies[0].start()
    copies[1].start()
    orbitals_copy.wait()
    for a in range(16):
        coeff_ref[a] = jnp.transpose(orbitals_ref[a].astype(F32)).astype(BF16)
    for f in range(2):
        count = info_ref[f, 7]
        scale = 2.0 * info_ref[f, 6].astype(F32)
        coeffs = coeff_ref[:, 16 * f : 16 * f + 16, :].reshape(256, 256)
        copies[2 * f].wait()
        copies[2 * f + 1].wait()
        if f == 0:
            copies[2].start()
            copies[3].start()
        for part in range(4):
            columns = slice(part * 256, (part + 1) * 256)
            flat = jnp.dot(coeffs, plane_ref[f, 1, :, columns], preferred_element_type=F32)
            flat += jnp.dot(coeffs, plane_ref[f, 0, :, columns], preferred_element_type=F32)
            psi = product((depth_ref[f, 0], depth_ref[f, 1]), split(flat), NN)
            total = jnp.zeros((32, 256), F32)
            for m in range(16):
                orbital = psi[m * 32 : (m + 1) * 32]
                total += orbital * orbital * (m < count).astype(F32)
            total = total * scale
            for tile in range(2):
                here = total[:, tile * 128 : (tile + 1) * 128]
                turned = pltpu.roll(here, 64, 1)
                owner = 2 * (2 * part + tile)
                low = lanes_of(here.shape) < 64
                if f == 0:
                    out_ref[33 * owner : 33 * owner + 32, :] = here
                    out_ref[33 * owner + 33 : 33 * owner + 65, :] = turned
                else:
                    for first, value in ((33 * owner, turned), (33 * owner + 33, here)):
                        place = slice(first, first + 32)
                        out_ref[place, :] = jnp.where(low, out_ref[place, :], value)
    lane = lanes_of((1, 128))
    note = jnp.zeros((1, 128), F32)
    for place in range(16):
        note = jnp.where(lane == place, info_ref[place // 8, place % 8].astype(F32), note)
    for owner in range(16):
        out_ref[33 * owner + 32 : 33 * owner + 33, :] = note


def densities(info, orbitals):
    planes = jnp.asarray(plane_tables())
    depths = jnp.asarray(depth_tables())
    return pl.pallas_call(
        density_kernel,
        in_specs=[
            pl.BlockSpec(memory_space=pltpu.SMEM),
            pl.BlockSpec(memory_space=pl.ANY),
            pl.BlockSpec(memory_space=pl.ANY),
            pl.BlockSpec(memory_space=pl.ANY),
        ],
        out_specs=pl.BlockSpec(memory_space=pltpu.VMEM),
        out_shape=jax.ShapeDtypeStruct((528, 128), F32),
        scratch_shapes=[
            pltpu.VMEM((16, 256, 32), BF16),
            pltpu.VMEM((16, 32, 256), BF16),
            pltpu.VMEM((2, 2, 256, 1024), BF16),
            pltpu.VMEM((2, 2, 512, 256), BF16),
            pltpu.SemaphoreType.DMA((5,)),
        ],
        compiler_params=pltpu.CompilerParams(vmem_limit_bytes=56 * 1024 * 1024),
        name="densities",
    )(info, orbitals, planes, depths)


def first_cell(info_ref):
    def touched(number):
        cell = info_ref[number, 1]
        return cell >> 1, ((cell + info_ref[number, 4] - 1) & 31) >> 1

    first, last = touched(0)
    shared = jnp.int32(1)
    for number in range(1, 32):
        one, other = touched(number)
        shared = shared * ((one == first) | (other == first)).astype(jnp.int32)
    return (2 * jnp.where(shared == 1, first, last) + 31) & 31


def deposit_kernel(info_ref, own_ref, past_ref, out_ref, cell_ref):
    cell_ref[...] = jnp.full((8, 128), first_cell(info_ref).astype(F32))
    out_ref[...] = jnp.zeros(out_ref.shape, F32)

    def source(s, carry):
        own = own_ref[pl.ds(s * 33, 32), :]
        past = past_ref[pl.ds(s * 17, 16), :]
        lane = lanes_of((16, 128))
        adds = []
        for f in range(2):
            for first, piece in ((0, own), (32, past)):
                number = first + 2 * s + f
                odd = info_ref[number, 0] & 1
                cell_y = info_ref[number, 1]
                cell_z = info_ref[number, 2]
                tile = cell_z >> 3
                after = (tile + 1) & 3
                offset = (cell_z & 7) * 16
                kept = odd == 1 if first else odd == 0
                low = jnp.where(kept, offset, 256)
                part_inside = (lane >= low) & (lane < low + 32)
                part_beyond = lane < jnp.where(kept, offset - 96, 0)
                inside = (lane >= offset) & (lane < offset + 32)
                beyond = lane < offset - 96
                for r in range(2):
                    row = (cell_y + r) & 31
                    turned = pltpu.roll(piece, (offset + 128 - (64 * f + 32 * r)) & 127, 1)
                    if first:
                        adds.append((row, tile, 0, jnp.where(part_inside, turned, 0.0)))
                        adds.append((row, after, 0, jnp.where(part_beyond, turned, 0.0)))
                    else:
                        start = pl.multiple_of(odd * 16, 16)
                        top, rest = turned[0:16], turned[16:32]
                        adds.append((row, tile, start, jnp.where(inside, top, 0.0)))
                        adds.append((row, after, start, jnp.where(beyond, top, 0.0)))
                        adds.append((row, tile, 16, jnp.where(part_inside, rest, 0.0)))
                        adds.append((row, after, 16, jnp.where(part_beyond, rest, 0.0)))
        for row, tile, start, value in adds:
            out_ref[row, tile, pl.ds(start, 16), :] += value
        return carry

    lax.fori_loop(0, 16, source, 0, unroll=4)


def deposits(info, own, past):
    return pl.pallas_call(
        deposit_kernel,
        in_specs=[
            pl.BlockSpec(memory_space=pltpu.SMEM),
            pl.BlockSpec(memory_space=pltpu.VMEM),
            pl.BlockSpec(memory_space=pltpu.VMEM),
        ],
        out_specs=[pl.BlockSpec(memory_space=pltpu.VMEM)] * 2,
        out_shape=[
            jax.ShapeDtypeStruct((32, 4, 32, 128), F32),
            jax.ShapeDtypeStruct((8, 128), F32),
        ],
        compiler_params=pltpu.CompilerParams(vmem_limit_bytes=VMEM_LIMIT),
        name="deposits",
    )(info, own, past)


def forward_kernel(back_ref, held_ref, table_ref, cell_ref, total_ref, out_ref, turned_ref):
    b = pl.program_id(0)

    @pl.when(b == 0)
    def _():
        out_ref[pl.ds(16, 256, stride=17), :] = jnp.broadcast_to(cell_ref[0:1, :], (256, 128))

    for g in range(16):
        for jj in range(2):
            for tile in range(4):
                turned_ref[tile, pl.ds(jj * 16 + g, 8, stride=PITCH), :] = held_ref[
                    (g * 2 + jj) * 4 + tile
                ]
    for tile in range(4):
        columns = slice(tile * 128, (tile + 1) * 128)
        for x in range(8):
            total_ref[x, :, columns] = (
                back_ref[x, :, columns] + turned_ref[tile, x * PITCH : x * PITCH + 32, :]
            )
    total = total_ref[...].reshape(256, 512)
    near, far = total[:, :256], total[:, 256:]
    for parity, value in ((0, near + far), (1, near - far)):
        table = (table_ref[2 * parity], table_ref[2 * parity + 1])
        waves = product(table, split(value), NT)
        for tile in range(2):
            place = pl.ds(8 * parity + 2 * b + tile, 256, stride=17)
            out_ref[place, :] = waves[:, tile * 128 : (tile + 1) * 128]


def forward_z(background, held, table, cell):
    return pl.pallas_call(
        forward_kernel,
        grid=(4,),
        in_specs=[
            pl.BlockSpec((8, 32, 512), lambda b: (b, 0, 0)),
            pl.BlockSpec((128, 8, 128), lambda b: (0, b, 0)),
            pl.BlockSpec((4, 256, 256), lambda b: (0, 0, 0)),
            pl.BlockSpec((8, 128), lambda b: (0, 0)),
        ],
        out_specs=[
            pl.BlockSpec((8, 32, 512), lambda b: (b, 0, 0)),
            pl.BlockSpec((4352, 128), lambda b: (0, 0)),
        ],
        out_shape=[
            jax.ShapeDtypeStruct((32, 32, 512), F32),
            jax.ShapeDtypeStruct((4352, 128), F32),
        ],
        scratch_shapes=[pltpu.VMEM((4, 8 * PITCH, 128), F32)],
        compiler_params=pltpu.CompilerParams(vmem_limit_bytes=VMEM_LIMIT),
        name="forward_z",
    )(background, held, table, cell)


def planes_kernel(
    place_ref, in_ref, tables_ref, window_ref, out_ref, grid_ref, wave_ref, cells_ref
):
    kk = pl.program_id(0)

    @pl.when(kk == 0)
    def _():
        for group in range(16):
            row = group * 272 + 16
            cells_ref[group] = jnp.max(in_ref[row : row + 1, :]).astype(jnp.int32)

    def table(i):
        return tables_ref[2 * i], tables_ref[2 * i + 1]

    for quad in range(4):
        parts = [
            jnp.concatenate(
                [
                    in_ref[pl.ds((group * 16 + 4 * quad + i) * 17 + 8 * kk, 8), :]
                    for group in range(16)
                ]
            )
            for i in range(4)
        ]
        for i, part in enumerate(exchange(parts)):
            grid_ref[:, i, :, quad * 128 : (quad + 1) * 128] = part.reshape(16, 8, 128)
    grid = grid_ref[...].reshape(512, 512)
    near, far = grid[:, :256], grid[:, 256:]
    value = jnp.concatenate(
        [product(split(near + far), table(0), NN), product(split(near - far), table(2), NN)], 1
    )
    near, far = value[:256], value[256:]
    value = jnp.concatenate(
        [product(table(3), split(near + far), NN), product(table(4), split(near - far), NN)], 0
    )

    def folded(wave):
        lowest = jnp.minimum(wave, NG - wave)
        return lowest * lowest

    def ordered(place):
        return jnp.where(place < 256, 2 * place, 2 * place - 511)

    square = (
        folded(ordered(lax.broadcasted_iota(jnp.int32, (NG, 1), 0)))
        + folded(ordered(lax.broadcasted_iota(jnp.int32, (1, NG), 1)))
        + folded(2 * place_ref[0] + kk)
    )
    factor = (NG * SPACING) ** 2 / math.pi / float(NG) ** 3
    value = value * jnp.where(square > 0, factor / jnp.maximum(square, 1).astype(F32), 0.0)
    even = product(table(0), split(value[:256]), NN)
    odd = product(table(2), split(value[256:]), NN)
    for i, value in enumerate(split(jnp.concatenate([even + odd, even - odd, even[:32] + odd[:32]]))):
        wave_ref[i] = value
    lane = lanes_of((16, 128))
    for group in range(16):
        place = pl.ds(pl.multiple_of(cells_ref[group] * 16, 16), 64)
        window = (window_ref[0, place, :], window_ref[1, place, :])
        rows = slice(group * 32, group * 32 + 64)
        value = product(window, (wave_ref[0, rows, :], wave_ref[1, rows, :]), NT)
        joined = jnp.zeros((16, 128), F32)
        spare = jnp.zeros((16, 128), F32)
        for cell in range(4):
            piece = jnp.concatenate([value[16 * cell : 16 * cell + 16]] * 2, 1)
            here = pltpu.roll(piece, 32 * cell, 1) if cell else piece
            joined = jnp.where((lane >> 5) == cell, here, joined)
            here = pltpu.roll(piece, (16 * cell + 96) % 128, 1)
            spare = jnp.where(((lane >> 4) & 3) == cell, here, spare)
        out_ref[pl.ds(group * 48 + kk, 16, stride=3), :] = joined
        place = pl.ds(group * 48 + 2, 16, stride=3)
        out_ref[place, :] = jnp.where((lane >> 6) == kk, spare, out_ref[place, :])


def solve_planes(place, waves, tables, window):
    return pl.pallas_call(
        planes_kernel,
        grid=(2,),
        in_specs=[
            pl.BlockSpec(memory_space=pltpu.SMEM),
            pl.BlockSpec(memory_space=pltpu.VMEM),
            pl.BlockSpec(memory_space=pltpu.VMEM),
            pl.BlockSpec(memory_space=pltpu.VMEM),
        ],
        out_specs=pl.BlockSpec((768, 128), lambda kk: (0, 0)),
        out_shape=jax.ShapeDtypeStruct((768, 128), F32),
        scratch_shapes=[
            pltpu.VMEM((16, 4, 8, 512), F32),
            pltpu.VMEM((2, 544, 512), BF16),
            pltpu.SMEM((16,), jnp.int32),
        ],
        compiler_params=pltpu.CompilerParams(vmem_limit_bytes=VMEM_LIMIT),
        name="solve_planes",
    )(place, waves, tables, window)


def boxes_kernel(info_ref, in_ref, table_ref, out_ref, grid_ref):
    even = product(split(in_ref[pl.ds(0, 256, stride=3), :]), (table_ref[0], table_ref[1]), TN)
    odd = product(split(in_ref[pl.ds(1, 256, stride=3), :]), (table_ref[2], table_ref[3]), TN)
    spare = split(in_ref[pl.ds(2, 256, stride=3), :])
    spare_even = product(spare, (table_ref[0], table_ref[1]), TN)
    spare_odd = product(spare, (table_ref[2], table_ref[3]), TN)
    for cell in range(4):
        for tile in range(4):
            columns = slice(tile % 2 * 128, tile % 2 * 128 + 128)
            rows = slice(32 * cell, 32 * cell + 32)
            near, far = even[rows, columns], odd[rows, columns]
            grid_ref[tile, 48 * cell : 48 * cell + 32, :] = near + far if tile < 2 else near - far
            near = spare_even[16 * cell : 16 * cell + 16, columns]
            far = spare_odd[64 + 16 * cell : 80 + 16 * cell, columns]
            place = slice(48 * cell + 32, 48 * cell + 48)
            grid_ref[tile, place, :] = near + far if tile < 2 else near - far
    base = first_cell(info_ref)

    def source(s, carry):
        lane = lanes_of((32, 128))
        group = lane >> 5
        total = jnp.zeros((32, 128), F32)
        for f in range(2):
            number = 2 * s + f
            start = (info_ref[number, 0] & 1) * 16
            cell_z = info_ref[number, 2]
            tile = cell_z >> 3
            after = (tile + 1) & 3
            offset = (cell_z & 7) * 16
            for r in range(2):
                cell = (info_ref[number, 1] + r - base) & 3
                place = pl.ds(pl.multiple_of(cell * 48 + start, 16), 32)
                value = jnp.where(
                    lane >= offset, grid_ref[tile, place, :], grid_ref[after, place, :]
                )
                value = pltpu.roll(value, (64 * f + 32 * r + 128 - offset) & 127, 1)
                total = jnp.where(group == 2 * f + r, value, total)
        out_ref[s] = total
        return carry

    lax.fori_loop(0, 16, source, 0, unroll=4)


def boxes(info, waves, table):
    return pl.pallas_call(
        boxes_kernel,
        grid=(1,),
        in_specs=[
            pl.BlockSpec(memory_space=pltpu.SMEM),
            pl.BlockSpec(memory_space=pltpu.VMEM),
            pl.BlockSpec((4, 256, 256), lambda i: (0, 0, 0)),
        ],
        out_specs=pl.BlockSpec(memory_space=pltpu.VMEM),
        out_shape=jax.ShapeDtypeStruct((16, 32, 128), F32),
        scratch_shapes=[pltpu.VMEM((4, 192, 128), F32)],
        compiler_params=pltpu.CompilerParams(vmem_limit_bytes=VMEM_LIMIT),
        name="boxes",
    )(info, waves, table)


def layout_kernel(info_ref, in_ref, out_ref):
    row = lax.broadcasted_iota(jnp.int32, (32, 128), 0)
    lane = lanes_of((32, 128))
    for quad in range(4):
        parts = exchange([in_ref[4 * quad + i] for i in range(4)])
        for f in range(2):
            for r in range(2):
                inside = (
                    (row < info_ref[f, 3] * 16)
                    & (16 * r + 4 * quad + (lane >> 5) < info_ref[f, 4] * 16)
                    & ((lane & 31) < info_ref[f, 5] * 16)
                )
                out_ref[pl.ds((4 * r + quad) * 2 + f, 32, stride=16), :] = jnp.where(
                    inside, parts[2 * f + r], 0.0
                )


def lay_out(info, pieces):
    return pl.pallas_call(
        layout_kernel,
        in_specs=[
            pl.BlockSpec(memory_space=pltpu.SMEM),
            pl.BlockSpec(memory_space=pltpu.VMEM),
        ],
        out_specs=pl.BlockSpec(memory_space=pltpu.VMEM),
        out_shape=jax.ShapeDtypeStruct((512, 128), F32),
        compiler_params=pltpu.CompilerParams(vmem_limit_bytes=VMEM_LIMIT),
        name="lay_out",
    )(info, pieces)


def along_frag(block, distance):
    devices = range(lax.axis_size("frag"))
    route = [(i, (i + distance) % len(devices)) for i in devices]
    return lax.ppermute(block, "frag", route)


def traded(block, axis):
    return lax.all_to_all(block, axis, split_axis=0, concat_axis=0, tiled=True)


def body(background, orbitals, frag_info):
    tables, window = jnp.asarray(wave_tables()), jnp.asarray(window_table())
    place = (lax.axis_index("frag") * 16 + lax.axis_index("grp")).astype(jnp.int32).reshape(1)
    frag_info, place = lax.optimization_barrier((frag_info, place))
    coeffs = orbitals.reshape(16, 256, 32)
    own = traded(densities(frag_info, coeffs).reshape(16, 1, 4224), "grp")
    past = along_frag(own[:, :, 2048:], 1)
    info = jnp.concatenate([own[:, 0, 4096:4112], past[:, 0, 2048:2064]])
    info = info.astype(jnp.int32).reshape(64, 8)
    own, past = own.reshape(528, 128), past.reshape(272, 128)
    region, cell = deposits(info, own, past)
    held = traded(region.reshape(16, 256, 128), "grp").reshape(128, 32, 128)
    total_density, spectrum = forward_z(background, held, tables, cell)
    spectrum = traded(spectrum.reshape(256, 1, 2176), BOTH).reshape(4352, 128)
    spectrum = solve_planes(place, spectrum, tables, window)
    spectrum = traded(spectrum.reshape(256, 1, 384), BOTH).reshape(768, 128)
    pieces = boxes(info, spectrum, tables)
    pieces = lay_out(frag_info, traded(pieces, "grp"))
    frag_potential = pieces.reshape(256, 2, 128).transpose(1, 0, 2).reshape(2, 32768)
    return total_density, frag_potential


def solution(mesh):
    return jax.shard_map(
        body,
        mesh=mesh,
        in_specs=(
            P("frag", "grp", None),
            P(None, None, None, ("frag", "grp")),
            P(("frag", "grp"), None),
        ),
        out_specs=(P("frag", "grp", None), P(("frag", "grp"), None)),
        check_vma=False,
    )
```

```python
import math

import jax
import jax.numpy as jnp
import ml_dtypes
import numpy as np
from jax import lax
from jax.experimental import pallas as pl
from jax.experimental.pallas import tpu as pltpu
from jax.sharding import PartitionSpec as P

NG = 512
SPACING = 0.2
F32 = jnp.float32
BF16 = jnp.bfloat16
BOTH = ("frag", "grp")
PITCH = 40
VMEM_LIMIT = 24 * 1024 * 1024


def halves(table):
    high = table.astype(ml_dtypes.bfloat16)
    low = (table - high.astype(np.float64)).astype(ml_dtypes.bfloat16)
    return np.stack([high, low])


def synthesis_table(span):
    frequency = np.arange(16)[:, None] - 8
    point = np.arange(32)[None, :]
    angle = 2.0 * math.pi * np.mod(frequency * point, span * 16) / (span * 16)
    live = (frequency >= -4 * span) & (frequency < 4 * span) & (point < 16 * span)
    return np.where(live, (np.cos(angle) + np.sin(angle)) * math.sqrt(2.0 / 16) / span, 0.0)


def plane_tables():
    tables = []
    for span_y in (1, 2):
        for span_z in (1, 2):
            table_y = synthesis_table(span_y).reshape(16, 2, 16)
            table_z = synthesis_table(span_z)
            full = np.einsum("brg,cz->bcgrz", table_y, table_z)
            tables.append(halves(full.reshape(256, 1024)))
    return np.stack(tables)


def depth_tables():
    tables = []
    for span in (1, 2):
        full = np.einsum("ax,mn->mxan", synthesis_table(span), np.eye(16))
        tables.append(halves(full.reshape(512, 256)))
    return np.stack(tables)


def cas(rows, columns):
    angle = 2.0 * math.pi / NG * np.mod(rows[:, None] * columns[None, :], NG)
    return np.cos(angle) + np.sin(angle)


def row_order():
    block, low, high = np.meshgrid(np.arange(16), np.arange(4), np.arange(8), indexing="ij")
    return (block * 32 + high * 4 + low).reshape(-1)


def wave_tables():
    start = np.arange(256)
    even, odd = 2 * start, 2 * start + 1
    rows = row_order()[:256]
    tables = [
        cas(even, start),
        cas(odd, start),
        cas(start, odd),
        cas(even, rows),
        cas(odd, rows),
    ]
    return np.concatenate([halves(table) for table in tables])


def window_table():
    waves = np.concatenate([np.arange(0, NG, 2), np.arange(1, NG, 2)])
    return halves(cas(np.arange(NG + 64) % NG, waves))


def split(value):
    high = value.astype(BF16)
    return high, (value - high.astype(F32)).astype(BF16)


def product(left, right, dims):
    dims = (dims, ((), ()))
    total = lax.dot_general(left[0], right[1], dims, preferred_element_type=F32)
    total += lax.dot_general(left[1], right[0], dims, preferred_element_type=F32)
    return total + lax.dot_general(left[0], right[0], dims, preferred_element_type=F32)


NN = ((1,), (0,))
NT = ((1,), (1,))
TN = ((0,), (0,))


def lanes_of(shape):
    return lax.broadcasted_iota(jnp.int32, shape, len(shape) - 1)


def exchange(parts):
    lane = lanes_of(parts[0].shape)
    low = lane < 64
    even = (lane & 32) == 0

    def swapped(first, second):
        crossed = pltpu.roll(jnp.where(low, second, first), 64, 1)
        return jnp.where(low, first, crossed), jnp.where(low, crossed, second)

    a0, a2 = swapped(parts[0], parts[2])
    a1, a3 = swapped(parts[1], parts[3])
    return (
        jnp.where(even, a0, pltpu.roll(a1, 32, 1)),
        jnp.where(even, pltpu.roll(a0, 96, 1), a1),
        jnp.where(even, a2, pltpu.roll(a3, 32, 1)),
        jnp.where(even, pltpu.roll(a2, 96, 1), a3),
    )


def density_kernel(
    info_ref,
    source_ref,
    planes_ref,
    depths_ref,
    out_ref,
    orbitals_ref,
    coeff_ref,
    plane_ref,
    depth_ref,
    sems,
):
    orbitals_copy = pltpu.make_async_copy(source_ref, orbitals_ref, sems.at[4])
    orbitals_copy.start()
    copies = []
    for f in range(2):
        pair = 2 * info_ref[f, 4] + info_ref[f, 5] - 3
        copies.append(pltpu.make_async_copy(planes_ref.at[pair], plane_ref.at[f], sems.at[2 * f]))
        copies.append(
            pltpu.make_async_copy(
                depths_ref.at[info_ref[f, 3] - 1], depth_ref.at[f], sems.at[2 * f + 1]
            )
        )
    copies[0].start()
    copies[1].start()
    orbitals_copy.wait()
    for a in range(16):
        coeff_ref[a] = jnp.transpose(orbitals_ref[a].astype(F32)).astype(BF16)
    for f in range(2):
        count = info_ref[f, 7]
        scale = 2.0 * info_ref[f, 6].astype(F32)
        coeffs = coeff_ref[:, 16 * f : 16 * f + 16, :].reshape(256, 256)
        copies[2 * f].wait()
        copies[2 * f + 1].wait()
        if f == 0:
            copies[2].start()
            copies[3].start()
        for part in range(4):
            columns = slice(part * 256, (part + 1) * 256)
            flat = jnp.dot(coeffs, plane_ref[f, 1, :, columns], preferred_element_type=F32)
            flat += jnp.dot(coeffs, plane_ref[f, 0, :, columns], preferred_element_type=F32)
            psi = product((depth_ref[f, 0], depth_ref[f, 1]), split(flat), NN)
            total = jnp.zeros((32, 256), F32)
            for m in range(16):
                orbital = psi[m * 32 : (m + 1) * 32]
                total += orbital * orbital * (m < count).astype(F32)
            total = total * scale
            for tile in range(2):
                here = total[:, tile * 128 : (tile + 1) * 128]
                turned = pltpu.roll(here, 64, 1)
                owner = 2 * (2 * part + tile)
                low = lanes_of(here.shape) < 64
                if f == 0:
                    out_ref[33 * owner : 33 * owner + 32, :] = here
                    out_ref[33 * owner + 33 : 33 * owner + 65, :] = turned
                else:
                    for first, value in ((33 * owner, turned), (33 * owner + 33, here)):
                        place = slice(first, first + 32)
                        out_ref[place, :] = jnp.where(low, out_ref[place, :], value)
    lane = lanes_of((1, 128))
    note = jnp.zeros((1, 128), F32)
    for place in range(16):
        note = jnp.where(lane == place, info_ref[place // 8, place % 8].astype(F32), note)
    for owner in range(16):
        out_ref[33 * owner + 32 : 33 * owner + 33, :] = note


def densities(info, orbitals):
    planes = jnp.asarray(plane_tables())
    depths = jnp.asarray(depth_tables())
    return pl.pallas_call(
        density_kernel,
        in_specs=[
            pl.BlockSpec(memory_space=pltpu.SMEM),
            pl.BlockSpec(memory_space=pl.ANY),
            pl.BlockSpec(memory_space=pl.ANY),
            pl.BlockSpec(memory_space=pl.ANY),
        ],
        out_specs=pl.BlockSpec(memory_space=pltpu.VMEM),
        out_shape=jax.ShapeDtypeStruct((528, 128), F32),
        scratch_shapes=[
            pltpu.VMEM((16, 256, 32), BF16),
            pltpu.VMEM((16, 32, 256), BF16),
            pltpu.VMEM((2, 2, 256, 1024), BF16),
            pltpu.VMEM((2, 2, 512, 256), BF16),
            pltpu.SemaphoreType.DMA((5,)),
        ],
        compiler_params=pltpu.CompilerParams(vmem_limit_bytes=56 * 1024 * 1024),
        name="densities",
    )(info, orbitals, planes, depths)


def first_cell(info_ref):
    def touched(number):
        cell = info_ref[number, 1]
        return cell >> 1, ((cell + info_ref[number, 4] - 1) & 31) >> 1

    first, last = touched(0)
    shared = jnp.int32(1)
    for number in range(1, 32):
        one, other = touched(number)
        shared = shared * ((one == first) | (other == first)).astype(jnp.int32)
    return (2 * jnp.where(shared == 1, first, last) + 31) & 31


def landing(info_ref, number):
    cell_z = info_ref[number, 2]
    tile = cell_z >> 3
    return info_ref[number, 1], tile, (tile + 1) & 3, (cell_z & 7) * 16, info_ref[number, 0] & 1


def own_kernel(info_ref, own_ref, out_ref, cell_ref):
    cell_ref[...] = jnp.full((8, 128), first_cell(info_ref).astype(F32))
    out_ref[...] = jnp.zeros(out_ref.shape, F32)

    def source(s, carry):
        own = own_ref[pl.ds(s * 33, 32), :]
        lane = lanes_of((16, 128))
        adds = []
        for f in range(2):
            cell_y, tile, after, offset, odd = landing(info_ref, 2 * s + f)
            low = jnp.where(odd == 0, offset, 256)
            part_inside = (lane >= low) & (lane < low + 32)
            part_beyond = lane < jnp.where(odd == 0, offset - 96, 0)
            inside = (lane >= offset) & (lane < offset + 32)
            beyond = lane < offset - 96
            start = pl.multiple_of(odd * 16, 16)
            for r in range(2):
                row = (cell_y + r) & 31
                turned = pltpu.roll(own, (offset + 128 - (64 * f + 32 * r)) & 127, 1)
                top, rest = turned[0:16], turned[16:32]
                adds.append((row, tile, start, jnp.where(inside, top, 0.0)))
                adds.append((row, after, start, jnp.where(beyond, top, 0.0)))
                adds.append((row, tile, 16, jnp.where(part_inside, rest, 0.0)))
                adds.append((row, after, 16, jnp.where(part_beyond, rest, 0.0)))
        for row, tile, start, value in adds:
            out_ref[row, tile, pl.ds(start, 16), :] += value
        return carry

    lax.fori_loop(0, 16, source, 0, unroll=4)


def past_kernel(info_ref, past_ref, in_ref, out_ref):
    out_ref[...] = in_ref[...]

    def source(s, carry):
        past = past_ref[pl.ds(s * 17, 16), :]
        lane = lanes_of((16, 128))
        adds = []
        for f in range(2):
            cell_y, tile, after, offset, odd = landing(info_ref, 2 * s + f)
            low = jnp.where(odd == 1, offset, 256)
            inside = (lane >= low) & (lane < low + 32)
            beyond = lane < jnp.where(odd == 1, offset - 96, 0)
            for r in range(2):
                row = (cell_y + r) & 31
                turned = pltpu.roll(past, (offset + 128 - (64 * f + 32 * r)) & 127, 1)
                adds.append((row, tile, jnp.where(inside, turned, 0.0)))
                adds.append((row, after, jnp.where(beyond, turned, 0.0)))
        for row, tile, value in adds:
            out_ref[row, tile, 0:16, :] += value
        return carry

    lax.fori_loop(0, 16, source, 0, unroll=4)


def own_deposits(info, own):
    return pl.pallas_call(
        own_kernel,
        in_specs=[pl.BlockSpec(memory_space=pltpu.SMEM), pl.BlockSpec(memory_space=pltpu.VMEM)],
        out_specs=[pl.BlockSpec(memory_space=pltpu.VMEM)] * 2,
        out_shape=[
            jax.ShapeDtypeStruct((32, 4, 32, 128), F32),
            jax.ShapeDtypeStruct((8, 128), F32),
        ],
        compiler_params=pltpu.CompilerParams(vmem_limit_bytes=VMEM_LIMIT),
        name="own_deposits",
    )(info, own)


def past_deposits(info, past, region):
    return pl.pallas_call(
        past_kernel,
        in_specs=[
            pl.BlockSpec(memory_space=pltpu.SMEM),
            pl.BlockSpec(memory_space=pltpu.VMEM),
            pl.BlockSpec(memory_space=pltpu.VMEM),
        ],
        out_specs=pl.BlockSpec(memory_space=pltpu.VMEM),
        out_shape=jax.ShapeDtypeStruct((32, 4, 32, 128), F32),
        input_output_aliases={2: 0},
        compiler_params=pltpu.CompilerParams(vmem_limit_bytes=VMEM_LIMIT),
        name="past_deposits",
    )(info, past, region)


def forward_kernel(back_ref, held_ref, table_ref, cell_ref, total_ref, out_ref, turned_ref):
    b = pl.program_id(0)

    @pl.when(b == 0)
    def _():
        out_ref[pl.ds(16, 256, stride=17), :] = jnp.broadcast_to(cell_ref[0:1, :], (256, 128))

    for g in range(16):
        for jj in range(2):
            for tile in range(4):
                turned_ref[tile, pl.ds(jj * 16 + g, 8, stride=PITCH), :] = held_ref[
                    (g * 2 + jj) * 4 + tile
                ]
    for tile in range(4):
        columns = slice(tile * 128, (tile + 1) * 128)
        for x in range(8):
            total_ref[x, :, columns] = (
                back_ref[x, :, columns] + turned_ref[tile, x * PITCH : x * PITCH + 32, :]
            )
    total = total_ref[...].reshape(256, 512)
    near, far = total[:, :256], total[:, 256:]
    for parity, value in ((0, near + far), (1, near - far)):
        table = (table_ref[2 * parity], table_ref[2 * parity + 1])
        waves = product(table, split(value), NT)
        for tile in range(2):
            place = pl.ds(8 * parity + 2 * b + tile, 256, stride=17)
            out_ref[place, :] = waves[:, tile * 128 : (tile + 1) * 128]


def forward_z(background, held, table, cell):
    return pl.pallas_call(
        forward_kernel,
        grid=(4,),
        in_specs=[
            pl.BlockSpec((8, 32, 512), lambda b: (b, 0, 0)),
            pl.BlockSpec((128, 8, 128), lambda b: (0, b, 0)),
            pl.BlockSpec((4, 256, 256), lambda b: (0, 0, 0)),
            pl.BlockSpec((8, 128), lambda b: (0, 0)),
        ],
        out_specs=[
            pl.BlockSpec((8, 32, 512), lambda b: (b, 0, 0)),
            pl.BlockSpec((4352, 128), lambda b: (0, 0)),
        ],
        out_shape=[
            jax.ShapeDtypeStruct((32, 32, 512), F32),
            jax.ShapeDtypeStruct((4352, 128), F32),
        ],
        scratch_shapes=[pltpu.VMEM((4, 8 * PITCH, 128), F32)],
        compiler_params=pltpu.CompilerParams(vmem_limit_bytes=VMEM_LIMIT),
        name="forward_z",
    )(background, held, table, cell)


def planes_kernel(
    place_ref, in_ref, tables_ref, window_ref, out_ref, grid_ref, wave_ref, cells_ref
):
    kk = pl.program_id(0)

    @pl.when(kk == 0)
    def _():
        for group in range(16):
            row = group * 272 + 16
            cells_ref[group] = jnp.max(in_ref[row : row + 1, :]).astype(jnp.int32)

    def table(i):
        return tables_ref[2 * i], tables_ref[2 * i + 1]

    for quad in range(4):
        parts = [
            jnp.concatenate(
                [
                    in_ref[pl.ds((group * 16 + 4 * quad + i) * 17 + 8 * kk, 8), :]
                    for group in range(16)
                ]
            )
            for i in range(4)
        ]
        for i, part in enumerate(exchange(parts)):
            grid_ref[:, i, :, quad * 128 : (quad + 1) * 128] = part.reshape(16, 8, 128)
    grid = grid_ref[...].reshape(512, 512)
    near, far = grid[:, :256], grid[:, 256:]
    value = jnp.concatenate(
        [product(split(near + far), table(0), NN), product(split(near - far), table(2), NN)], 1
    )
    near, far = value[:256], value[256:]
    value = jnp.concatenate(
        [product(table(3), split(near + far), NN), product(table(4), split(near - far), NN)], 0
    )

    def folded(wave):
        lowest = jnp.minimum(wave, NG - wave)
        return lowest * lowest

    def ordered(place):
        return jnp.where(place < 256, 2 * place, 2 * place - 511)

    square = (
        folded(ordered(lax.broadcasted_iota(jnp.int32, (NG, 1), 0)))
        + folded(ordered(lax.broadcasted_iota(jnp.int32, (1, NG), 1)))
        + folded(2 * place_ref[0] + kk)
    )
    factor = (NG * SPACING) ** 2 / math.pi / float(NG) ** 3
    value = value * jnp.where(square > 0, factor / jnp.maximum(square, 1).astype(F32), 0.0)
    even = product(table(0), split(value[:256]), NN)
    odd = product(table(2), split(value[256:]), NN)
    for i, value in enumerate(split(jnp.concatenate([even + odd, even - odd, even[:32] + odd[:32]]))):
        wave_ref[i] = value
    lane = lanes_of((16, 128))
    for group in range(16):
        place = pl.ds(pl.multiple_of(cells_ref[group] * 16, 16), 64)
        window = (window_ref[0, place, :], window_ref[1, place, :])
        rows = slice(group * 32, group * 32 + 64)
        value = product(window, (wave_ref[0, rows, :], wave_ref[1, rows, :]), NT)
        joined = jnp.zeros((16, 128), F32)
        spare = jnp.zeros((16, 128), F32)
        for cell in range(4):
            piece = jnp.concatenate([value[16 * cell : 16 * cell + 16]] * 2, 1)
            here = pltpu.roll(piece, 32 * cell, 1) if cell else piece
            joined = jnp.where((lane >> 5) == cell, here, joined)
            here = pltpu.roll(piece, (16 * cell + 96) % 128, 1)
            spare = jnp.where(((lane >> 4) & 3) == cell, here, spare)
        out_ref[pl.ds(group * 48 + kk, 16, stride=3), :] = joined
        place = pl.ds(group * 48 + 2, 16, stride=3)
        out_ref[place, :] = jnp.where((lane >> 6) == kk, spare, out_ref[place, :])


def solve_planes(place, waves, tables, window):
    return pl.pallas_call(
        planes_kernel,
        grid=(2,),
        in_specs=[
            pl.BlockSpec(memory_space=pltpu.SMEM),
            pl.BlockSpec(memory_space=pltpu.VMEM),
            pl.BlockSpec(memory_space=pltpu.VMEM),
            pl.BlockSpec(memory_space=pltpu.VMEM),
        ],
        out_specs=pl.BlockSpec((768, 128), lambda kk: (0, 0)),
        out_shape=jax.ShapeDtypeStruct((768, 128), F32),
        scratch_shapes=[
            pltpu.VMEM((16, 4, 8, 512), F32),
            pltpu.VMEM((2, 544, 512), BF16),
            pltpu.SMEM((16,), jnp.int32),
        ],
        compiler_params=pltpu.CompilerParams(vmem_limit_bytes=VMEM_LIMIT),
        name="solve_planes",
    )(place, waves, tables, window)


def boxes_kernel(info_ref, in_ref, table_ref, out_ref, grid_ref):
    even = product(split(in_ref[pl.ds(0, 256, stride=3), :]), (table_ref[0], table_ref[1]), TN)
    odd = product(split(in_ref[pl.ds(1, 256, stride=3), :]), (table_ref[2], table_ref[3]), TN)
    spare = split(in_ref[pl.ds(2, 256, stride=3), :])
    spare_even = product(spare, (table_ref[0], table_ref[1]), TN)
    spare_odd = product(spare, (table_ref[2], table_ref[3]), TN)
    for cell in range(4):
        for tile in range(4):
            columns = slice(tile % 2 * 128, tile % 2 * 128 + 128)
            rows = slice(32 * cell, 32 * cell + 32)
            near, far = even[rows, columns], odd[rows, columns]
            grid_ref[tile, 48 * cell : 48 * cell + 32, :] = near + far if tile < 2 else near - far
            near = spare_even[16 * cell : 16 * cell + 16, columns]
            far = spare_odd[64 + 16 * cell : 80 + 16 * cell, columns]
            place = slice(48 * cell + 32, 48 * cell + 48)
            grid_ref[tile, place, :] = near + far if tile < 2 else near - far
    base = first_cell(info_ref)

    def source(s, carry):
        lane = lanes_of((32, 128))
        group = lane >> 5
        total = jnp.zeros((32, 128), F32)
        for f in range(2):
            number = 2 * s + f
            start = (info_ref[number, 0] & 1) * 16
            cell_z = info_ref[number, 2]
            tile = cell_z >> 3
            after = (tile + 1) & 3
            offset = (cell_z & 7) * 16
            for r in range(2):
                cell = (info_ref[number, 1] + r - base) & 3
                place = pl.ds(pl.multiple_of(cell * 48 + start, 16), 32)
                value = jnp.where(
                    lane >= offset, grid_ref[tile, place, :], grid_ref[after, place, :]
                )
                value = pltpu.roll(value, (64 * f + 32 * r + 128 - offset) & 127, 1)
                total = jnp.where(group == 2 * f + r, value, total)
        out_ref[s] = total
        return carry

    lax.fori_loop(0, 16, source, 0, unroll=4)


def boxes(info, waves, table):
    return pl.pallas_call(
        boxes_kernel,
        grid=(1,),
        in_specs=[
            pl.BlockSpec(memory_space=pltpu.SMEM),
            pl.BlockSpec(memory_space=pltpu.VMEM),
            pl.BlockSpec((4, 256, 256), lambda i: (0, 0, 0)),
        ],
        out_specs=pl.BlockSpec(memory_space=pltpu.VMEM),
        out_shape=jax.ShapeDtypeStruct((16, 32, 128), F32),
        scratch_shapes=[pltpu.VMEM((4, 192, 128), F32)],
        compiler_params=pltpu.CompilerParams(vmem_limit_bytes=VMEM_LIMIT),
        name="boxes",
    )(info, waves, table)


def layout_kernel(info_ref, in_ref, out_ref):
    row = lax.broadcasted_iota(jnp.int32, (32, 128), 0)
    lane = lanes_of((32, 128))
    for quad in range(4):
        parts = exchange([in_ref[4 * quad + i] for i in range(4)])
        for f in range(2):
            for r in range(2):
                inside = (
                    (row < info_ref[f, 3] * 16)
                    & (16 * r + 4 * quad + (lane >> 5) < info_ref[f, 4] * 16)
                    & ((lane & 31) < info_ref[f, 5] * 16)
                )
                out_ref[pl.ds((4 * r + quad) * 2 + f, 32, stride=16), :] = jnp.where(
                    inside, parts[2 * f + r], 0.0
                )


def lay_out(info, pieces):
    return pl.pallas_call(
        layout_kernel,
        in_specs=[
            pl.BlockSpec(memory_space=pltpu.SMEM),
            pl.BlockSpec(memory_space=pltpu.VMEM),
        ],
        out_specs=pl.BlockSpec(memory_space=pltpu.VMEM),
        out_shape=jax.ShapeDtypeStruct((512, 128), F32),
        compiler_params=pltpu.CompilerParams(vmem_limit_bytes=VMEM_LIMIT),
        name="lay_out",
    )(info, pieces)


def along_frag(block, distance):
    devices = range(lax.axis_size("frag"))
    route = [(i, (i + distance) % len(devices)) for i in devices]
    return lax.ppermute(block, "frag", route)


def traded(block, axis):
    return lax.all_to_all(block, axis, split_axis=0, concat_axis=0, tiled=True)


def body(background, orbitals, frag_info):
    tables, window = jnp.asarray(wave_tables()), jnp.asarray(window_table())
    place = (lax.axis_index("frag") * 16 + lax.axis_index("grp")).astype(jnp.int32).reshape(1)
    frag_info, place = lax.optimization_barrier((frag_info, place))
    coeffs = orbitals.reshape(16, 256, 32)
    own = traded(densities(frag_info, coeffs).reshape(16, 1, 4224), "grp")
    past = along_frag(own[:, :, 2048:], 1)
    info = own[:, 0, 4096:4112].astype(jnp.int32).reshape(32, 8)
    past_info = past[:, 0, 2048:2064].astype(jnp.int32).reshape(32, 8)
    region, cell = own_deposits(info, own.reshape(528, 128))
    region = past_deposits(past_info, past.reshape(272, 128), region)
    held = traded(region.reshape(16, 256, 128), "grp").reshape(128, 32, 128)
    total_density, spectrum = forward_z(background, held, tables, cell)
    spectrum = traded(spectrum.reshape(256, 1, 2176), BOTH).reshape(4352, 128)
    spectrum = solve_planes(place, spectrum, tables, window)
    spectrum = traded(spectrum.reshape(256, 1, 384), BOTH).reshape(768, 128)
    pieces = boxes(info, spectrum, tables)
    pieces = lay_out(frag_info, traded(pieces, "grp"))
    frag_potential = pieces.reshape(256, 2, 128).transpose(1, 0, 2).reshape(2, 32768)
    return total_density, frag_potential


def solution(mesh):
    return jax.shard_map(
        body,
        mesh=mesh,
        in_specs=(
            P("frag", "grp", None),
            P(None, None, None, ("frag", "grp")),
            P(("frag", "grp"), None),
        ),
        out_specs=(P("frag", "grp", None), P(("frag", "grp"), None)),
        check_vma=False,
    )
```

```python
import math

import jax
import jax.numpy as jnp
import ml_dtypes
import numpy as np
from jax import lax
from jax.experimental import pallas as pl
from jax.experimental.pallas import tpu as pltpu
from jax.sharding import PartitionSpec as P

NG = 512
SPACING = 0.2
F32 = jnp.float32
BF16 = jnp.bfloat16
BOTH = ("frag", "grp")
PITCH = 40
VMEM_LIMIT = 24 * 1024 * 1024


def halves(table):
    high = table.astype(ml_dtypes.bfloat16)
    low = (table - high.astype(np.float64)).astype(ml_dtypes.bfloat16)
    return np.stack([high, low])


def synthesis_table(span):
    frequency = np.arange(16)[:, None] - 8
    point = np.arange(32)[None, :]
    angle = 2.0 * math.pi * np.mod(frequency * point, span * 16) / (span * 16)
    live = (frequency >= -4 * span) & (frequency < 4 * span) & (point < 16 * span)
    return np.where(live, (np.cos(angle) + np.sin(angle)) * math.sqrt(2.0 / 16) / span, 0.0)


def plane_tables():
    tables = []
    for span_y in (1, 2):
        for span_z in (1, 2):
            table_y = synthesis_table(span_y).reshape(16, 2, 16)
            table_z = synthesis_table(span_z)
            full = np.einsum("brg,cz->bcgrz", table_y, table_z)
            tables.append(halves(full.reshape(256, 1024)))
    return np.stack(tables)


def depth_tables():
    tables = []
    for span in (1, 2):
        full = np.einsum("ax,mn->mxan", synthesis_table(span), np.eye(16))
        tables.append(halves(full.reshape(512, 256)))
    return np.stack(tables)


def cas(rows, columns):
    angle = 2.0 * math.pi / NG * np.mod(rows[:, None] * columns[None, :], NG)
    return np.cos(angle) + np.sin(angle)


def row_order():
    block, low, high = np.meshgrid(np.arange(16), np.arange(4), np.arange(8), indexing="ij")
    return (block * 32 + high * 4 + low).reshape(-1)


def wave_tables():
    start = np.arange(256)
    even, odd = 2 * start, 2 * start + 1
    rows = row_order()[:256]
    tables = [
        cas(even, start),
        cas(odd, start),
        cas(start, odd),
        cas(even, rows),
        cas(odd, rows),
    ]
    return np.concatenate([halves(table) for table in tables])


def window_table():
    waves = np.concatenate([np.arange(0, NG, 2), np.arange(1, NG, 2)])
    return halves(cas(np.arange(NG + 64) % NG, waves))


def split(value):
    high = value.astype(BF16)
    return high, (value - high.astype(F32)).astype(BF16)


def product(left, right, dims):
    dims = (dims, ((), ()))
    total = lax.dot_general(left[0], right[1], dims, preferred_element_type=F32)
    total += lax.dot_general(left[1], right[0], dims, preferred_element_type=F32)
    return total + lax.dot_general(left[0], right[0], dims, preferred_element_type=F32)


NN = ((1,), (0,))
NT = ((1,), (1,))
TN = ((0,), (0,))


def lanes_of(shape):
    return lax.broadcasted_iota(jnp.int32, shape, len(shape) - 1)


def exchange(parts):
    lane = lanes_of(parts[0].shape)
    low = lane < 64
    even = (lane & 32) == 0

    def swapped(first, second):
        crossed = pltpu.roll(jnp.where(low, second, first), 64, 1)
        return jnp.where(low, first, crossed), jnp.where(low, crossed, second)

    a0, a2 = swapped(parts[0], parts[2])
    a1, a3 = swapped(parts[1], parts[3])
    return (
        jnp.where(even, a0, pltpu.roll(a1, 32, 1)),
        jnp.where(even, pltpu.roll(a0, 96, 1), a1),
        jnp.where(even, a2, pltpu.roll(a3, 32, 1)),
        jnp.where(even, pltpu.roll(a2, 96, 1), a3),
    )


def density_kernel(
    info_ref,
    source_ref,
    planes_ref,
    depths_ref,
    out_ref,
    orbitals_ref,
    coeff_ref,
    plane_ref,
    depth_ref,
    sems,
):
    orbitals_copy = pltpu.make_async_copy(source_ref, orbitals_ref, sems.at[4])
    orbitals_copy.start()
    copies = []
    for f in range(2):
        pair = 2 * info_ref[f, 4] + info_ref[f, 5] - 3
        copies.append(pltpu.make_async_copy(planes_ref.at[pair], plane_ref.at[f], sems.at[2 * f]))
        copies.append(
            pltpu.make_async_copy(
                depths_ref.at[info_ref[f, 3] - 1], depth_ref.at[f], sems.at[2 * f + 1]
            )
        )
    copies[0].start()
    copies[1].start()
    orbitals_copy.wait()
    for a in range(16):
        coeff_ref[a] = jnp.transpose(orbitals_ref[a].astype(F32)).astype(BF16)
    for f in range(2):
        count = info_ref[f, 7]
        scale = 2.0 * info_ref[f, 6].astype(F32)
        coeffs = coeff_ref[:, 16 * f : 16 * f + 16, :].reshape(256, 256)
        copies[2 * f].wait()
        copies[2 * f + 1].wait()
        if f == 0:
            copies[2].start()
            copies[3].start()
        for part in range(4):
            columns = slice(part * 256, (part + 1) * 256)
            flat = jnp.dot(coeffs, plane_ref[f, 1, :, columns], preferred_element_type=F32)
            flat += jnp.dot(coeffs, plane_ref[f, 0, :, columns], preferred_element_type=F32)
            psi = product((depth_ref[f, 0], depth_ref[f, 1]), split(flat), NN)
            total = jnp.zeros((32, 256), F32)
            for m in range(16):
                orbital = psi[m * 32 : (m + 1) * 32]
                total += orbital * orbital * (m < count).astype(F32)
            total = total * scale
            for tile in range(2):
                here = total[:, tile * 128 : (tile + 1) * 128]
                turned = pltpu.roll(here, 64, 1)
                owner = 2 * (2 * part + tile)
                low = lanes_of(here.shape) < 64
                if f == 0:
                    out_ref[33 * owner : 33 * owner + 32, :] = here
                    out_ref[33 * owner + 33 : 33 * owner + 65, :] = turned
                else:
                    for first, value in ((33 * owner, turned), (33 * owner + 33, here)):
                        place = slice(first, first + 32)
                        out_ref[place, :] = jnp.where(low, out_ref[place, :], value)
    lane = lanes_of((1, 128))
    note = jnp.zeros((1, 128), F32)
    for place in range(16):
        note = jnp.where(lane == place, info_ref[place // 8, place % 8].astype(F32), note)
    for owner in range(16):
        out_ref[33 * owner + 32 : 33 * owner + 33, :] = note


def densities(info, orbitals):
    planes = jnp.asarray(plane_tables())
    depths = jnp.asarray(depth_tables())
    return pl.pallas_call(
        density_kernel,
        in_specs=[
            pl.BlockSpec(memory_space=pltpu.SMEM),
            pl.BlockSpec(memory_space=pl.ANY),
            pl.BlockSpec(memory_space=pl.ANY),
            pl.BlockSpec(memory_space=pl.ANY),
        ],
        out_specs=pl.BlockSpec(memory_space=pltpu.VMEM),
        out_shape=jax.ShapeDtypeStruct((528, 128), F32),
        scratch_shapes=[
            pltpu.VMEM((16, 256, 32), BF16),
            pltpu.VMEM((16, 32, 256), BF16),
            pltpu.VMEM((2, 2, 256, 1024), BF16),
            pltpu.VMEM((2, 2, 512, 256), BF16),
            pltpu.SemaphoreType.DMA((5,)),
        ],
        compiler_params=pltpu.CompilerParams(vmem_limit_bytes=56 * 1024 * 1024),
        name="densities",
    )(info, orbitals, planes, depths)


def first_cell(info_ref):
    root = info_ref[0, 1]
    lowest = jnp.int32(0)
    for number in range(1, 32):
        lowest = jnp.minimum(lowest, ((info_ref[number, 1] - root + 16) & 31) - 16)
    return (root + lowest) & 31


def landing(info_ref, number):
    cell_z = info_ref[number, 2]
    tile = cell_z >> 3
    return info_ref[number, 1], tile, (tile + 1) & 3, (cell_z & 7) * 16, info_ref[number, 0] & 1


def own_kernel(info_ref, own_ref, out_ref, cell_ref):
    cell_ref[...] = jnp.full((8, 128), first_cell(info_ref).astype(F32))
    out_ref[...] = jnp.zeros(out_ref.shape, F32)

    def source(s, carry):
        own = own_ref[pl.ds(s * 33, 32), :]
        lane = lanes_of((16, 128))
        adds = []
        for f in range(2):
            cell_y, tile, after, offset, odd = landing(info_ref, 2 * s + f)
            low = jnp.where(odd == 0, offset, 256)
            part_inside = (lane >= low) & (lane < low + 32)
            part_beyond = lane < jnp.where(odd == 0, offset - 96, 0)
            inside = (lane >= offset) & (lane < offset + 32)
            beyond = lane < offset - 96
            start = pl.multiple_of(odd * 16, 16)
            for r in range(2):
                row = (cell_y + r) & 31
                turned = pltpu.roll(own, (offset + 128 - (64 * f + 32 * r)) & 127, 1)
                top, rest = turned[0:16], turned[16:32]
                adds.append((row, tile, start, jnp.where(inside, top, 0.0)))
                adds.append((row, after, start, jnp.where(beyond, top, 0.0)))
                adds.append((row, tile, 16, jnp.where(part_inside, rest, 0.0)))
                adds.append((row, after, 16, jnp.where(part_beyond, rest, 0.0)))
        for row, tile, start, value in adds:
            out_ref[row, tile, pl.ds(start, 16), :] += value
        return carry

    lax.fori_loop(0, 16, source, 0, unroll=4)


def past_kernel(info_ref, past_ref, in_ref, out_ref):
    out_ref[...] = in_ref[...]

    def source(s, carry):
        past = past_ref[pl.ds(s * 17, 16), :]
        lane = lanes_of((16, 128))
        adds = []
        for f in range(2):
            cell_y, tile, after, offset, odd = landing(info_ref, 2 * s + f)
            low = jnp.where(odd == 1, offset, 256)
            inside = (lane >= low) & (lane < low + 32)
            beyond = lane < jnp.where(odd == 1, offset - 96, 0)
            for r in range(2):
                row = (cell_y + r) & 31
                turned = pltpu.roll(past, (offset + 128 - (64 * f + 32 * r)) & 127, 1)
                adds.append((row, tile, jnp.where(inside, turned, 0.0)))
                adds.append((row, after, jnp.where(beyond, turned, 0.0)))
        for row, tile, value in adds:
            out_ref[row, tile, 0:16, :] += value
        return carry

    lax.fori_loop(0, 16, source, 0, unroll=4)


def own_deposits(info, own):
    return pl.pallas_call(
        own_kernel,
        in_specs=[pl.BlockSpec(memory_space=pltpu.SMEM), pl.BlockSpec(memory_space=pltpu.VMEM)],
        out_specs=[pl.BlockSpec(memory_space=pltpu.VMEM)] * 2,
        out_shape=[
            jax.ShapeDtypeStruct((32, 4, 32, 128), F32),
            jax.ShapeDtypeStruct((8, 128), F32),
        ],
        compiler_params=pltpu.CompilerParams(vmem_limit_bytes=VMEM_LIMIT),
        name="own_deposits",
    )(info, own)


def past_deposits(info, past, region):
    return pl.pallas_call(
        past_kernel,
        in_specs=[
            pl.BlockSpec(memory_space=pltpu.SMEM),
            pl.BlockSpec(memory_space=pltpu.VMEM),
            pl.BlockSpec(memory_space=pltpu.VMEM),
        ],
        out_specs=pl.BlockSpec(memory_space=pltpu.VMEM),
        out_shape=jax.ShapeDtypeStruct((32, 4, 32, 128), F32),
        input_output_aliases={2: 0},
        compiler_params=pltpu.CompilerParams(vmem_limit_bytes=VMEM_LIMIT),
        name="past_deposits",
    )(info, past, region)


def forward_kernel(back_ref, held_ref, table_ref, cell_ref, total_ref, out_ref, turned_ref):
    b = pl.program_id(0)

    @pl.when(b == 0)
    def _():
        out_ref[pl.ds(16, 256, stride=17), :] = jnp.broadcast_to(cell_ref[0:1, :], (256, 128))

    for g in range(16):
        for jj in range(2):
            for tile in range(4):
                turned_ref[tile, pl.ds(jj * 16 + g, 8, stride=PITCH), :] = held_ref[
                    (g * 2 + jj) * 4 + tile
                ]
    for tile in range(4):
        columns = slice(tile * 128, (tile + 1) * 128)
        for x in range(8):
            total_ref[x, :, columns] = (
                back_ref[x, :, columns] + turned_ref[tile, x * PITCH : x * PITCH + 32, :]
            )
    total = total_ref[...].reshape(256, 512)
    near, far = total[:, :256], total[:, 256:]
    for parity, value in ((0, near + far), (1, near - far)):
        table = (table_ref[2 * parity], table_ref[2 * parity + 1])
        waves = product(table, split(value), NT)
        for tile in range(2):
            place = pl.ds(8 * parity + 2 * b + tile, 256, stride=17)
            out_ref[place, :] = waves[:, tile * 128 : (tile + 1) * 128]


def forward_z(background, held, table, cell):
    return pl.pallas_call(
        forward_kernel,
        grid=(4,),
        in_specs=[
            pl.BlockSpec((8, 32, 512), lambda b: (b, 0, 0)),
            pl.BlockSpec((128, 8, 128), lambda b: (0, b, 0)),
            pl.BlockSpec((4, 256, 256), lambda b: (0, 0, 0)),
            pl.BlockSpec((8, 128), lambda b: (0, 0)),
        ],
        out_specs=[
            pl.BlockSpec((8, 32, 512), lambda b: (b, 0, 0)),
            pl.BlockSpec((4352, 128), lambda b: (0, 0)),
        ],
        out_shape=[
            jax.ShapeDtypeStruct((32, 32, 512), F32),
            jax.ShapeDtypeStruct((4352, 128), F32),
        ],
        scratch_shapes=[pltpu.VMEM((4, 9 * PITCH, 128), F32)],
        compiler_params=pltpu.CompilerParams(vmem_limit_bytes=VMEM_LIMIT),
        name="forward_z",
    )(background, held, table, cell)


def planes_kernel(
    place_ref, in_ref, tables_ref, window_ref, out_ref, grid_ref, wave_ref, cells_ref
):
    kk = pl.program_id(0)

    @pl.when(kk == 0)
    def _():
        for group in range(16):
            row = group * 272 + 16
            cells_ref[group] = jnp.max(in_ref[row : row + 1, :]).astype(jnp.int32)

    def table(i):
        return tables_ref[2 * i], tables_ref[2 * i + 1]

    for quad in range(4):
        parts = [
            jnp.concatenate(
                [
                    in_ref[pl.ds((group * 16 + 4 * quad + i) * 17 + 8 * kk, 8), :]
                    for group in range(16)
                ]
            )
            for i in range(4)
        ]
        for i, part in enumerate(exchange(parts)):
            grid_ref[:, i, :, quad * 128 : (quad + 1) * 128] = part.reshape(16, 8, 128)
    grid = grid_ref[...].reshape(512, 512)
    near, far = grid[:, :256], grid[:, 256:]
    value = jnp.concatenate(
        [product(split(near + far), table(0), NN), product(split(near - far), table(2), NN)], 1
    )
    near, far = value[:256], value[256:]
    value = jnp.concatenate(
        [product(table(3), split(near + far), NN), product(table(4), split(near - far), NN)], 0
    )

    def folded(wave):
        lowest = jnp.minimum(wave, NG - wave)
        return lowest * lowest

    def ordered(place):
        return jnp.where(place < 256, 2 * place, 2 * place - 511)

    square = (
        folded(ordered(lax.broadcasted_iota(jnp.int32, (NG, 1), 0)))
        + folded(ordered(lax.broadcasted_iota(jnp.int32, (1, NG), 1)))
        + folded(2 * place_ref[0] + kk)
    )
    factor = (NG * SPACING) ** 2 / math.pi / float(NG) ** 3
    value = value * jnp.where(square > 0, factor / jnp.maximum(square, 1).astype(F32), 0.0)
    even = product(table(0), split(value[:256]), NN)
    odd = product(table(2), split(value[256:]), NN)
    for i, value in enumerate(split(jnp.concatenate([even + odd, even - odd, even[:32] + odd[:32]]))):
        wave_ref[i] = value
    lane = lanes_of((16, 128))
    for group in range(16):
        place = pl.ds(pl.multiple_of(cells_ref[group] * 16, 16), 64)
        window = (window_ref[0, place, :], window_ref[1, place, :])
        rows = slice(group * 32, group * 32 + 64)
        value = product(window, (wave_ref[0, rows, :], wave_ref[1, rows, :]), NT)
        joined = jnp.zeros((16, 128), F32)
        spare = jnp.zeros((16, 128), F32)
        for cell in range(4):
            piece = jnp.concatenate([value[16 * cell : 16 * cell + 16]] * 2, 1)
            here = pltpu.roll(piece, 32 * cell, 1) if cell else piece
            joined = jnp.where((lane >> 5) == cell, here, joined)
            here = pltpu.roll(piece, (16 * cell + 96) % 128, 1)
            spare = jnp.where(((lane >> 4) & 3) == cell, here, spare)
        out_ref[pl.ds(group * 48 + kk, 16, stride=3), :] = joined
        place = pl.ds(group * 48 + 2, 16, stride=3)
        out_ref[place, :] = jnp.where((lane >> 6) == kk, spare, out_ref[place, :])


def solve_planes(place, waves, tables, window):
    return pl.pallas_call(
        planes_kernel,
        grid=(2,),
        in_specs=[
            pl.BlockSpec(memory_space=pltpu.SMEM),
            pl.BlockSpec(memory_space=pltpu.VMEM),
            pl.BlockSpec(memory_space=pltpu.VMEM),
            pl.BlockSpec(memory_space=pltpu.VMEM),
        ],
        out_specs=pl.BlockSpec((768, 128), lambda kk: (0, 0)),
        out_shape=jax.ShapeDtypeStruct((768, 128), F32),
        scratch_shapes=[
            pltpu.VMEM((16, 4, 8, 512), F32),
            pltpu.VMEM((2, 544, 512), BF16),
            pltpu.SMEM((16,), jnp.int32),
        ],
        compiler_params=pltpu.CompilerParams(vmem_limit_bytes=VMEM_LIMIT),
        name="solve_planes",
    )(place, waves, tables, window)


def boxes_kernel(info_ref, in_ref, table_ref, out_ref, grid_ref):
    even = product(split(in_ref[pl.ds(0, 256, stride=3), :]), (table_ref[0], table_ref[1]), TN)
    odd = product(split(in_ref[pl.ds(1, 256, stride=3), :]), (table_ref[2], table_ref[3]), TN)
    spare = split(in_ref[pl.ds(2, 256, stride=3), :])
    spare_even = product(spare, (table_ref[0], table_ref[1]), TN)
    spare_odd = product(spare, (table_ref[2], table_ref[3]), TN)
    for cell in range(4):
        for tile in range(4):
            columns = slice(tile % 2 * 128, tile % 2 * 128 + 128)
            rows = slice(32 * cell, 32 * cell + 32)
            near, far = even[rows, columns], odd[rows, columns]
            grid_ref[tile, 48 * cell : 48 * cell + 32, :] = near + far if tile < 2 else near - far
            near = spare_even[16 * cell : 16 * cell + 16, columns]
            far = spare_odd[64 + 16 * cell : 80 + 16 * cell, columns]
            place = slice(48 * cell + 32, 48 * cell + 48)
            grid_ref[tile, place, :] = near + far if tile < 2 else near - far
    base = first_cell(info_ref)

    def source(s, carry):
        lane = lanes_of((32, 128))
        group = lane >> 5
        total = jnp.zeros((32, 128), F32)
        for f in range(2):
            number = 2 * s + f
            start = (info_ref[number, 0] & 1) * 16
            cell_z = info_ref[number, 2]
            tile = cell_z >> 3
            after = (tile + 1) & 3
            offset = (cell_z & 7) * 16
            for r in range(2):
                cell = (info_ref[number, 1] + r - base) & 3
                place = pl.ds(pl.multiple_of(cell * 48 + start, 16), 32)
                value = jnp.where(
                    lane >= offset, grid_ref[tile, place, :], grid_ref[after, place, :]
                )
                value = pltpu.roll(value, (64 * f + 32 * r + 128 - offset) & 127, 1)
                total = jnp.where(group == 2 * f + r, value, total)
        out_ref[s] = total
        return carry

    lax.fori_loop(0, 16, source, 0, unroll=4)


def boxes(info, waves, table):
    return pl.pallas_call(
        boxes_kernel,
        grid=(1,),
        in_specs=[
            pl.BlockSpec(memory_space=pltpu.SMEM),
            pl.BlockSpec(memory_space=pltpu.VMEM),
            pl.BlockSpec((4, 256, 256), lambda i: (0, 0, 0)),
        ],
        out_specs=pl.BlockSpec(memory_space=pltpu.VMEM),
        out_shape=jax.ShapeDtypeStruct((16, 32, 128), F32),
        scratch_shapes=[pltpu.VMEM((4, 192, 128), F32)],
        compiler_params=pltpu.CompilerParams(vmem_limit_bytes=VMEM_LIMIT),
        name="boxes",
    )(info, waves, table)


def layout_kernel(info_ref, in_ref, out_ref):
    row = lax.broadcasted_iota(jnp.int32, (32, 128), 0)
    lane = lanes_of((32, 128))
    for quad in range(4):
        parts = exchange([in_ref[4 * quad + i] for i in range(4)])
        for f in range(2):
            for r in range(2):
                inside = (
                    (row < info_ref[f, 3] * 16)
                    & (16 * r + 4 * quad + (lane >> 5) < info_ref[f, 4] * 16)
                    & ((lane & 31) < info_ref[f, 5] * 16)
                )
                out_ref[pl.ds((4 * r + quad) * 2 + f, 32, stride=16), :] = jnp.where(
                    inside, parts[2 * f + r], 0.0
                )


def lay_out(info, pieces):
    return pl.pallas_call(
        layout_kernel,
        in_specs=[
            pl.BlockSpec(memory_space=pltpu.SMEM),
            pl.BlockSpec(memory_space=pltpu.VMEM),
        ],
        out_specs=pl.BlockSpec(memory_space=pltpu.VMEM),
        out_shape=jax.ShapeDtypeStruct((512, 128), F32),
        compiler_params=pltpu.CompilerParams(vmem_limit_bytes=VMEM_LIMIT),
        name="lay_out",
    )(info, pieces)


def along_frag(block, distance):
    devices = range(lax.axis_size("frag"))
    route = [(i, (i + distance) % len(devices)) for i in devices]
    return lax.ppermute(block, "frag", route)


def traded(block, axis):
    return lax.all_to_all(block, axis, split_axis=0, concat_axis=0, tiled=True)


def body(background, orbitals, frag_info):
    tables, window = jnp.asarray(wave_tables()), jnp.asarray(window_table())
    place = (lax.axis_index("frag") * 16 + lax.axis_index("grp")).astype(jnp.int32).reshape(1)
    frag_info, place = lax.optimization_barrier((frag_info, place))
    coeffs = orbitals.reshape(16, 256, 32)
    own = traded(densities(frag_info, coeffs).reshape(16, 1, 4224), "grp")
    past = along_frag(own[:, :, 2048:], 1)
    info = own[:, 0, 4096:4112].astype(jnp.int32).reshape(32, 8)
    past_info = past[:, 0, 2048:2064].astype(jnp.int32).reshape(32, 8)
    region, cell = own_deposits(info, own.reshape(528, 128))
    region = past_deposits(past_info, past.reshape(272, 128), region)
    held = traded(region.reshape(16, 256, 128), "grp").reshape(128, 32, 128)
    total_density, spectrum = forward_z(background, held, tables, cell)
    spectrum = traded(spectrum.reshape(256, 1, 2176), BOTH).reshape(4352, 128)
    spectrum = solve_planes(place, spectrum, tables, window)
    spectrum = traded(spectrum.reshape(256, 1, 384), BOTH).reshape(768, 128)
    pieces = boxes(info, spectrum, tables)
    pieces = lay_out(frag_info, traded(pieces, "grp"))
    frag_potential = pieces.reshape(256, 2, 128).transpose(1, 0, 2).reshape(2, 32768)
    return total_density, frag_potential


def solution(mesh):
    return jax.shard_map(
        body,
        mesh=mesh,
        in_specs=(
            P("frag", "grp", None),
            P(None, None, None, ("frag", "grp")),
            P(("frag", "grp"), None),
        ),
        out_specs=(P("frag", "grp", None), P(("frag", "grp"), None)),
        check_vma=False,
    )
```

```python
import math

import jax
import jax.numpy as jnp
import ml_dtypes
import numpy as np
from jax import lax
from jax.experimental import pallas as pl
from jax.experimental.pallas import tpu as pltpu
from jax.sharding import PartitionSpec as P

NG = 512
SPACING = 0.2
F32 = jnp.float32
BF16 = jnp.bfloat16
BOTH = ("frag", "grp")
PITCH = 40
VMEM_LIMIT = 24 * 1024 * 1024


def halves(table):
    high = table.astype(ml_dtypes.bfloat16)
    low = (table - high.astype(np.float64)).astype(ml_dtypes.bfloat16)
    return np.stack([high, low])


def synthesis_table(span):
    frequency = np.arange(16)[:, None] - 8
    point = np.arange(32)[None, :]
    angle = 2.0 * math.pi * np.mod(frequency * point, span * 16) / (span * 16)
    live = (frequency >= -4 * span) & (frequency < 4 * span) & (point < 16 * span)
    return np.where(live, (np.cos(angle) + np.sin(angle)) * math.sqrt(2.0 / 16) / span, 0.0)


def plane_tables():
    tables = []
    for span_y in (1, 2):
        for span_z in (1, 2):
            table_y = synthesis_table(span_y).reshape(16, 2, 16)
            table_z = synthesis_table(span_z)
            full = np.einsum("brg,cz->bcgrz", table_y, table_z)
            tables.append(halves(full.reshape(256, 1024)))
    return np.stack(tables)


def depth_tables():
    tables = []
    for span in (1, 2):
        full = np.einsum("ax,mn->mxan", synthesis_table(span), np.eye(16))
        tables.append(halves(full.reshape(512, 256)))
    return np.stack(tables)


def cas(rows, columns):
    angle = 2.0 * math.pi / NG * np.mod(rows[:, None] * columns[None, :], NG)
    return np.cos(angle) + np.sin(angle)


def row_order():
    block, low, high = np.meshgrid(np.arange(16), np.arange(4), np.arange(8), indexing="ij")
    return (block * 32 + high * 4 + low).reshape(-1)


def wave_tables():
    start = np.arange(256)
    even, odd = 2 * start, 2 * start + 1
    rows = row_order()[:256]
    tables = [
        cas(even, start),
        cas(odd, start),
        cas(start, odd),
        cas(even, rows),
        cas(odd, rows),
    ]
    return np.concatenate([halves(table) for table in tables])


def window_table():
    waves = np.concatenate([np.arange(0, NG, 2), np.arange(1, NG, 2)])
    return halves(cas(np.arange(NG + 64) % NG, waves))


def split(value):
    high = value.astype(BF16)
    return high, (value - high.astype(F32)).astype(BF16)


def product(left, right, dims):
    dims = (dims, ((), ()))
    total = lax.dot_general(left[0], right[1], dims, preferred_element_type=F32)
    total += lax.dot_general(left[1], right[0], dims, preferred_element_type=F32)
    return total + lax.dot_general(left[0], right[0], dims, preferred_element_type=F32)


NN = ((1,), (0,))
NT = ((1,), (1,))
TN = ((0,), (0,))


def lanes_of(shape):
    return lax.broadcasted_iota(jnp.int32, shape, len(shape) - 1)


def exchange(parts):
    lane = lanes_of(parts[0].shape)
    low = lane < 64
    even = (lane & 32) == 0

    def swapped(first, second):
        crossed = pltpu.roll(jnp.where(low, second, first), 64, 1)
        return jnp.where(low, first, crossed), jnp.where(low, crossed, second)

    a0, a2 = swapped(parts[0], parts[2])
    a1, a3 = swapped(parts[1], parts[3])
    return (
        jnp.where(even, a0, pltpu.roll(a1, 32, 1)),
        jnp.where(even, pltpu.roll(a0, 96, 1), a1),
        jnp.where(even, a2, pltpu.roll(a3, 32, 1)),
        jnp.where(even, pltpu.roll(a2, 96, 1), a3),
    )


def density_kernel(
    info_ref,
    source_ref,
    planes_ref,
    depths_ref,
    out_ref,
    orbitals_ref,
    coeff_ref,
    plane_ref,
    depth_ref,
    sems,
):
    orbitals_copy = pltpu.make_async_copy(source_ref, orbitals_ref, sems.at[6])
    orbitals_copy.start()
    copies = []
    for f in range(2):
        pair = 2 * info_ref[f, 4] + info_ref[f, 5] - 3
        copies.append(
            pltpu.make_async_copy(
                depths_ref.at[info_ref[f, 3] - 1], depth_ref.at[f], sems.at[3 * f]
            )
        )
        for half in range(2):
            columns = pl.ds(512 * half, 512)
            copies.append(
                pltpu.make_async_copy(
                    planes_ref.at[pair, :, :, columns],
                    plane_ref.at[f, :, :, columns],
                    sems.at[3 * f + 1 + half],
                )
            )
    for copy in copies[:3]:
        copy.start()
    orbitals_copy.wait()
    for a in range(16):
        coeff_ref[a] = jnp.transpose(orbitals_ref[a].astype(F32)).astype(BF16)
    for f in range(2):
        count = info_ref[f, 7]
        scale = 2.0 * info_ref[f, 6].astype(F32)
        coeffs = coeff_ref[:, 16 * f : 16 * f + 16, :].reshape(256, 256)
        copies[3 * f].wait()
        for part in range(4):
            if part % 2 == 0:
                copies[3 * f + 1 + part // 2].wait()
            if f == 0 and part == 2:
                for copy in copies[3:]:
                    copy.start()
            columns = slice(part * 256, (part + 1) * 256)
            flat = jnp.dot(coeffs, plane_ref[f, 1, :, columns], preferred_element_type=F32)
            flat += jnp.dot(coeffs, plane_ref[f, 0, :, columns], preferred_element_type=F32)
            psi = product((depth_ref[f, 0], depth_ref[f, 1]), split(flat), NN)
            total = jnp.zeros((32, 256), F32)
            for m in range(16):
                orbital = psi[m * 32 : (m + 1) * 32]
                total += orbital * orbital * (m < count).astype(F32)
            total = total * scale
            for tile in range(2):
                here = total[:, tile * 128 : (tile + 1) * 128]
                turned = pltpu.roll(here, 64, 1)
                owner = 2 * (2 * part + tile)
                low = lanes_of(here.shape) < 64
                if f == 0:
                    out_ref[33 * owner : 33 * owner + 32, :] = here
                    out_ref[33 * owner + 33 : 33 * owner + 65, :] = turned
                else:
                    for first, value in ((33 * owner, turned), (33 * owner + 33, here)):
                        place = slice(first, first + 32)
                        out_ref[place, :] = jnp.where(low, out_ref[place, :], value)
    lane = lanes_of((1, 128))
    note = jnp.zeros((1, 128), F32)
    for place in range(16):
        note = jnp.where(lane == place, info_ref[place // 8, place % 8].astype(F32), note)
    for owner in range(16):
        out_ref[33 * owner + 32 : 33 * owner + 33, :] = note


def densities(info, orbitals):
    planes = jnp.asarray(plane_tables())
    depths = jnp.asarray(depth_tables())
    return pl.pallas_call(
        density_kernel,
        in_specs=[
            pl.BlockSpec(memory_space=pltpu.SMEM),
            pl.BlockSpec(memory_space=pl.ANY),
            pl.BlockSpec(memory_space=pl.ANY),
            pl.BlockSpec(memory_space=pl.ANY),
        ],
        out_specs=pl.BlockSpec(memory_space=pltpu.VMEM),
        out_shape=jax.ShapeDtypeStruct((528, 128), F32),
        scratch_shapes=[
            pltpu.VMEM((16, 256, 32), BF16),
            pltpu.VMEM((16, 32, 256), BF16),
            pltpu.VMEM((2, 2, 256, 1024), BF16),
            pltpu.VMEM((2, 2, 512, 256), BF16),
            pltpu.SemaphoreType.DMA((7,)),
        ],
        compiler_params=pltpu.CompilerParams(vmem_limit_bytes=56 * 1024 * 1024),
        name="densities",
    )(info, orbitals, planes, depths)


def first_cell(info_ref):
    root = info_ref[0, 1]
    lowest = jnp.int32(0)
    for number in range(1, 32):
        lowest = jnp.minimum(lowest, ((info_ref[number, 1] - root + 16) & 31) - 16)
    return (root + lowest) & 31


def landing(info_ref, number):
    cell_z = info_ref[number, 2]
    tile = cell_z >> 3
    return info_ref[number, 1], tile, (tile + 1) & 3, (cell_z & 7) * 16, info_ref[number, 0] & 1


def own_kernel(info_ref, own_ref, out_ref, cell_ref):
    cell_ref[...] = jnp.full((8, 128), first_cell(info_ref).astype(F32))
    out_ref[...] = jnp.zeros(out_ref.shape, F32)

    def source(s, carry):
        own = own_ref[pl.ds(s * 33, 32), :]
        lane = lanes_of((16, 128))
        adds = []
        for f in range(2):
            cell_y, tile, after, offset, odd = landing(info_ref, 2 * s + f)
            low = jnp.where(odd == 0, offset, 256)
            part_inside = (lane >= low) & (lane < low + 32)
            part_beyond = lane < jnp.where(odd == 0, offset - 96, 0)
            inside = (lane >= offset) & (lane < offset + 32)
            beyond = lane < offset - 96
            start = pl.multiple_of(odd * 16, 16)
            for r in range(2):
                row = (cell_y + r) & 31
                turned = pltpu.roll(own, (offset + 128 - (64 * f + 32 * r)) & 127, 1)
                top, rest = turned[0:16], turned[16:32]
                adds.append((row, tile, start, jnp.where(inside, top, 0.0)))
                adds.append((row, after, start, jnp.where(beyond, top, 0.0)))
                adds.append((row, tile, 16, jnp.where(part_inside, rest, 0.0)))
                adds.append((row, after, 16, jnp.where(part_beyond, rest, 0.0)))
        for row, tile, start, value in adds:
            out_ref[row, tile, pl.ds(start, 16), :] += value
        return carry

    lax.fori_loop(0, 16, source, 0, unroll=4)


def past_kernel(info_ref, past_ref, in_ref, out_ref):
    out_ref[...] = in_ref[...]

    def source(s, carry):
        past = past_ref[pl.ds(s * 17, 16), :]
        lane = lanes_of((16, 128))
        adds = []
        for f in range(2):
            cell_y, tile, after, offset, odd = landing(info_ref, 2 * s + f)
            low = jnp.where(odd == 1, offset, 256)
            inside = (lane >= low) & (lane < low + 32)
            beyond = lane < jnp.where(odd == 1, offset - 96, 0)
            for r in range(2):
                row = (cell_y + r) & 31
                turned = pltpu.roll(past, (offset + 128 - (64 * f + 32 * r)) & 127, 1)
                adds.append((row, tile, jnp.where(inside, turned, 0.0)))
                adds.append((row, after, jnp.where(beyond, turned, 0.0)))
        for row, tile, value in adds:
            out_ref[row, tile, 0:16, :] += value
        return carry

    lax.fori_loop(0, 16, source, 0, unroll=4)


def own_deposits(info, own):
    return pl.pallas_call(
        own_kernel,
        in_specs=[pl.BlockSpec(memory_space=pltpu.SMEM), pl.BlockSpec(memory_space=pltpu.VMEM)],
        out_specs=[pl.BlockSpec(memory_space=pltpu.VMEM)] * 2,
        out_shape=[
            jax.ShapeDtypeStruct((32, 4, 32, 128), F32),
            jax.ShapeDtypeStruct((8, 128), F32),
        ],
        compiler_params=pltpu.CompilerParams(vmem_limit_bytes=VMEM_LIMIT),
        name="own_deposits",
    )(info, own)


def past_deposits(info, past, region):
    return pl.pallas_call(
        past_kernel,
        in_specs=[
            pl.BlockSpec(memory_space=pltpu.SMEM),
            pl.BlockSpec(memory_space=pltpu.VMEM),
            pl.BlockSpec(memory_space=pltpu.VMEM),
        ],
        out_specs=pl.BlockSpec(memory_space=pltpu.VMEM),
        out_shape=jax.ShapeDtypeStruct((32, 4, 32, 128), F32),
        input_output_aliases={2: 0},
        compiler_params=pltpu.CompilerParams(vmem_limit_bytes=VMEM_LIMIT),
        name="past_deposits",
    )(info, past, region)


def forward_kernel(back_ref, held_ref, table_ref, cell_ref, total_ref, out_ref, turned_ref):
    b = pl.program_id(0)

    @pl.when(b == 0)
    def _():
        out_ref[pl.ds(16, 256, stride=17), :] = jnp.broadcast_to(cell_ref[0:1, :], (256, 128))

    for g in range(16):
        for jj in range(2):
            for tile in range(4):
                turned_ref[tile, pl.ds(jj * 16 + g, 8, stride=PITCH), :] = held_ref[
                    (g * 2 + jj) * 4 + tile
                ]
    for tile in range(4):
        columns = slice(tile * 128, (tile + 1) * 128)
        for x in range(8):
            total_ref[x, :, columns] = (
                back_ref[x, :, columns] + turned_ref[tile, x * PITCH : x * PITCH + 32, :]
            )
    total = total_ref[...].reshape(256, 512)
    near, far = total[:, :256], total[:, 256:]
    for parity, value in ((0, near + far), (1, near - far)):
        table = (table_ref[2 * parity], table_ref[2 * parity + 1])
        waves = product(table, split(value), NT)
        for tile in range(2):
            place = pl.ds(8 * parity + 2 * b + tile, 256, stride=17)
            out_ref[place, :] = waves[:, tile * 128 : (tile + 1) * 128]


def forward_z(background, held, table, cell):
    return pl.pallas_call(
        forward_kernel,
        grid=(4,),
        in_specs=[
            pl.BlockSpec((8, 32, 512), lambda b: (b, 0, 0)),
            pl.BlockSpec((128, 8, 128), lambda b: (0, b, 0)),
            pl.BlockSpec((4, 256, 256), lambda b: (0, 0, 0)),
            pl.BlockSpec((8, 128), lambda b: (0, 0)),
        ],
        out_specs=[
            pl.BlockSpec((8, 32, 512), lambda b: (b, 0, 0)),
            pl.BlockSpec((4352, 128), lambda b: (0, 0)),
        ],
        out_shape=[
            jax.ShapeDtypeStruct((32, 32, 512), F32),
            jax.ShapeDtypeStruct((4352, 128), F32),
        ],
        scratch_shapes=[pltpu.VMEM((4, 9 * PITCH, 128), F32)],
        compiler_params=pltpu.CompilerParams(vmem_limit_bytes=VMEM_LIMIT),
        name="forward_z",
    )(background, held, table, cell)


def planes_kernel(
    place_ref, in_ref, tables_ref, window_ref, out_ref, grid_ref, wave_ref, cells_ref
):
    kk = pl.program_id(0)

    @pl.when(kk == 0)
    def _():
        for group in range(16):
            row = group * 272 + 16
            cells_ref[group] = jnp.max(in_ref[row : row + 1, :]).astype(jnp.int32)

    def table(i):
        return tables_ref[2 * i], tables_ref[2 * i + 1]

    for quad in range(4):
        parts = [
            jnp.concatenate(
                [
                    in_ref[pl.ds((group * 16 + 4 * quad + i) * 17 + 8 * kk, 8), :]
                    for group in range(16)
                ]
            )
            for i in range(4)
        ]
        for i, part in enumerate(exchange(parts)):
            grid_ref[:, i, :, quad * 128 : (quad + 1) * 128] = part.reshape(16, 8, 128)
    grid = grid_ref[...].reshape(512, 512)
    near, far = grid[:, :256], grid[:, 256:]
    value = jnp.concatenate(
        [product(split(near + far), table(0), NN), product(split(near - far), table(2), NN)], 1
    )
    near, far = value[:256], value[256:]
    value = jnp.concatenate(
        [product(table(3), split(near + far), NN), product(table(4), split(near - far), NN)], 0
    )

    def folded(wave):
        lowest = jnp.minimum(wave, NG - wave)
        return lowest * lowest

    def ordered(place):
        return jnp.where(place < 256, 2 * place, 2 * place - 511)

    square = (
        folded(ordered(lax.broadcasted_iota(jnp.int32, (NG, 1), 0)))
        + folded(ordered(lax.broadcasted_iota(jnp.int32, (1, NG), 1)))
        + folded(2 * place_ref[0] + kk)
    )
    factor = (NG * SPACING) ** 2 / math.pi / float(NG) ** 3
    value = value * jnp.where(square > 0, factor / jnp.maximum(square, 1).astype(F32), 0.0)
    even = product(table(0), split(value[:256]), NN)
    odd = product(table(2), split(value[256:]), NN)
    for i, value in enumerate(split(jnp.concatenate([even + odd, even - odd, even[:32] + odd[:32]]))):
        wave_ref[i] = value
    lane = lanes_of((16, 128))
    for group in range(16):
        place = pl.ds(pl.multiple_of(cells_ref[group] * 16, 16), 64)
        window = (window_ref[0, place, :], window_ref[1, place, :])
        rows = slice(group * 32, group * 32 + 64)
        value = product(window, (wave_ref[0, rows, :], wave_ref[1, rows, :]), NT)
        joined = jnp.zeros((16, 128), F32)
        spare = jnp.zeros((16, 128), F32)
        for cell in range(4):
            piece = jnp.concatenate([value[16 * cell : 16 * cell + 16]] * 2, 1)
            here = pltpu.roll(piece, 32 * cell, 1) if cell else piece
            joined = jnp.where((lane >> 5) == cell, here, joined)
            here = pltpu.roll(piece, (16 * cell + 96) % 128, 1)
            spare = jnp.where(((lane >> 4) & 3) == cell, here, spare)
        out_ref[pl.ds(group * 48 + kk, 16, stride=3), :] = joined
        place = pl.ds(group * 48 + 2, 16, stride=3)
        out_ref[place, :] = jnp.where((lane >> 6) == kk, spare, out_ref[place, :])


def solve_planes(place, waves, tables, window):
    return pl.pallas_call(
        planes_kernel,
        grid=(2,),
        in_specs=[
            pl.BlockSpec(memory_space=pltpu.SMEM),
            pl.BlockSpec(memory_space=pltpu.VMEM),
            pl.BlockSpec(memory_space=pltpu.VMEM),
            pl.BlockSpec(memory_space=pltpu.VMEM),
        ],
        out_specs=pl.BlockSpec((768, 128), lambda kk: (0, 0)),
        out_shape=jax.ShapeDtypeStruct((768, 128), F32),
        scratch_shapes=[
            pltpu.VMEM((16, 4, 8, 512), F32),
            pltpu.VMEM((2, 544, 512), BF16),
            pltpu.SMEM((16,), jnp.int32),
        ],
        compiler_params=pltpu.CompilerParams(vmem_limit_bytes=VMEM_LIMIT),
        name="solve_planes",
    )(place, waves, tables, window)


def boxes_kernel(info_ref, in_ref, table_ref, out_ref, grid_ref):
    even = product(split(in_ref[pl.ds(0, 256, stride=3), :]), (table_ref[0], table_ref[1]), TN)
    odd = product(split(in_ref[pl.ds(1, 256, stride=3), :]), (table_ref[2], table_ref[3]), TN)
    spare = split(in_ref[pl.ds(2, 256, stride=3), :])
    spare_even = product(spare, (table_ref[0], table_ref[1]), TN)
    spare_odd = product(spare, (table_ref[2], table_ref[3]), TN)
    for cell in range(4):
        for tile in range(4):
            columns = slice(tile % 2 * 128, tile % 2 * 128 + 128)
            rows = slice(32 * cell, 32 * cell + 32)
            near, far = even[rows, columns], odd[rows, columns]
            grid_ref[tile, 48 * cell : 48 * cell + 32, :] = near + far if tile < 2 else near - far
            near = spare_even[16 * cell : 16 * cell + 16, columns]
            far = spare_odd[64 + 16 * cell : 80 + 16 * cell, columns]
            place = slice(48 * cell + 32, 48 * cell + 48)
            grid_ref[tile, place, :] = near + far if tile < 2 else near - far
    base = first_cell(info_ref)

    def source(s, carry):
        lane = lanes_of((32, 128))
        group = lane >> 5
        total = jnp.zeros((32, 128), F32)
        for f in range(2):
            number = 2 * s + f
            start = (info_ref[number, 0] & 1) * 16
            cell_z = info_ref[number, 2]
            tile = cell_z >> 3
            after = (tile + 1) & 3
            offset = (cell_z & 7) * 16
            for r in range(2):
                cell = (info_ref[number, 1] + r - base) & 3
                place = pl.ds(pl.multiple_of(cell * 48 + start, 16), 32)
                value = jnp.where(
                    lane >= offset, grid_ref[tile, place, :], grid_ref[after, place, :]
                )
                value = pltpu.roll(value, (64 * f + 32 * r + 128 - offset) & 127, 1)
                total = jnp.where(group == 2 * f + r, value, total)
        out_ref[s] = total
        return carry

    lax.fori_loop(0, 16, source, 0, unroll=4)


def boxes(info, waves, table):
    return pl.pallas_call(
        boxes_kernel,
        grid=(1,),
        in_specs=[
            pl.BlockSpec(memory_space=pltpu.SMEM),
            pl.BlockSpec(memory_space=pltpu.VMEM),
            pl.BlockSpec((4, 256, 256), lambda i: (0, 0, 0)),
        ],
        out_specs=pl.BlockSpec(memory_space=pltpu.VMEM),
        out_shape=jax.ShapeDtypeStruct((16, 32, 128), F32),
        scratch_shapes=[pltpu.VMEM((4, 192, 128), F32)],
        compiler_params=pltpu.CompilerParams(vmem_limit_bytes=VMEM_LIMIT),
        name="boxes",
    )(info, waves, table)


def layout_kernel(info_ref, in_ref, out_ref):
    row = lax.broadcasted_iota(jnp.int32, (32, 128), 0)
    lane = lanes_of((32, 128))
    for quad in range(4):
        parts = exchange([in_ref[4 * quad + i] for i in range(4)])
        for f in range(2):
            for r in range(2):
                inside = (
                    (row < info_ref[f, 3] * 16)
                    & (16 * r + 4 * quad + (lane >> 5) < info_ref[f, 4] * 16)
                    & ((lane & 31) < info_ref[f, 5] * 16)
                )
                out_ref[pl.ds((4 * r + quad) * 2 + f, 32, stride=16), :] = jnp.where(
                    inside, parts[2 * f + r], 0.0
                )


def lay_out(info, pieces):
    return pl.pallas_call(
        layout_kernel,
        in_specs=[
            pl.BlockSpec(memory_space=pltpu.SMEM),
            pl.BlockSpec(memory_space=pltpu.VMEM),
        ],
        out_specs=pl.BlockSpec(memory_space=pltpu.VMEM),
        out_shape=jax.ShapeDtypeStruct((512, 128), F32),
        compiler_params=pltpu.CompilerParams(vmem_limit_bytes=VMEM_LIMIT),
        name="lay_out",
    )(info, pieces)


def along_frag(block, distance):
    devices = range(lax.axis_size("frag"))
    route = [(i, (i + distance) % len(devices)) for i in devices]
    return lax.ppermute(block, "frag", route)


def traded(block, axis):
    return lax.all_to_all(block, axis, split_axis=0, concat_axis=0, tiled=True)


def body(background, orbitals, frag_info):
    tables, window = jnp.asarray(wave_tables()), jnp.asarray(window_table())
    place = (lax.axis_index("frag") * 16 + lax.axis_index("grp")).astype(jnp.int32).reshape(1)
    frag_info, place = lax.optimization_barrier((frag_info, place))
    coeffs = orbitals.reshape(16, 256, 32)
    own = traded(densities(frag_info, coeffs).reshape(16, 1, 4224), "grp")
    past = along_frag(own[:, :, 2048:], 1)
    info = own[:, 0, 4096:4112].astype(jnp.int32).reshape(32, 8)
    past_info = past[:, 0, 2048:2064].astype(jnp.int32).reshape(32, 8)
    region, cell = own_deposits(info, own.reshape(528, 128))
    region = past_deposits(past_info, past.reshape(272, 128), region)
    held = traded(region.reshape(16, 256, 128), "grp").reshape(128, 32, 128)
    total_density, spectrum = forward_z(background, held, tables, cell)
    spectrum = traded(spectrum.reshape(256, 1, 2176), BOTH).reshape(4352, 128)
    spectrum = solve_planes(place, spectrum, tables, window)
    spectrum = traded(spectrum.reshape(256, 1, 384), BOTH).reshape(768, 128)
    pieces = boxes(info, spectrum, tables)
    pieces = lay_out(frag_info, traded(pieces, "grp"))
    frag_potential = pieces.reshape(256, 2, 128).transpose(1, 0, 2).reshape(2, 32768)
    return total_density, frag_potential


def solution(mesh):
    return jax.shard_map(
        body,
        mesh=mesh,
        in_specs=(
            P("frag", "grp", None),
            P(None, None, None, ("frag", "grp")),
            P(("frag", "grp"), None),
        ),
        out_specs=(P("frag", "grp", None), P(("frag", "grp"), None)),
        check_vma=False,
    )
```
